32 devices in a mesh: dp: 4 (over y, x), ctx: 8 (over z, core).
Axes of the slice: x: 2, y: 2, z: 4, core: 2. Of those that a mesh axis runs over, the one named last changes fastest.
Arguments:
- segment_ids: int32 [4, 1024], P('dp'), may hold values from 0 to 7, never falling along the last dimension, each value on 1 to 512 neighbouring positions
- queries: bfloat16 [4, 1024, 2048], P('dp', 'ctx'), may hold values from -600 to 600
- keys: bfloat16 [4, 1024, 1024], P('dp', 'ctx'), may hold values from -600 to 600
- values: bfloat16 [4, 1024, 1024], P('dp', 'ctx'), may hold values from -6 to 6
- query_gain: float32 [256], replicated, may hold values from 0.1 to 1.9
- key_gain: float32 [256], replicated, may hold values from 0.1 to 1.9
- out_grad: bfloat16 [4, 1024, 2048], P('dp', 'ctx'), may hold values from -9 to 9
Outputs:
- attended: bfloat16 [4, 1024, 2048], P('dp', 'ctx')
- query_grad: bfloat16 [4, 1024, 2048], P('dp', 'ctx')
- key_grad: bfloat16 [4, 1024, 1024], P('dp', 'ctx')
- value_grad: bfloat16 [4, 1024, 1024], P('dp', 'ctx')
- query_gain_grad: float32 [256], replicated
- key_gain_grad: float32 [256], replicated
The draws below stay inside these ranges and needn't reach their ends.
Inputs may be any that keep to these rules, and one draw needn't show every extreme that they name: `segment_ids`: in each packed sequence the document numbers never fall along the positions; every document holds 1 to 512 positions and one holds exactly 512.
All inputs are finite; a program needn't handle non-finite values.
Results may differ from the reference program's by a relative error of at most 0.0081.
Values may be sent and summed in bfloat16 or wider, within the bound.
No kernel may reach another device: no remote copies, remote signals or barrier semaphores. Data moves between devices by JAX's collectives and lax.ppermute only.
A program may use at most 64 MiB of HBM per device.

```python
import math
import jax
import jax.numpy as jnp
import numpy as np
from jax import lax

HEADS = 8
KV_HEADS = 4
HEAD_DIM = 256
TOK_DEV = 128
GREACH = 4
SEQS = 4
SEQ_LEN = 1024
DOCS = 8
WINDOW = 512


def scaled_rows(key, heads):
    first = jax.random.fold_in(key, 0)
    second = jax.random.fold_in(key, 1)
    fourth = jax.random.fold_in(key, 3)
    shape = (SEQS, SEQ_LEN, heads, HEAD_DIM)
    base = jnp.clip(jax.random.normal(first, shape, jnp.float32), -6.0, 6.0)
    row_scale = 10.0 ** jax.random.uniform(second, (SEQS, SEQ_LEN, heads, 1), jnp.float32)
    col_scale = 10.0 ** jax.random.uniform(fourth, (HEAD_DIM,), jnp.float32)
    return (base * row_scale * col_scale).reshape(SEQS, SEQ_LEN, heads * HEAD_DIM)


def draw_queries(key, part):
    return scaled_rows(jax.random.fold_in(key, 101), HEADS).astype(jnp.bfloat16)


def draw_keys(key, part):
    return scaled_rows(jax.random.fold_in(key, 202), KV_HEADS).astype(jnp.bfloat16)


def draw_out_grad(key, part):
    inner = jax.random.fold_in(key, 303)
    shape = (SEQS, SEQ_LEN, HEADS * HEAD_DIM)
    along = jnp.arange(SEQ_LEN, dtype=jnp.float32) / SEQ_LEN
    across = jnp.arange(SEQS, dtype=jnp.float32) / SEQS
    rise = 0.25 * (1.0 + 2.0 * along)[None, :, None] * (1.0 + 2.0 * across)[:, None, None]
    base = jnp.clip(jax.random.normal(inner, shape, jnp.float32), -4.0, 4.0)
    return (base * rise).astype(jnp.bfloat16)


def block_scale(key, dims, cuts, low, high):
    factor_of = 1.0
    for dim, blocks in cuts:
        heights = jax.random.uniform(jax.random.fold_in(jax.random.fold_in(key, 6), dim), (blocks,), jnp.float32, low / len(cuts), high / len(cuts))
        factor_of = factor_of * jnp.repeat(jnp.exp(heights), dims[dim] // blocks).reshape((-1,) + (1,) * (len(dims) - 1 - dim))
    return factor_of


def profile(amount, total, most, lean):
    loads = [(1 << 20) // math.isqrt(standing ** lean) + 1 for standing in range(2, amount + 1)]
    spare, given = total - most - (amount - 1), [1] * (amount - 1)
    while spare > 0:
        candidates = [i for i in range(amount - 1) if given[i] < most]
        pool, remaining = sum([loads[i] for i in candidates]), spare
        for i in candidates:
            addition = min(most - given[i], max(1, remaining * loads[i] // pool), spare)
            given[i] = given[i] + addition
            spare = spare - addition
    return np.array([most] + given)


def uneven(rng, amount, total, most, skew):
    if amount == 2:
        one = jax.random.randint(rng, (), max(1, total - most), min(most, total - 1) + 1)
        return jnp.stack([one, total - one])
    lengths = jnp.asarray(profile(amount, total, most, skew), jnp.int32)
    twos = (amount - 1) // 2
    giver, receiver = lengths[1:1 + 2 * twos:2], lengths[2:2 + 2 * twos:2]
    slack = jnp.minimum(giver - 1, most - receiver)
    passed = jax.random.randint(jax.random.fold_in(rng, 1), (twos,), 0, 1 << 20) % (slack + 1)
    lengths = lengths.at[1:1 + 2 * twos:2].set(giver - passed).at[2:2 + 2 * twos:2].set(receiver + passed)
    return lengths[jax.random.permutation(jax.random.fold_in(rng, 2), amount)]


def noise(key, shape, spread, limit, cuts=(), kind=jnp.bfloat16):
    entries = jax.random.normal(key, shape, jnp.float32) * spread
    if len(cuts) > 0:
        entries = block_scale(key, shape, cuts, -0.22, 0.18) * entries
    return jnp.clip(entries, min=-limit, max=limit).astype(kind)


def setup_inputs(seed: int = 0) -> dict:
    arg_keys = jax.random.split(jax.random.key(seed), 8)
    segment_ids = jax.vmap(lambda own: jnp.searchsorted(jnp.cumsum(uneven(own, DOCS, SEQ_LEN, WINDOW, 2)), jnp.arange(SEQ_LEN), side="right"))(jax.random.split(arg_keys[0], SEQS)).reshape((SEQS, SEQ_LEN)).astype(jnp.int32)
    queries = draw_queries(jax.random.fold_in(arg_keys[7], 71), 0)
    keys = draw_keys(jax.random.fold_in(arg_keys[7], 71), 0)
    values = noise(arg_keys[3], (SEQS, SEQ_LEN, KV_HEADS * HEAD_DIM), 1.0, 6.0, ((0, 4), (1, 8)))
    query_gain = jnp.clip(1.0 + 0.18 * jax.random.normal(arg_keys[4], (HEAD_DIM,), jnp.float32), 0.1, 1.9)
    key_gain = jnp.clip(1.0 + 0.18 * jax.random.normal(arg_keys[5], (HEAD_DIM,), jnp.float32), 0.1, 1.9)
    out_grad = draw_out_grad(jax.random.fold_in(arg_keys[7], 71), 0)
    return dict(segment_ids=segment_ids, queries=queries, keys=keys, values=values, query_gain=query_gain, key_gain=key_gain, out_grad=out_grad)


epsilon = 1e-06

def normalize(field, gain_vec):
    as_float = field.astype(jnp.float32)
    inverse = lax.rsqrt(lax.optimization_barrier(jnp.mean(as_float * as_float, -1, keepdims=True)) + epsilon)
    normed = as_float * inverse
    return (normed, inverse, normed * gain_vec)

def norm_backward(upstream, normed, inverse, gain_vec):
    scaled = upstream * gain_vec
    grad_in = inverse * (scaled - normed * lax.optimization_barrier(jnp.mean(scaled * normed, -1, keepdims=True)))
    return (grad_in, lax.optimization_barrier(jnp.sum(upstream * normed, axis=(0, 1))))

def reference(segment_ids, queries, keys, values, query_gain, key_gain, out_grad):
    groups = HEADS // KV_HEADS
    reach_rows = GREACH * TOK_DEV
    blocks = SEQ_LEN // TOK_DEV
    band_rows = reach_rows + TOK_DEV
    column_ids = jnp.arange(band_rows)[None, :]
    row_ids = jnp.arange(TOK_DEV)[:, None]
    in_window = (column_ids <= row_ids + reach_rows) & (column_ids > row_ids)

    def banded(field):
        tiled = field.reshape((blocks + GREACH, TOK_DEV) + field.shape[1:])
        return jnp.concatenate([tiled[offset:offset + blocks] for offset in range(GREACH + 1)], axis=1)

    def folded(parts):
        pieces = parts.reshape(blocks, GREACH + 1, TOK_DEV, KV_HEADS, HEAD_DIM)
        summed = jnp.zeros((blocks + GREACH, TOK_DEV, KV_HEADS, HEAD_DIM), jnp.float32)
        for offset in range(GREACH + 1):
            summed = summed + jnp.pad(pieces[:, offset], ((offset, GREACH - offset), (0, 0), (0, 0), (0, 0)))
        return summed[GREACH:].reshape(SEQ_LEN, KV_HEADS, HEAD_DIM)

    def one_sequence(items):
        seg_row, query_seq, key_seq, value_seq, grad_seq = items
        q_normed, q_inverse, q_gained = normalize(query_seq.reshape(SEQ_LEN, HEADS, HEAD_DIM), query_gain)
        q_scaled = (q_gained * HEAD_DIM ** (-0.5)).astype(jnp.bfloat16)
        k_normed, k_inverse, k_gained = normalize(key_seq.reshape(SEQ_LEN, KV_HEADS, HEAD_DIM), key_gain)
        k_rounded = k_gained.astype(jnp.bfloat16)
        lead_zeros = jnp.zeros((reach_rows, KV_HEADS, HEAD_DIM), jnp.bfloat16)
        band_keys = banded(jnp.concatenate([lead_zeros, k_rounded])).astype(jnp.float32)
        band_values = banded(jnp.concatenate([lead_zeros, value_seq.reshape(SEQ_LEN, KV_HEADS, HEAD_DIM)])).astype(jnp.float32)
        band_seg = banded(jnp.concatenate([jnp.full((reach_rows,), -1, jnp.int32), seg_row.astype(jnp.int32)]))
        query_seg = seg_row.astype(jnp.int32).reshape(blocks, TOK_DEV)
        live_mask = (query_seg[:, :, None] == band_seg[:, None, :]) & in_window[None]
        q_grouped = q_scaled.astype(jnp.float32).reshape(blocks, TOK_DEV, KV_HEADS, groups, HEAD_DIM)
        scores = jnp.einsum('bikgd,bjkd->bkgij', q_grouped, band_keys)
        weights = jnp.where(live_mask[:, None, None], jnp.exp(scores), 0.0)
        probs = weights / lax.optimization_barrier(jnp.sum(weights, -1, keepdims=True))
        probs_back = lax.optimization_barrier(probs.astype(jnp.bfloat16)).astype(jnp.float32)
        attended = jnp.einsum('bkgij,bjkd->bikgd', probs_back, band_values)
        attended = attended.astype(jnp.bfloat16).reshape(SEQ_LEN, HEADS * HEAD_DIM)
        grad_grouped = grad_seq.astype(jnp.float32).reshape(blocks, TOK_DEV, KV_HEADS, groups, HEAD_DIM)
        dprob = jnp.einsum('bikgd,bjkd->bkgij', grad_grouped, band_values)
        centre = lax.optimization_barrier(jnp.sum(probs * dprob, -1, keepdims=True))
        dscore = lax.optimization_barrier((probs * (dprob - centre)).astype(jnp.bfloat16)).astype(jnp.float32)
        dq_scaled = jnp.einsum('bkgij,bjkd->bikgd', dscore, band_keys).reshape(SEQ_LEN, HEADS, HEAD_DIM)
        key_parts = jnp.einsum('bkgij,bikgd->bjkd', dscore, q_grouped)
        key_parts = lax.optimization_barrier(key_parts.astype(jnp.bfloat16)).astype(jnp.float32)
        value_parts = jnp.einsum('bkgij,bikgd->bjkd', probs_back, grad_grouped)
        value_parts = lax.optimization_barrier(value_parts.astype(jnp.bfloat16)).astype(jnp.float32)
        dk_rounded = folded(key_parts)
        value_grad = folded(value_parts).astype(jnp.bfloat16).reshape(SEQ_LEN, KV_HEADS * HEAD_DIM)
        query_grad, query_gain_part = norm_backward(dq_scaled * HEAD_DIM ** (-0.5), q_normed, q_inverse, query_gain)
        key_grad, key_gain_part = norm_backward(dk_rounded, k_normed, k_inverse, key_gain)
        return (attended, query_grad.astype(jnp.bfloat16).reshape(SEQ_LEN, HEADS * HEAD_DIM), key_grad.astype(jnp.bfloat16).reshape(SEQ_LEN, KV_HEADS * HEAD_DIM), value_grad, query_gain_part, key_gain_part)
    results = lax.map(one_sequence, (segment_ids, queries, keys, values, out_grad))
    factor = (SEQS * SEQ_LEN) ** (-0.5)
    return (results[0], results[1], results[2], results[3], lax.optimization_barrier(jnp.sum(results[4], 0)) * factor, lax.optimization_barrier(jnp.sum(results[5], 0)) * factor)
```

```python
import functools

import jax
import jax.numpy as jnp
from jax import lax
from jax.experimental import pallas as pl
from jax.experimental.pallas import tpu as pltpu
from jax.sharding import PartitionSpec as P

HEADS = 8
KV_HEADS = 4
HEAD_DIM = 256
WINDOW = 512
GROUPS = HEADS // KV_HEADS
MY_KV = KV_HEADS // 2
EPSILON = 1e-06
BF16 = jnp.bfloat16
F32 = jnp.float32


def call(body, out_shape, flops, moved, name):
    return pl.pallas_call(
        body,
        out_shape=out_shape,
        compiler_params=pltpu.CompilerParams(vmem_limit_bytes=48 * 2**20),
        cost_estimate=pl.CostEstimate(flops=flops, bytes_accessed=moved, transcendentals=0),
        name=name,
    )


def shape(rows, cols, dtype=BF16):
    return jax.ShapeDtypeStruct((rows, cols), dtype)


def core_index():
    return lax.axis_index("ctx") % 2


def cols(first, width):
    return pl.ds(pl.multiple_of(first * HEAD_DIM, HEAD_DIM), width * HEAD_DIM)


def first_payload(keys, values, straight, cross):
    core = core_index()
    for out, side in ((straight, core), (cross, 1 - core)):
        out[:, :HEAD_DIM] = keys[0, :, cols(side * MY_KV, 1)]
        out[:, HEAD_DIM:] = values[0, :, cols(side * MY_KV, 1)]


def swap_payload(keys, values, queries, out_grad, out):
    other = 1 - core_index()
    kv = MY_KV * HEAD_DIM
    out[:, :kv] = keys[0, :, cols(other * MY_KV, MY_KV)]
    out[:, kv : 2 * kv] = values[0, :, cols(other * MY_KV, MY_KV)]
    wide = MY_KV * GROUPS
    out[:, 2 * kv : 4 * kv] = queries[0, :, cols(other * wide, wide)]
    out[:, 4 * kv :] = out_grad[0, :, cols(other * wide, wide)]


def second_payload(keys, values, swapped, out):
    core = core_index()
    rows = keys.shape[1]
    kv = MY_KV * HEAD_DIM
    out[:rows, :HEAD_DIM] = keys[0, :, cols(core * MY_KV + 1, 1)]
    out[:rows, HEAD_DIM:] = values[0, :, cols(core * MY_KV + 1, 1)]
    out[rows:, :HEAD_DIM] = swapped[:, HEAD_DIM : 2 * HEAD_DIM]
    out[rows:, HEAD_DIM:] = swapped[:, kv + HEAD_DIM : kv + 2 * HEAD_DIM]


def normalize(field):
    inverse = lax.rsqrt(jnp.mean(field * field, -1, keepdims=True) + EPSILON)
    return field * inverse, inverse


def dot(left, right, over):
    return lax.dot_general(left, right, ((over[:1], over[1:]), ((), ())), preferred_element_type=F32)


def attend(
    chunk, segments, queries, out_grad, keys, values, swapped, near_a, near_b, far, query_gain, key_gain,
    own_attended, own_query_grad, own_part, swap_out, near_part, far_part, gains,
):
    core = core_index()
    chip = lax.axis_index("ctx") // 2
    rows = queries.shape[1]
    pair = 2 * rows
    kv = MY_KV * HEAD_DIM
    wide = GROUPS * HEAD_DIM
    gain_q = query_gain[...]
    gain_k = key_gain[...]

    def segment(tile, half):
        block = 2 * (chip + tile - 2) + jnp.where(half == 0, core, 1 - core)
        first = pl.multiple_of(jnp.maximum(block, 0) * rows, rows)
        return jnp.where(block >= 0, segments[:, pl.ds(first, rows)], -1)

    key_seg = jnp.concatenate([segment(tile, half) for tile in range(3) for half in range(2)], 1)
    query_seg = jnp.concatenate(
        [jnp.broadcast_to(segment(2, half), (rows, rows)).T[:, :1] for half in range(2)], 0
    )

    def place(index):
        half = (index // rows) % 2
        return index % rows + rows * jnp.where(half == 0, core, 1 - core) + (index // pair) * pair

    query_place = place(lax.broadcasted_iota(jnp.int32, (pair, 1), 0)) + 2 * pair
    key_place = place(lax.broadcasted_iota(jnp.int32, (1, 3 * pair), 1))
    behind = query_place - key_place
    live = (query_seg == key_seg) & (behind >= 0) & (behind < WINDOW)
    live = jnp.concatenate([live] * GROUPS, 0)

    own_head = core * MY_KV + chunk
    at_k = slice(chunk * HEAD_DIM, (chunk + 1) * HEAD_DIM)
    at_v = slice(kv + chunk * HEAD_DIM, kv + (chunk + 1) * HEAD_DIM)
    band_k = jnp.concatenate(
        [far[:, :HEAD_DIM], near_a[:, :HEAD_DIM], near_b[:, :HEAD_DIM], keys[0, :, cols(own_head, 1)], swapped[:, at_k]], 0
    )
    band_v = jnp.concatenate(
        [far[:, HEAD_DIM:], near_a[:, HEAD_DIM:], near_b[:, HEAD_DIM:], values[0, :, cols(own_head, 1)], swapped[:, at_v]], 0
    )
    k_normed, _ = normalize(band_k.astype(F32))
    k_rounded = (k_normed * gain_k).astype(BF16)

    def heads(field, base):
        first = own_head * GROUPS
        return jnp.concatenate(
            [
                part
                for g in range(GROUPS)
                for part in (
                    field[0, :, cols(first + g, 1)],
                    swapped[:, base + chunk * wide + g * HEAD_DIM : base + chunk * wide + (g + 1) * HEAD_DIM],
                )
            ],
            0,
        )

    q_normed, q_inverse = normalize(heads(queries, 2 * kv).astype(F32))
    q_scaled = (q_normed * gain_q * HEAD_DIM ** (-0.5)).astype(BF16)
    grads = heads(out_grad, 4 * kv)

    scores = dot(q_scaled, k_rounded, (1, 1))
    weights = jnp.where(live, jnp.exp(scores), 0.0)
    probs = weights * (1.0 / jnp.sum(weights, -1, keepdims=True))
    probs_low = probs.astype(BF16)
    attended = dot(probs_low, band_v, (1, 0)).astype(BF16)
    dprob = dot(grads, band_v, (1, 1))
    centre = jnp.sum(probs * dprob, -1, keepdims=True)
    dscore = (probs * (dprob - centre)).astype(BF16)
    key_parts = dot(dscore, q_scaled, (0, 0))
    value_parts = dot(probs_low, grads, (0, 0))
    far_part[:, :HEAD_DIM] = key_parts[:pair].astype(BF16)
    far_part[:, HEAD_DIM:] = value_parts[:pair].astype(BF16)
    near_part[:, :HEAD_DIM] = key_parts[pair : 2 * pair]
    near_part[:, HEAD_DIM:] = value_parts[pair : 2 * pair]
    own_part[:, :HEAD_DIM] = key_parts[2 * pair : 2 * pair + rows]
    own_part[:, HEAD_DIM:] = value_parts[2 * pair : 2 * pair + rows]
    swap_out[:, 2 * wide : 2 * wide + HEAD_DIM] = key_parts[2 * pair + rows :].astype(BF16)
    swap_out[:, 2 * wide + HEAD_DIM :] = value_parts[2 * pair + rows :].astype(BF16)

    dq = dot(dscore, k_rounded, (1, 0)) * HEAD_DIM ** (-0.5)
    scaled = dq * gain_q
    query_grad = q_inverse * (scaled - q_normed * jnp.mean(scaled * q_normed, -1, keepdims=True))
    query_grad = query_grad.astype(BF16)
    for g in range(GROUPS):
        here = slice(g * HEAD_DIM, (g + 1) * HEAD_DIM)
        top = g * pair
        own_attended[:, here] = attended[top : top + rows]
        own_query_grad[:, here] = query_grad[top : top + rows]
        swap_out[:, here] = attended[top + rows : top + pair]
        swap_out[:, wide + g * HEAD_DIM : wide + (g + 1) * HEAD_DIM] = query_grad[top + rows : top + pair]
    gains[0:1, :] = jnp.sum(dq * q_normed, 0, keepdims=True)
    gains[1:2, :] = jnp.sum(key_parts * k_normed, 0, keepdims=True)


def assemble(att_0, att_1, grad_0, grad_1, swap_0, swap_1, attended, query_grad):
    core = core_index()
    wide = GROUPS * HEAD_DIM
    for chunk, (att, grad, swap) in enumerate(((att_0, grad_0, swap_0), (att_1, grad_1, swap_1))):
        mine = cols((core * MY_KV + chunk) * GROUPS, GROUPS)
        other = cols(((1 - core) * MY_KV + chunk) * GROUPS, GROUPS)
        attended[0, :, mine] = att[...]
        query_grad[0, :, mine] = grad[...]
        attended[0, :, other] = swap[:, :wide]
        query_grad[0, :, other] = swap[:, wide : 2 * wide]


def finish(
    keys, key_gain, part_0, part_1, swap_0, swap_1, straight_0, straight_1, cross_0, cross_1, key_grad, value_grad
):
    core = core_index()
    gain_k = key_gain[...]
    base = 2 * GROUPS * HEAD_DIM
    for chunk, (part, swap, straight, cross) in enumerate(
        ((part_0, swap_0, straight_0, cross_0), (part_1, swap_1, straight_1, cross_1))
    ):
        for side, local, arrived in (
            (core, part[...], straight),
            (1 - core, swap[:, base:].astype(F32), cross),
        ):
            here = cols(side * MY_KV + chunk, 1)
            total = local + arrived[...].astype(F32)
            normed, inverse = normalize(keys[0, :, here].astype(F32))
            scaled = total[:, :HEAD_DIM] * gain_k
            grad = inverse * (scaled - normed * jnp.mean(scaled * normed, -1, keepdims=True))
            key_grad[0, :, here] = grad.astype(BF16)
            value_grad[0, :, here] = total[:, HEAD_DIM:].astype(BF16)


def shards(segment_ids, queries, keys, values, query_gain, key_gain, out_grad):
    rows = queries.shape[1]
    pair = 2 * rows
    size = lax.axis_size("ctx")
    kv = MY_KV * HEAD_DIM
    wide = GROUPS * HEAD_DIM
    gain_q = query_gain.reshape(1, HEAD_DIM)
    gain_k = key_gain.reshape(1, HEAD_DIM)

    def move(field, by, cross=False):
        pairs = [(i, (i ^ 1 if cross else i) + by) for i in range(size) if 0 <= (i ^ 1 if cross else i) + by < size]
        return lax.ppermute(field, "ctx", pairs)

    straight, cross = call(
        first_payload, (shape(rows, 2 * HEAD_DIM),) * 2, 0, 2**19, "first_payload"
    )(keys, values)
    near_a0 = move(straight, 2)
    near_b0 = move(cross, 2, cross=True)
    swapped = call(swap_payload, shape(rows, 6 * kv), 0, 3 * 2**19, "swap_payload")(keys, values, queries, out_grad)
    swapped = move(swapped, 0, cross=True)
    near_1 = call(second_payload, shape(pair, 2 * HEAD_DIM), 0, 2**19, "second_payload")(keys, values, swapped)
    near_1 = move(near_1, 2)
    far_0 = move(jnp.concatenate([near_a0, near_b0], 0), 2)
    far_1 = move(near_1, 2)

    def chunk_call(chunk, near_a, near_b, far):
        return call(
            functools.partial(attend, chunk),
            (
                shape(rows, wide),
                shape(rows, wide),
                shape(rows, 2 * HEAD_DIM, F32),
                shape(rows, 2 * wide + 2 * HEAD_DIM),
                shape(pair, 2 * HEAD_DIM, F32),
                shape(pair, 2 * HEAD_DIM),
                shape(2, HEAD_DIM, F32),
            ),
            6 * 2 * GROUPS * pair * 3 * pair * HEAD_DIM,
            4 * 2**20,
            "attend",
        )(segment_ids, queries, out_grad, keys, values, swapped, near_a, near_b, far, gain_q, gain_k)

    def descend(near_part, far_part):
        arrived = move(far_part, -2)
        total = (near_part + arrived.astype(F32)).astype(BF16)
        return move(total[:rows], -2), move(total[rows:], -2, cross=True)

    att_0, grad_0, part_0, swap_0, near_part_0, far_part_0, gains_0 = chunk_call(0, near_a0, near_b0, far_0)
    straight_0, cross_0 = descend(near_part_0, far_part_0)
    swap_0 = move(swap_0, 0, cross=True)
    att_1, grad_1, part_1, swap_1, near_part_1, far_part_1, gains_1 = chunk_call(1, near_1[:rows], near_1[rows:], far_1)
    straight_1, cross_1 = descend(near_part_1, far_part_1)
    swap_1 = move(swap_1, 0, cross=True)

    gains = lax.all_gather(gains_0 + gains_1, ("dp", "ctx"))
    attended, query_grad = call(
        assemble, (jax.ShapeDtypeStruct(queries.shape, BF16),) * 2, 0, 2 * 2**20, "assemble"
    )(att_0, att_1, grad_0, grad_1, swap_0, swap_1)
    key_grad, value_grad = call(
        finish, (jax.ShapeDtypeStruct(keys.shape, BF16),) * 2, 0, 2 * 2**20, "finish"
    )(keys, gain_k, part_0, part_1, swap_0, swap_1, straight_0, straight_1, cross_0, cross_1)

    factor = (lax.axis_size("dp") * queries.shape[0] * size * rows) ** (-0.5)
    gains = jnp.sum(gains, 0) * factor
    return attended, query_grad, key_grad, value_grad, gains[0], gains[1]


def solution(mesh):
    block = P("dp", "ctx", None)
    return jax.shard_map(
        shards,
        mesh=mesh,
        in_specs=(P("dp", None), block, block, block, P(), P(), block),
        out_specs=(block, block, block, block, P(), P()),
        check_vma=False,
    )
```

```python
import functools

import jax
import jax.numpy as jnp
from jax import lax
from jax.experimental import pallas as pl
from jax.experimental.pallas import tpu as pltpu
from jax.sharding import PartitionSpec as P

HEADS = 8
KV_HEADS = 4
HEAD_DIM = 256
WINDOW = 512
GREACH = 4
GROUPS = HEADS // KV_HEADS
EPSILON = 1e-06
BF16 = jnp.bfloat16
F32 = jnp.float32
CHUNKS = ((0, 1), (1, 1), (2, 1), (3, 1))
LAG = 2

VMEM = pl.BlockSpec(memory_space=pltpu.VMEM)
ANY = pl.BlockSpec(memory_space=pl.ANY)


def call(body, name, ins, outs, after=(), flops=0, moved=2**18, in_specs=None, out_specs=None, **more):
    names = list(ins)

    def kernel(*refs):
        used = len(names) + len(after)
        body(*refs[: len(names)], *refs[used:])

    specs = [(in_specs or {}).get(key, VMEM) for key in names] + [ANY] * len(after)
    return pl.pallas_call(
        kernel,
        out_shape=list(outs.values()),
        in_specs=specs,
        out_specs=[(out_specs or {}).get(key, VMEM) for key in outs],
        compiler_params=pltpu.CompilerParams(vmem_limit_bytes=40 * 2**20),
        cost_estimate=pl.CostEstimate(flops=flops, bytes_accessed=moved, transcendentals=0),
        name=name,
        **more,
    )(*ins.values(), *after)


def shape(rows, cols, dtype=BF16):
    return jax.ShapeDtypeStruct((rows, cols), dtype)


def core_index():
    return lax.axis_index("ctx") % 2


def payload(chunks, places, keys, values, *rest):
    outs, sems = rest[:-1], rest[-1]
    copies = []
    for index, ((first, count), (out, at)) in enumerate(zip(chunks, places)):
        here = pl.ds(first * HEAD_DIM, count * HEAD_DIM)
        for side, field in enumerate((keys, values)):
            to = outs[out].at[:, pl.ds(at + side * count * HEAD_DIM, count * HEAD_DIM)]
            copies.append(pltpu.make_async_copy(field.at[0, :, here], to, sems.at[2 * index + side]))
    for copy in copies:
        copy.start()
    for copy in copies:
        copy.wait()


def normalize(field):
    inverse = lax.rsqrt(jnp.mean(field * field, -1, keepdims=True) + EPSILON)
    return field * inverse, inverse


def dot(left, right, over):
    return lax.dot_general(left, right, ((over[:1], over[1:]), ((), ())), preferred_element_type=F32)


def attend(
    count, at_own, at_x, at_near, at_y, at_far, segments, queries, out_grad, own, across_x, arrived_near, across_y, arrived_far,
    query_gain, key_gain, *rest,
):
    attended, query_grad, part_own, part_near, part_far, part_swap, gains = rest[-7:]
    position = lax.axis_index("ctx")
    rows = queries.shape[1]
    band = (GREACH + 1) * rows
    gain_q = query_gain[...]
    gain_k = key_gain[...]

    def segment(distance):
        block = position - distance
        first = pl.multiple_of(jnp.maximum(block, 0) * rows, rows)
        return jnp.where(block >= 0, segments[:, pl.ds(first, rows)], -1)

    key_seg = jnp.concatenate([segment(distance) for distance in range(GREACH, -1, -1)], 1)
    query_seg = jnp.broadcast_to(segment(0), (rows, rows)).T[:, :1]
    back = (
        lax.broadcasted_iota(jnp.int32, (rows, band), 0)
        - lax.broadcasted_iota(jnp.int32, (rows, band), 1)
        + GREACH * rows
    )
    live = (query_seg == key_seg) & (back >= 0) & (back < WINDOW)
    live = jnp.concatenate([live] * GROUPS, 0)

    query_gains = jnp.zeros((1, HEAD_DIM), F32)
    key_gains = jnp.zeros((1, HEAD_DIM), F32)
    blocks = ((arrived_far, at_far), (across_y, at_y), (arrived_near, at_near), (across_x, at_x), (own, at_own))

    def band_of(index):
        return jnp.concatenate(
            [field[:, at + index * HEAD_DIM : at + (index + 1) * HEAD_DIM] for field, at in blocks], 0
        )

    for head in range(count):
        at_k = slice(head * HEAD_DIM, (head + 1) * HEAD_DIM)
        at_v = slice((count + head) * HEAD_DIM, (count + head + 1) * HEAD_DIM)
        at_q = [slice((head * GROUPS + g) * HEAD_DIM, (head * GROUPS + g + 1) * HEAD_DIM) for g in range(GROUPS)]
        band_v = band_of(count + head)
        k_normed, _ = normalize(band_of(head).astype(F32))
        k_rounded = (k_normed * gain_k).astype(BF16)
        q_normed, q_inverse = normalize(jnp.concatenate([queries[0, :, at] for at in at_q], 0).astype(F32))
        q_scaled = (q_normed * gain_q * HEAD_DIM ** (-0.5)).astype(BF16)
        grads = jnp.concatenate([out_grad[0, :, at] for at in at_q], 0)

        scores = dot(q_scaled, k_rounded, (1, 1))
        weights = jnp.where(live, jnp.exp(scores), 0.0)
        probs = weights * (1.0 / jnp.sum(weights, -1, keepdims=True))
        probs_low = probs.astype(BF16)
        dprob = dot(grads, band_v, (1, 1))
        centre = jnp.sum(probs * dprob, -1, keepdims=True)
        dscore = (probs * (dprob - centre)).astype(BF16)
        key_parts = dot(dscore, q_scaled, (0, 0))
        value_parts = dot(probs_low, grads, (0, 0))
        for at, parts in ((at_k, key_parts), (at_v, value_parts)):
            part_far[:, at] = parts[:rows]
            part_swap[:rows, at] = parts[rows : 2 * rows].astype(BF16)
            part_near[:, at] = parts[2 * rows : 3 * rows]
            part_swap[rows:, at] = parts[3 * rows : 4 * rows].astype(BF16)
            part_own[:, at] = parts[4 * rows :]

        output = dot(probs_low, band_v, (1, 0)).astype(BF16)
        dq = dot(dscore, k_rounded, (1, 0)) * HEAD_DIM ** (-0.5)
        scaled = dq * gain_q
        grad = q_inverse * (scaled - q_normed * jnp.mean(scaled * q_normed, -1, keepdims=True))
        grad = grad.astype(BF16)
        for g, at in enumerate(at_q):
            attended[0, :, at] = output[g * rows : (g + 1) * rows]
            query_grad[0, :, at] = grad[g * rows : (g + 1) * rows]
        query_gains = query_gains + jnp.sum(dq * q_normed, 0, keepdims=True)
        key_gains = key_gains + jnp.sum(key_parts * k_normed, 0, keepdims=True)
    gains[0:1, :] = query_gains
    gains[1:2, :] = key_gains


def finish(count, at, keys, key_gain, part_own, swapped, arrived, *rest):
    key_grad, value_grad = rest[-2:]
    rows = part_own.shape[0]
    gain_k = key_gain[...]
    for head in range(count):

        def total(index):
            here = slice(index * HEAD_DIM, (index + 1) * HEAD_DIM)
            there = slice(at + index * HEAD_DIM, at + (index + 1) * HEAD_DIM)
            extra = jnp.where(core_index() == 0, swapped[rows:, here].astype(F32), 0.0)
            return part_own[:, here] + extra + arrived[:, there].astype(F32)

        out = slice(head * HEAD_DIM, (head + 1) * HEAD_DIM)
        normed, inverse = normalize(keys[0, :, out].astype(F32))
        scaled = total(head) * gain_k
        grad = inverse * (scaled - normed * jnp.mean(scaled * normed, -1, keepdims=True))
        key_grad[0, :, out] = grad.astype(BF16)
        value_grad[0, :, out] = total(count + head).astype(BF16)


def columns(rows, width, first):
    return pl.BlockSpec((1, rows, width), lambda i: (0, 0, first // width))


def move(field, axis, target):
    size = lax.axis_size(axis)
    return lax.ppermute(field, axis, [(i, target(i)) for i in range(size) if 0 <= target(i) < size])


def up(field):
    return move(field, "ctx", lambda i: i + 2)


def down(field):
    return move(field, "ctx", lambda i: i - 2)


def swap(field):
    return move(field, "ctx", lambda i: i ^ 1)


def total_over(field, axis):
    step = 1
    while step < lax.axis_size(axis):
        field = field + move(field, axis, lambda i: i ^ step)
        step *= 2
    return field


def shards(segment_ids, queries, keys, values, query_gain, key_gain, out_grad):
    rows = queries.shape[1]
    gain_q = query_gain.reshape(1, HEAD_DIM)
    gain_k = key_gain.reshape(1, HEAD_DIM)
    amount = len(CHUNKS)
    width = [2 * count * HEAD_DIM for _, count in CHUNKS] + [0] * LAG
    pinned = [pltpu.with_memory_space_constraint(field, pltpu.HBM) for field in (keys, values)]

    def gather(chunks, after=(), joined=False):
        each = [2 * count * HEAD_DIM for _, count in chunks]
        places = [(0, sum(each[:i])) if joined else (i, 0) for i in range(len(chunks))]
        return call(
            functools.partial(payload, chunks, places),
            "payload",
            dict(keys=pinned[0], values=pinned[1]),
            {i: shape(rows, wide) for i, wide in enumerate([sum(each)] if joined else each)},
            after,
            in_specs=dict(keys=ANY, values=ANY),
            scratch_shapes=[pltpu.SemaphoreType.DMA((2 * len(chunks),))],
        )

    own = list(gather(CHUNKS[:LAG], joined=True))
    arrived = up(own[0])
    near = {chunk: (arrived, sum(width[:chunk])) for chunk in range(LAG)}
    own = [(own[0], sum(width[:chunk])) for chunk in range(LAG)]
    own += [(field, 0) for field in gather(CHUNKS[LAG:], own[0][:1])]
    far, next_behind, third_behind = {}, {}, {}

    def climb(steps, after=()):
        ins, outs, jobs = {}, {}, []

        def use(place, chunk):
            field, at = place
            key = next((key for key, value in ins.items() if value is field), f"in{len(ins)}")
            ins[key] = field
            return key, slice(at, at + width[chunk])

        across = 0
        for step in steps:
            rise = 0
            if step + LAG < amount:
                jobs.append((f"rise{step}", rise, use(own[step + LAG], step + LAG), None))
                rise += width[step + LAG]
            if step < amount:
                jobs.append((f"rise{step}", rise, use(near[step], step), None))
                outs[f"rise{step}"] = shape(rows, rise + width[step])
                jobs.append(("across", across, use(own[step], step), use(near[step], step)))
                next_behind[step] = across
                across += width[step]
            if step >= LAG:
                chunk = step - LAG
                jobs.append(("across", across, use(near[chunk], chunk), use(far[chunk], chunk)))
                third_behind[chunk] = across
                across += width[chunk]
        outs["across"] = shape(rows, across)

        def body(*refs):
            ref = dict(zip(list(ins) + list(outs), refs))
            for to, at, (key, here), other in jobs:
                value = ref[key][:, here]
                if other is not None:
                    value = jnp.where(core_index() == 0, value, ref[other[0]][:, other[1]])
                ref[to][:, at : at + value.shape[1]] = value

        made = dict(zip(outs, call(body, "climb", ins, outs, after)))
        exchanged = swap(made["across"])
        for step in steps:
            if step < amount:
                arrived = up(made[f"rise{step}"])
                ahead = 0
                if step + LAG < amount:
                    near[step + LAG] = (arrived, 0)
                    ahead = width[step + LAG]
                far[step] = (arrived, ahead)
                next_behind[step] = (exchanged, next_behind[step])
            if step >= LAG:
                third_behind[step - LAG] = (exchanged, third_behind[step - LAG])
        return [made["across"]]

    parts, sunk = [], {}

    def sink(step, after=()):
        fresh, older = step < amount, step >= LAG
        mine, below = width[step], width[step - LAG] if older else 0
        ins = {}
        if fresh:
            ins.update(far=parts[step]["far"], swapped=parts[step]["swap"])
        if older:
            ins.update(
                near=parts[step - LAG]["near"], swapped_old=parts[step - LAG]["swap"], arrived=sunk[step - LAG]
            )

        def body(*refs):
            ref = dict(zip(list(ins) + ["out"], refs))
            first = core_index() == 0
            if fresh:
                extra = jnp.where(first, 0.0, ref["swapped"][:rows, :].astype(F32))
                ref["out"][:, :mine] = (ref["far"][...] + extra).astype(BF16)
            if older:
                swapped = ref["swapped_old"]
                extra = jnp.where(first, swapped[:rows, :], swapped[rows:, :]).astype(F32)
                arrived = ref["arrived"][:, :below].astype(F32)
                ref["out"][:, mine:] = (ref["near"][...] + extra + arrived).astype(BF16)

        (total,) = call(body, "sink", ins, dict(out=shape(rows, mine + below)), after)
        sunk[step] = down(total)
        return total

    outputs, key_outputs, gains, last = [], [], 0.0, []
    order = climb(range(LAG))
    for chunk, (first, count) in enumerate(CHUNKS):
        order = climb([chunk + LAG], order)
        wide = columns(rows, GROUPS * count * HEAD_DIM, GROUPS * first * HEAD_DIM)
        held = (own, next_behind, near, third_behind, far)
        *outputs, part_own, part_near, part_far, part_swap, chunk_gains = call(
            functools.partial(attend, count, *(place[chunk][1] for place in held)),
            "attend",
            dict(
                segments=segment_ids, queries=queries, out_grad=out_grad, own=own[chunk][0],
                **{f"behind{i}": place[chunk][0] for i, place in enumerate(held[1:])}, gain_q=gain_q, gain_k=gain_k,
            ),
            dict(
                attended=jax.ShapeDtypeStruct(queries.shape, BF16),
                query_grad=jax.ShapeDtypeStruct(queries.shape, BF16),
                own=shape(rows, width[chunk], F32), near=shape(rows, width[chunk], F32),
                far=shape(rows, width[chunk], F32), swap=shape(2 * rows, width[chunk]),
                gains=shape(2, HEAD_DIM, F32),
            ),
            [*outputs, *last, *([sunk[chunk - LAG]] if chunk >= LAG else [])],
            flops=12 * GROUPS * rows * (GREACH + 1) * rows * count * HEAD_DIM,
            moved=2**21,
            grid=(1,),
            in_specs=dict(queries=wide, out_grad=wide),
            out_specs=dict(attended=wide, query_grad=wide),
            input_output_aliases={10 + i: i for i in range(len(outputs))},
        )
        gains = gains + chunk_gains
        parts.append(dict(own=part_own, near=part_near, far=part_far, swap=swap(part_swap)))
        last = [sink(chunk)]

    for step in range(amount, amount + LAG):
        sink(step)
    for chunk, (first, count) in enumerate(CHUNKS):
        narrow = columns(rows, count * HEAD_DIM, first * HEAD_DIM)
        key_outputs = call(
            functools.partial(finish, count, width[chunk + LAG]),
            "finish",
            dict(
                keys=keys, gain=gain_k, own=parts[chunk]["own"], swapped=parts[chunk]["swap"], arrived=sunk[chunk + LAG]
            ),
            dict(
                key_grad=jax.ShapeDtypeStruct(keys.shape, BF16), value_grad=jax.ShapeDtypeStruct(keys.shape, BF16)
            ),
            key_outputs,
            grid=(1,),
            in_specs=dict(keys=narrow),
            out_specs=dict(key_grad=narrow, value_grad=narrow),
            input_output_aliases={5 + i: i for i in range(len(key_outputs))},
        )

    gains = total_over(total_over(gains, "ctx"), "dp")
    factor = (lax.axis_size("dp") * queries.shape[0] * lax.axis_size("ctx") * rows) ** (-0.5)
    gains = gains * factor
    return *outputs, *key_outputs, gains[0], gains[1]


def solution(mesh):
    block = P("dp", "ctx", None)
    return jax.shard_map(
        shards,
        mesh=mesh,
        in_specs=(P("dp", None), block, block, block, P(), P(), block),
        out_specs=(block, block, block, block, P(), P()),
        check_vma=False,
    )
```

```python
import functools

import jax
import jax.numpy as jnp
from jax import lax
from jax.experimental import pallas as pl
from jax.experimental.pallas import tpu as pltpu
from jax.sharding import PartitionSpec as P

HEADS = 8
KV_HEADS = 4
HEAD_DIM = 256
WINDOW = 512
GREACH = 4
GROUPS = HEADS // KV_HEADS
EPSILON = 1e-06
BF16 = jnp.bfloat16
F32 = jnp.float32
CHUNKS = ((0, 1), (1, 1), (2, 1), (3, 1))
LAG = 2

PIECES = 4

VMEM = pl.BlockSpec(memory_space=pltpu.VMEM)
ANY = pl.BlockSpec(memory_space=pl.ANY)


def call(body, name, ins, outs, after=(), cost=0, in_specs=None, out_specs=None, **more):
    names = list(ins)

    def kernel(*refs):
        used = len(names) + len(after)
        body(*refs[: len(names)], *refs[used:])

    specs = [(in_specs or {}).get(key, VMEM) for key in names] + [ANY] * len(after)
    return pl.pallas_call(
        kernel,
        out_shape=list(outs.values()),
        in_specs=specs,
        out_specs=[(out_specs or {}).get(key, VMEM) for key in outs],
        compiler_params=pltpu.CompilerParams(vmem_limit_bytes=40 * 2**20),
        cost_estimate=pl.CostEstimate(flops=cost, bytes_accessed=1, transcendentals=0),
        name=name,
        **more,
    )(*ins.values(), *after)


def shape(rows, cols, dtype=BF16):
    return jax.ShapeDtypeStruct((rows, cols), dtype)


def core_index():
    return lax.axis_index("ctx") % 2


def payload(chunks, places, keys, values, *rest):
    outs, sems = rest[:-1], rest[-1]
    copies = []
    for index, ((first, count), (out, at)) in enumerate(zip(chunks, places)):
        here = pl.ds(first * HEAD_DIM, count * HEAD_DIM)
        for side, field in enumerate((keys, values)):
            to = pl.ds(at + side * count * HEAD_DIM, count * HEAD_DIM)
            for piece in range(PIECES):
                share = field.shape[1] // PIECES
                rows = pl.ds(piece * share, share)
                sem = sems.at[(2 * index + side) * PIECES + piece]
                copies.append(pltpu.make_async_copy(field.at[0, rows, here], outs[out].at[rows, to], sem))
    for copy in copies:
        copy.start()
    for copy in copies:
        copy.wait()


def normalize(field):
    inverse = lax.rsqrt(jnp.mean(field * field, -1, keepdims=True) + EPSILON)
    return field * inverse, inverse


def dot(left, right, over):
    return lax.dot_general(left, right, ((over[:1], over[1:]), ((), ())), preferred_element_type=F32)


def attend(
    first, count, at_own, at_x, at_near, at_y, at_far, segments, queries, out_grad, own, across_x, arrived_near, across_y, arrived_far,
    query_gain, key_gain, *rest,
):
    attended, query_grad, part_own, part_near, part_far, part_third, part_next, gains = rest
    position = lax.axis_index("ctx")
    rows = queries.shape[1]
    band = (GREACH + 1) * rows
    gain_q = query_gain[...]
    gain_k = key_gain[...]

    def segment(distance):
        block = position - distance
        first = pl.multiple_of(jnp.maximum(block, 0) * rows, rows)
        return jnp.where(block >= 0, segments[:, pl.ds(first, rows)], -1)

    key_seg = jnp.concatenate([segment(distance) for distance in range(GREACH, -1, -1)], 1)
    query_seg = jnp.broadcast_to(segment(0), (rows, rows)).T[:, :1]
    back = (
        lax.broadcasted_iota(jnp.int32, (rows, band), 0)
        - lax.broadcasted_iota(jnp.int32, (rows, band), 1)
        + GREACH * rows
    )
    live = (query_seg == key_seg) & (back >= 0) & (back < WINDOW)
    live = jnp.concatenate([live] * GROUPS, 0)

    query_gains = jnp.zeros((1, HEAD_DIM), F32)
    key_gains = jnp.zeros((1, HEAD_DIM), F32)
    blocks = ((arrived_far, at_far), (across_y, at_y), (arrived_near, at_near), (across_x, at_x), (own, at_own))

    def band_of(index):
        return jnp.concatenate(
            [field[:, at + index * HEAD_DIM : at + (index + 1) * HEAD_DIM] for field, at in blocks], 0
        )

    for head in range(count):
        at_k = slice(head * HEAD_DIM, (head + 1) * HEAD_DIM)
        at_v = slice((count + head) * HEAD_DIM, (count + head + 1) * HEAD_DIM)
        at_q = [slice((head * GROUPS + g) * HEAD_DIM, (head * GROUPS + g + 1) * HEAD_DIM) for g in range(GROUPS)]
        from_q = [slice(at.start + first * GROUPS * HEAD_DIM, at.stop + first * GROUPS * HEAD_DIM) for at in at_q]
        band_v = band_of(count + head)
        k_normed, _ = normalize(band_of(head).astype(F32))
        k_rounded = (k_normed * gain_k).astype(BF16)
        q_normed, q_inverse = normalize(jnp.concatenate([queries[0, :, at] for at in from_q], 0).astype(F32))
        q_scaled = (q_normed * gain_q * HEAD_DIM ** (-0.5)).astype(BF16)
        grads = jnp.concatenate([out_grad[0, :, at] for at in from_q], 0)

        scores = dot(q_scaled, k_rounded, (1, 1))
        weights = jnp.where(live, jnp.exp(scores), 0.0)
        probs = weights * (1.0 / jnp.sum(weights, -1, keepdims=True))
        probs_low = probs.astype(BF16)
        dprob = dot(grads, band_v, (1, 1))
        centre = jnp.sum(probs * dprob, -1, keepdims=True)
        dscore = (probs * (dprob - centre)).astype(BF16)
        key_parts = dot(dscore, q_scaled, (0, 0))
        value_parts = dot(probs_low, grads, (0, 0))
        for at, parts in ((at_k, key_parts), (at_v, value_parts)):
            part_far[:, at] = parts[:rows]
            part_third[:, at] = parts[rows : 2 * rows].astype(BF16)
            part_near[:, at] = parts[2 * rows : 3 * rows]
            part_next[:, at] = parts[3 * rows : 4 * rows].astype(BF16)
            part_own[:, at] = parts[4 * rows :]

        output = dot(probs_low, band_v, (1, 0)).astype(BF16)
        dq = dot(dscore, k_rounded, (1, 0)) * HEAD_DIM ** (-0.5)
        scaled = dq * gain_q
        grad = q_inverse * (scaled - q_normed * jnp.mean(scaled * q_normed, -1, keepdims=True))
        grad = grad.astype(BF16)
        for g, at in enumerate(at_q):
            attended[:, at] = output[g * rows : (g + 1) * rows]
            query_grad[:, at] = grad[g * rows : (g + 1) * rows]
        query_gains = query_gains + jnp.sum(dq * q_normed, 0, keepdims=True)
        key_gains = key_gains + jnp.sum(key_parts * k_normed, 0, keepdims=True)
    gains[0:1, :] = query_gains
    gains[1:2, :] = key_gains


def assemble(*refs):
    amount = len(CHUNKS)
    for index, out in enumerate(refs[-2:]):
        for (first, count), part in zip(CHUNKS, refs[index * amount : (index + 1) * amount]):
            out[0, :, first * GROUPS * HEAD_DIM : (first + count) * GROUPS * HEAD_DIM] = part[...]


def add(left, right, out):
    out[...] = left[...] + right[...]


def finish(count, at, keys, key_gain, part_own, swapped, arrived, *rest):
    key_grad, value_grad = rest[-2:]
    rows = part_own.shape[0]
    gain_k = key_gain[...]
    for head in range(count):

        def total(index):
            here = slice(index * HEAD_DIM, (index + 1) * HEAD_DIM)
            there = slice(at + index * HEAD_DIM, at + (index + 1) * HEAD_DIM)
            extra = jnp.where(core_index() == 0, swapped[:, here].astype(F32), 0.0)
            return part_own[:, here] + extra + arrived[:, there].astype(F32)

        out = slice(head * HEAD_DIM, (head + 1) * HEAD_DIM)
        normed, inverse = normalize(keys[0, :, out].astype(F32))
        scaled = total(head) * gain_k
        grad = inverse * (scaled - normed * jnp.mean(scaled * normed, -1, keepdims=True))
        key_grad[0, :, out] = grad.astype(BF16)
        value_grad[0, :, out] = total(count + head).astype(BF16)


def columns(rows, width, first):
    return pl.BlockSpec((1, rows, width), lambda i: (0, 0, first // width))


def move(field, axis, target):
    size = lax.axis_size(axis)
    return lax.ppermute(field, axis, [(i, target(i)) for i in range(size) if 0 <= target(i) < size])


def up(field):
    return move(field, "ctx", lambda i: i + 2)


def down(field):
    return move(field, "ctx", lambda i: i - 2)


def swap(field):
    return move(field, "ctx", lambda i: i ^ 1)


def total_over(field, axis, first, last, after=()):
    step = first
    while step < min(last, lax.axis_size(axis)):
        (field,) = call(add, "add", dict(a=field, b=move(field, axis, lambda i: i ^ step)), dict(o=field), after)
        step *= 2
    return field


def shards(segment_ids, queries, keys, values, query_gain, key_gain, out_grad):
    rows = queries.shape[1]
    gain_q = query_gain.reshape(1, HEAD_DIM)
    gain_k = key_gain.reshape(1, HEAD_DIM)
    amount = len(CHUNKS)
    width = [2 * count * HEAD_DIM for _, count in CHUNKS] + [0] * LAG
    pinned = [pltpu.with_memory_space_constraint(field, pltpu.HBM) for field in (keys, values)]

    def gather(chunks, after=(), joined=False):
        each = [2 * count * HEAD_DIM for _, count in chunks]
        places = [(0, sum(each[:i])) if joined else (i, 0) for i in range(len(chunks))]
        return call(
            functools.partial(payload, chunks, places),
            "payload",
            dict(keys=pinned[0], values=pinned[1]),
            {i: shape(rows, wide) for i, wide in enumerate([sum(each)] if joined else each)},
            after,
            in_specs=dict(keys=ANY, values=ANY),
            scratch_shapes=[pltpu.SemaphoreType.DMA((2 * len(chunks) * PIECES,))],
        )

    own = list(gather(CHUNKS[:LAG], joined=True))
    arrived = up(own[0])
    near = {chunk: (arrived, sum(width[:chunk])) for chunk in range(LAG)}
    own = [(own[0], sum(width[:chunk])) for chunk in range(LAG)]
    own += [(field, 0) for field in gather(CHUNKS[LAG:], own[0][:1])]
    far, next_behind, third_behind = {}, {}, {}

    def climb(steps, after=()):
        ins, outs, jobs = {}, {}, []

        def use(place, chunk):
            field, at = place
            key = next((key for key, value in ins.items() if value is field), f"in{len(ins)}")
            ins[key] = field
            return key, slice(at, at + width[chunk])

        def exchange(to, kept, chunk, first, second):
            at = outs[to].shape[1] if to in outs else 0
            jobs.append((to, at, use(first[chunk], chunk), use(second[chunk], chunk)))
            outs[to] = shape(rows, at + width[chunk])
            kept[chunk] = (to, at)

        for step in steps:
            rise = 0
            if step + LAG < amount:
                jobs.append((f"rise{step}", rise, use(own[step + LAG], step + LAG), None))
                rise += width[step + LAG]
            if step < amount:
                jobs.append((f"rise{step}", rise, use(near[step], step), None))
                outs[f"rise{step}"] = shape(rows, rise + width[step])
                exchange("next", next_behind, step, own, near)
            if step >= LAG:
                exchange("third", third_behind, step - LAG, near, far)

        def body(*refs):
            ref = dict(zip(list(ins) + list(outs), refs))
            for to, at, (key, here), other in jobs:
                value = ref[key][:, here]
                if other is not None:
                    value = jnp.where(core_index() == 0, value, ref[other[0]][:, other[1]])
                ref[to][:, at : at + value.shape[1]] = value

        made = dict(zip(outs, call(body, "climb", ins, outs, after, cost=10**9 * max(0, steps[0] - LAG))))
        exchanged = {to: swap(made[to]) for to in ("next", "third") if to in made}
        for step in steps:
            if step < amount:
                arrived = up(made[f"rise{step}"])
                ahead = 0
                if step + LAG < amount:
                    near[step + LAG] = (arrived, 0)
                    ahead = width[step + LAG]
                far[step] = (arrived, ahead)
                next_behind[step] = (exchanged["next"], next_behind[step][1])
            if step >= LAG:
                third_behind[step - LAG] = (exchanged["third"], third_behind[step - LAG][1])
        return [next(iter(made.values()))]

    parts, sunk = [], {}

    def sink(step, after=()):
        fresh, older = step < amount, step >= LAG
        mine, below = width[step], width[step - LAG] if older else 0
        ins = {}
        if fresh:
            ins.update(far=parts[step]["far"], third=parts[step]["third"])
        if older:
            chunk = step - LAG
            ins.update(near=parts[chunk]["near"], arrived=sunk[chunk])
            ins.update(third_old=parts[chunk]["third"], next_old=parts[chunk]["next"])

        def body(*refs):
            ref = dict(zip(list(ins) + ["out"], refs))
            first = core_index() == 0
            if fresh:
                extra = jnp.where(first, 0.0, ref["third"][...].astype(F32))
                ref["out"][:, :mine] = (ref["far"][...] + extra).astype(BF16)
            if older:
                extra = jnp.where(first, ref["third_old"][...], ref["next_old"][...]).astype(F32)
                arrived = ref["arrived"][:, :below].astype(F32)
                ref["out"][:, mine:] = (ref["near"][...] + extra + arrived).astype(BF16)

        (total,) = call(body, "sink", ins, dict(out=shape(rows, mine + below)), after)
        sunk[step] = down(total)
        return total

    made, gains, last, token = [], [], [], []
    order = climb(range(LAG))
    for chunk, (first, count) in enumerate(CHUNKS):
        order = climb([chunk + LAG], order + token + ([sunk[chunk - LAG]] if chunk >= LAG else []))
        held = (own, next_behind, near, third_behind, far)
        wide = shape(rows, GROUPS * count * HEAD_DIM)
        whole, low = shape(rows, width[chunk], F32), shape(rows, width[chunk])
        result = call(
            functools.partial(attend, first, count, *(place[chunk][1] for place in held)),
            "attend",
            dict(
                segments=segment_ids, queries=queries, out_grad=out_grad, own=own[chunk][0],
                **{f"behind{i}": place[chunk][0] for i, place in enumerate(held[1:])}, gain_q=gain_q, gain_k=gain_k,
            ),
            dict(
                attended=wide, query_grad=wide, own=whole, near=whole, far=whole, third=low, next=low,
                gains=shape(2, HEAD_DIM, F32),
            ),
            last,
        )
        made.append(result[:2])
        gains.append(result[7])
        token = [result[7]]
        parts.append(
            dict(own=result[2], near=result[3], far=result[4], third=swap(result[5]), next=swap(result[6]))
        )
        last = [sink(chunk, last)]

    for step in range(amount, amount + LAG):
        last = [sink(step, last)]
    key_outputs = []
    for chunk, (first, count) in enumerate(CHUNKS):
        narrow = columns(rows, count * HEAD_DIM, first * HEAD_DIM)
        key_outputs = call(
            functools.partial(finish, count, width[chunk + LAG]),
            "finish",
            dict(
                keys=keys, gain=gain_k, own=parts[chunk]["own"], next=parts[chunk]["next"], arrived=sunk[chunk + LAG]
            ),
            dict(
                key_grad=jax.ShapeDtypeStruct(keys.shape, BF16), value_grad=jax.ShapeDtypeStruct(keys.shape, BF16)
            ),
            key_outputs,
            cost=2**32,
            grid=(1,),
            in_specs=dict(keys=narrow),
            out_specs=dict(key_grad=narrow, value_grad=narrow),
            input_output_aliases={5 + i: i for i in range(len(key_outputs))},
        )
    attended, query_grad = call(
        assemble,
        "assemble",
        {(i, chunk): made[chunk][i] for i in range(2) for chunk in range(amount)},
        dict(a=jax.ShapeDtypeStruct(queries.shape, BF16), b=jax.ShapeDtypeStruct(queries.shape, BF16)),
        last,
    )

    total = gains[0]
    for more in gains[1:]:
        (total,) = call(add, "add", dict(a=total, b=more), dict(o=more))
    total = total_over(total, "dp", 1, lax.axis_size("dp"))
    total = total_over(total, "ctx", 1, 2, last)
    total = total_over(total, "ctx", 2, lax.axis_size("ctx"))
    factor = (lax.axis_size("dp") * queries.shape[0] * lax.axis_size("ctx") * rows) ** (-0.5)
    total = total * factor
    return attended, query_grad, *key_outputs, total[0], total[1]


def solution(mesh):
    block = P("dp", "ctx", None)
    return jax.shard_map(
        shards,
        mesh=mesh,
        in_specs=(P("dp", None), block, block, block, P(), P(), block),
        out_specs=(block, block, block, block, P(), P()),
        check_vma=False,
    )
```

```python
import functools

import jax
import jax.numpy as jnp
from jax import lax
from jax.experimental import pallas as pl
from jax.experimental.pallas import tpu as pltpu
from jax.sharding import PartitionSpec as P

HEADS = 8
KV_HEADS = 4
HEAD_DIM = 256
WINDOW = 512
GREACH = 4
GROUPS = HEADS // KV_HEADS
EPSILON = 1e-06
BF16 = jnp.bfloat16
F32 = jnp.float32
CHUNKS = ((0, 2), (2, 2))
LAG = 2

PIECES = 4

VMEM = pl.BlockSpec(memory_space=pltpu.VMEM)
ANY = pl.BlockSpec(memory_space=pl.ANY)


def call(body, name, ins, outs, after=(), cost=0, in_specs=None, out_specs=None, **more):
    names = list(ins)

    def kernel(*refs):
        used = len(names) + len(after)
        body(*refs[: len(names)], *refs[used:])

    specs = [(in_specs or {}).get(key, VMEM) for key in names] + [ANY] * len(after)
    return pl.pallas_call(
        kernel,
        out_shape=list(outs.values()),
        in_specs=specs,
        out_specs=[(out_specs or {}).get(key, VMEM) for key in outs],
        compiler_params=pltpu.CompilerParams(vmem_limit_bytes=40 * 2**20),
        cost_estimate=pl.CostEstimate(flops=cost, bytes_accessed=1, transcendentals=0),
        name=name,
        **more,
    )(*ins.values(), *after)


def shape(rows, cols, dtype=BF16):
    return jax.ShapeDtypeStruct((rows, cols), dtype)


def core_index():
    return lax.axis_index("ctx") % 2


def payload(chunks, keys, values, *rest):
    extra = len(rest[:-1]) - len(chunks)
    small, outs, kept, sems = rest[: extra // 2], rest[extra // 2 : -1 - extra // 2], rest[-1 - extra // 2 : -1], rest[-1]
    copies = [pltpu.make_async_copy(old, new, sems.at[i]) for i, (old, new) in enumerate(zip(small, kept))]
    for (first, count), out in zip(chunks, outs):
        here = pl.ds(first * HEAD_DIM, count * HEAD_DIM)
        for side, field in enumerate((keys, values)):
            to = pl.ds(side * count * HEAD_DIM, count * HEAD_DIM)
            for piece in range(PIECES):
                share = field.shape[1] // PIECES
                rows = pl.ds(piece * share, share)
                sem = sems.at[len(copies)]
                copies.append(pltpu.make_async_copy(field.at[0, rows, here], out.at[rows, to], sem))
    for copy in copies:
        copy.start()
    for copy in copies:
        copy.wait()


def normalize(field):
    inverse = lax.rsqrt(jnp.mean(field * field, -1, keepdims=True) + EPSILON)
    return field * inverse, inverse


def dot(left, right, over):
    return lax.dot_general(left, right, ((over[:1], over[1:]), ((), ())), preferred_element_type=F32)


def attend(
    first, count, at_own, at_x, at_near, at_far, segments, queries, out_grad, own, across_x, arrived_near, arrived_far,
    across_k, across_v,    query_gain, key_gain, *rest,
):
    attended, query_grad, part_own, part_near, part_far, third_k, third_v, part_next, gains = rest
    position = lax.axis_index("ctx")
    rows = queries.shape[1]
    band = (GREACH + 1) * rows
    gain_q = query_gain[...]
    gain_k = key_gain[...]

    def segment(distance):
        block = position - distance
        first = pl.multiple_of(jnp.maximum(block, 0) * rows, rows)
        return jnp.where(block >= 0, segments[:, pl.ds(first, rows)], -1)

    key_seg = jnp.concatenate([segment(distance) for distance in range(GREACH, -1, -1)], 1)
    query_seg = jnp.broadcast_to(segment(0), (rows, rows)).T[:, :1]
    back = (
        lax.broadcasted_iota(jnp.int32, (rows, band), 0)
        - lax.broadcasted_iota(jnp.int32, (rows, band), 1)
        + GREACH * rows
    )
    live = (query_seg == key_seg) & (back >= 0) & (back < WINDOW)
    live = jnp.concatenate([live] * GROUPS, 0)

    query_gains = jnp.zeros((1, HEAD_DIM), F32)
    key_gains = jnp.zeros((1, HEAD_DIM), F32)

    def band_of(index):
        third = (across_k, 0) if index < count else (across_v, -count * HEAD_DIM)
        blocks = ((arrived_far, at_far), third, (arrived_near, at_near), (across_x, at_x), (own, at_own))
        return jnp.concatenate(
            [field[:, at + index * HEAD_DIM : at + (index + 1) * HEAD_DIM] for field, at in blocks], 0
        )

    for head in range(count):
        at_k = slice(head * HEAD_DIM, (head + 1) * HEAD_DIM)
        at_v = slice((count + head) * HEAD_DIM, (count + head + 1) * HEAD_DIM)
        at_q = [slice((head * GROUPS + g) * HEAD_DIM, (head * GROUPS + g + 1) * HEAD_DIM) for g in range(GROUPS)]
        from_q = [slice(at.start + first * GROUPS * HEAD_DIM, at.stop + first * GROUPS * HEAD_DIM) for at in at_q]
        band_v = band_of(count + head)
        k_normed, _ = normalize(band_of(head).astype(F32))
        k_rounded = (k_normed * gain_k).astype(BF16)
        q_normed, q_inverse = normalize(jnp.concatenate([queries[0, :, at] for at in from_q], 0).astype(F32))
        q_scaled = (q_normed * gain_q * HEAD_DIM ** (-0.5)).astype(BF16)
        grads = jnp.concatenate([out_grad[0, :, at] for at in from_q], 0)

        scores = dot(q_scaled, k_rounded, (1, 1))
        weights = jnp.where(live, jnp.exp(scores), 0.0)
        probs = weights * (1.0 / jnp.sum(weights, -1, keepdims=True))
        probs_low = probs.astype(BF16)
        dprob = dot(grads, band_v, (1, 1))
        centre = jnp.sum(probs * dprob, -1, keepdims=True)
        dscore = (probs * (dprob - centre)).astype(BF16)
        key_parts = dot(dscore, q_scaled, (0, 0))
        value_parts = dot(probs_low, grads, (0, 0))
        for at, parts, third in ((at_k, key_parts, third_k), (at_v, value_parts, third_v)):
            part_far[:, at] = parts[:rows]
            third[:, at_k] = parts[rows : 2 * rows].astype(BF16)
            part_near[:, at] = parts[2 * rows : 3 * rows]
            part_next[:, at] = parts[3 * rows : 4 * rows].astype(BF16)
            part_own[:, at] = parts[4 * rows :]

        output = dot(probs_low, band_v, (1, 0)).astype(BF16)
        dq = dot(dscore, k_rounded, (1, 0)) * HEAD_DIM ** (-0.5)
        scaled = dq * gain_q
        grad = q_inverse * (scaled - q_normed * jnp.mean(scaled * q_normed, -1, keepdims=True))
        grad = grad.astype(BF16)
        for g, at in enumerate(at_q):
            attended[:, at] = output[g * rows : (g + 1) * rows]
            query_grad[:, at] = grad[g * rows : (g + 1) * rows]
        query_gains = query_gains + jnp.sum(dq * q_normed, 0, keepdims=True)
        key_gains = key_gains + jnp.sum(key_parts * k_normed, 0, keepdims=True)
    gains[0:1, :] = query_gains
    gains[1:2, :] = key_gains


def assemble(*refs):
    amount = len(CHUNKS)
    for index, out in enumerate(refs[-2:]):
        for (first, count), part in zip(CHUNKS, refs[index * amount : (index + 1) * amount]):
            out[0, :, first * GROUPS * HEAD_DIM : (first + count) * GROUPS * HEAD_DIM] = part[...]


def add(*refs):
    refs[-1][...] = sum(ref[...] for ref in refs[1:-1]) + refs[0][...]


def scale(factor, total, query_gains, key_gains):
    query_gains[...] = total[0:1, :] * factor
    key_gains[...] = total[1:2, :] * factor


def finish(count, at, keys, key_gain, part_own, swapped, arrived, *rest):
    key_grad, value_grad = rest[-2:]
    rows = part_own.shape[0]
    gain_k = key_gain[...]
    for head in range(count):

        def total(index):
            here = slice(index * HEAD_DIM, (index + 1) * HEAD_DIM)
            there = slice(at + index * HEAD_DIM, at + (index + 1) * HEAD_DIM)
            extra = jnp.where(core_index() == 0, swapped[:, here].astype(F32), 0.0)
            return part_own[:, here] + extra + arrived[:, there].astype(F32)

        out = slice(head * HEAD_DIM, (head + 1) * HEAD_DIM)
        normed, inverse = normalize(keys[0, :, out].astype(F32))
        scaled = total(head) * gain_k
        grad = inverse * (scaled - normed * jnp.mean(scaled * normed, -1, keepdims=True))
        key_grad[0, :, out] = grad.astype(BF16)
        value_grad[0, :, out] = total(count + head).astype(BF16)


def columns(rows, width, first):
    return pl.BlockSpec((1, rows, width), lambda i: (0, 0, first // width))


def move(field, axis, target):
    size = lax.axis_size(axis)
    return lax.ppermute(field, axis, [(i, target(i)) for i in range(size) if 0 <= target(i) < size])


def up(field):
    return move(field, "ctx", lambda i: i + 2)


def down(field):
    return move(field, "ctx", lambda i: i - 2)


def swap(field):
    return move(field, "ctx", lambda i: i ^ 1)


def total_over(field, axis, unit, most, after=()):
    while unit < lax.axis_size(axis):
        group = min(most, lax.axis_size(axis) // unit)
        others = [move(field, axis, lambda i: i ^ (by * unit)) for by in range(1, group)]
        (field,) = call(add, "add", dict(enumerate([field, *others])), dict(o=shape(*field.shape, F32)), after)
        unit *= group
    return field


def shards(segment_ids, queries, keys, values, query_gain, key_gain, out_grad):
    rows = queries.shape[1]
    gain_q = query_gain.reshape(1, HEAD_DIM)
    gain_k = key_gain.reshape(1, HEAD_DIM)
    amount = len(CHUNKS)
    width = [2 * count * HEAD_DIM for _, count in CHUNKS] + [0] * LAG
    def gather(chunks, small=(), after=()):
        sources = [pltpu.with_memory_space_constraint(field, pltpu.HBM) for field in (keys, values, *small)]
        made = call(
            functools.partial(payload, chunks),
            "payload",
            dict(enumerate(sources)),
            dict(
                enumerate(
                    [shape(rows, 2 * count * HEAD_DIM) for _, count in chunks]
                    + [jax.ShapeDtypeStruct(field.shape, field.dtype) for field in small]
                )
            ),
            after,
            in_specs=dict.fromkeys(range(len(sources)), ANY),
            scratch_shapes=[pltpu.SemaphoreType.DMA((2 * len(chunks) * PIECES + len(small),))],
        )
        return made[: len(chunks)], made[len(chunks) :]

    own, _ = gather(CHUNKS[:1])
    near = {0: (up(own[0]), 0)}
    more, (segments, gain_q, gain_k) = gather(CHUNKS[1:], (segment_ids, gain_q, gain_k), own)
    own = [(field, 0) for field in (*own, *more)]
    for chunk in range(1, LAG):
        near[chunk] = (up(own[chunk][0]), 0)
    far, next_behind, third_behind = {}, {}, {}

    def climb(steps, after=()):
        ins, outs, jobs = {}, {}, []

        def use(place, chunk):
            field, at = place
            key = next((key for key, value in ins.items() if value is field), f"in{len(ins)}")
            ins[key] = field
            return key, slice(at, at + width[chunk])

        def exchange(to, chunk, first, second, halves=1):
            part = width[chunk] // halves
            for half in range(halves):
                pick = [(key, slice(at.start + half * part, at.start + (half + 1) * part)) for key, at in (use(first[chunk], chunk), use(second[chunk], chunk))]
                jobs.append((f"{to}{half}", 0, *pick))
                outs[f"{to}{half}"] = shape(rows, part)

        for step in steps:
            rise = 0
            if step + LAG < amount:
                jobs.append((f"rise{step}", rise, use(own[step + LAG], step + LAG), None))
                rise += width[step + LAG]
            if step < amount:
                jobs.append((f"rise{step}", rise, use(near[step], step), None))
                outs[f"rise{step}"] = shape(rows, rise + width[step])
                exchange("next", step, own, near)
            if step >= LAG:
                exchange("third", step - LAG, near, far, 2)

        def body(*refs):
            ref = dict(zip(list(ins) + list(outs), refs))
            for to, at, (key, here), other in jobs:
                value = ref[key][:, here]
                if other is not None:
                    value = jnp.where(core_index() == 0, value, ref[other[0]][:, other[1]])
                ref[to][:, at : at + value.shape[1]] = value

        made = dict(zip(outs, call(body, "climb", ins, outs, after, cost=10**9 * steps[0])))
        for step in steps:
            if step < amount:
                arrived = up(made[f"rise{step}"])
                ahead = 0
                if step + LAG < amount:
                    near[step + LAG] = (arrived, 0)
                    ahead = width[step + LAG]
                far[step] = (arrived, ahead)
                next_behind[step] = (swap(made["next0"]), 0)
            if step >= LAG:
                third_behind[step - LAG] = [swap(made["third0"]), swap(made["third1"])]
        return [next(iter(made.values()))]

    parts, sunk = [], {}

    def sink(step, after=()):
        fresh, older = step < amount, step >= LAG
        mine, below = width[step], width[step - LAG] if older else 0
        ins = {}
        if fresh:
            ins.update(far=parts[step]["far"], third_k=parts[step]["third_k"], third_v=parts[step]["third_v"])
        if older:
            chunk = step - LAG
            ins.update(near=parts[chunk]["near"], arrived=sunk[chunk])
            ins.update(old_k=parts[chunk]["third_k"], old_v=parts[chunk]["third_v"], next_old=parts[chunk]["next"])

        def body(*refs):
            ref = dict(zip(list(ins) + ["out"], refs))
            first = core_index() == 0
            if fresh:
                for half, extra in ((slice(0, mine // 2), ref["third_k"]), (slice(mine // 2, mine), ref["third_v"])):
                    extra = jnp.where(first, 0.0, extra[...].astype(F32))
                    ref["out"][:, half] = (ref["far"][:, half] + extra).astype(BF16)
            if older:
                for half, extra in ((slice(0, below // 2), ref["old_k"]), (slice(below // 2, below), ref["old_v"])):
                    extra = jnp.where(first, extra[...], ref["next_old"][:, half]).astype(F32)
                    total = ref["near"][:, half] + extra + ref["arrived"][:, half].astype(F32)
                    ref["out"][:, mine + half.start : mine + half.stop] = total.astype(BF16)

        (total,) = call(body, "sink", ins, dict(out=shape(rows, mine + below)), after)
        sunk[step] = down(total)
        return total

    made, gains, last, token = [], [], [], []
    order = []
    for step in range(LAG):
        order = climb([step], order)
    for chunk, (first, count) in enumerate(CHUNKS):
        order = climb([chunk + LAG], order + token)
        held = (own, next_behind, near, far)
        wide = shape(rows, GROUPS * count * HEAD_DIM)
        whole, low, half = shape(rows, width[chunk], F32), shape(rows, width[chunk]), shape(rows, width[chunk] // 2)
        result = call(
            functools.partial(attend, first, count, *(place[chunk][1] for place in held)),
            "attend",
            dict(
                segments=segments, queries=queries, out_grad=out_grad, own=own[chunk][0],
                **{f"behind{i}": place[chunk][0] for i, place in enumerate(held[1:])},
                third_k=third_behind[chunk][0], third_v=third_behind[chunk][1], gain_q=gain_q, gain_k=gain_k,
            ),
            dict(
                attended=wide, query_grad=wide, own=whole, near=whole, far=whole,
                third_k=half, third_v=half, next=low,
                gains=shape(2, HEAD_DIM, F32),
            ),
            last,
        )
        made.append(result[:2])
        gains.append(result[8])
        token = [result[8]]
        parts.append(dict(zip(("own", "near", "far"), result[2:5])))
        parts[-1].update(third_k=swap(result[5]), third_v=swap(result[6]), next=swap(result[7]))
        last = [sink(chunk, last)]

    for step in range(amount, amount + LAG):
        order_gains = last
        last = [sink(step, last)]
    key_outputs = []
    for chunk, (first, count) in enumerate(CHUNKS):
        narrow = columns(rows, count * HEAD_DIM, first * HEAD_DIM)
        key_outputs = call(
            functools.partial(finish, count, width[chunk + LAG]),
            "finish",
            dict(
                keys=keys, gain=gain_k, own=parts[chunk]["own"], next=parts[chunk]["next"], arrived=sunk[chunk + LAG]
            ),
            dict(
                key_grad=jax.ShapeDtypeStruct(keys.shape, BF16), value_grad=jax.ShapeDtypeStruct(keys.shape, BF16)
            ),
            key_outputs,
            cost=2**31 * (1 + chunk),
            grid=(1,),
            in_specs=dict(keys=narrow),
            out_specs=dict(key_grad=narrow, value_grad=narrow),
            input_output_aliases={5 + i: i for i in range(len(key_outputs))},
        )
    attended, query_grad = call(
        assemble,
        "assemble",
        {(i, chunk): made[chunk][i] for i in range(2) for chunk in range(amount)},
        dict(a=jax.ShapeDtypeStruct(queries.shape, BF16), b=jax.ShapeDtypeStruct(queries.shape, BF16)),
        last,
    )

    (total,) = call(add, "add", dict(enumerate(gains)), dict(o=shape(2, HEAD_DIM, F32)))
    (total,) = call(add, "add", dict(a=total, b=swap(total)), dict(o=shape(2, HEAD_DIM, F32)), order_gains)
    total = total_over(total, "dp", 1, 2, last)
    total = total_over(total, "ctx", 2, 4)
    factor = (lax.axis_size("dp") * queries.shape[0] * lax.axis_size("ctx") * rows) ** (-0.5)
    row = shape(1, HEAD_DIM, F32)
    query_gains, key_gains = call(functools.partial(scale, factor), "scale", dict(t=total), dict(a=row, b=row))
    return attended, query_grad, *key_outputs, query_gains[0], key_gains[0]


def solution(mesh):
    block = P("dp", "ctx", None)
    return jax.shard_map(
        shards,
        mesh=mesh,
        in_specs=(P("dp", None), block, block, block, P(), P(), block),
        out_specs=(block, block, block, block, P(), P()),
        check_vma=False,
    )
```

```python
import functools

import jax
import jax.numpy as jnp
from jax import lax
from jax.experimental import pallas as pl
from jax.experimental.pallas import tpu as pltpu
from jax.sharding import PartitionSpec as P

HEADS = 8
KV_HEADS = 4
HEAD_DIM = 256
WINDOW = 512
GREACH = 4
GROUPS = HEADS // KV_HEADS
EPSILON = 1e-06
BF16 = jnp.bfloat16
F32 = jnp.float32
CHUNKS = ((0, 2), (2, 2))
LAG = 2

PIECES = 4

VMEM = pl.BlockSpec(memory_space=pltpu.VMEM)
ANY = pl.BlockSpec(memory_space=pl.ANY)


def call(body, name, ins, outs, after=(), cost=0, in_specs=None, out_specs=None, **more):
    names = list(ins)

    def kernel(*refs):
        used = len(names) + len(after)
        body(*refs[: len(names)], *refs[used:])

    specs = [(in_specs or {}).get(key, VMEM) for key in names] + [ANY] * len(after)
    return pl.pallas_call(
        kernel,
        out_shape=list(outs.values()),
        in_specs=specs,
        out_specs=[(out_specs or {}).get(key, VMEM) for key in outs],
        compiler_params=pltpu.CompilerParams(vmem_limit_bytes=40 * 2**20),
        cost_estimate=pl.CostEstimate(flops=cost, bytes_accessed=1, transcendentals=0),
        name=name,
        **more,
    )(*ins.values(), *after)


def shape(rows, cols, dtype=BF16):
    return jax.ShapeDtypeStruct((rows, cols), dtype)


def core_index():
    return lax.axis_index("ctx") % 2


def payload(chunks, keys, values, *rest):
    extra = len(rest[:-1]) - len(chunks)
    small, outs, kept, sems = rest[: extra // 2], rest[extra // 2 : -1 - extra // 2], rest[-1 - extra // 2 : -1], rest[-1]
    copies = [pltpu.make_async_copy(old, new, sems.at[i]) for i, (old, new) in enumerate(zip(small, kept))]
    for (first, count), out in zip(chunks, outs):
        here = pl.ds(first * HEAD_DIM, count * HEAD_DIM)
        for side, field in enumerate((keys, values)):
            to = pl.ds(side * count * HEAD_DIM, count * HEAD_DIM)
            for piece in range(PIECES):
                share = field.shape[1] // PIECES
                rows = pl.ds(piece * share, share)
                sem = sems.at[len(copies)]
                copies.append(pltpu.make_async_copy(field.at[0, rows, here], out.at[rows, to], sem))
    for copy in copies:
        copy.start()
    for copy in copies:
        copy.wait()


def normalize(field):
    inverse = lax.rsqrt(jnp.mean(field * field, -1, keepdims=True) + EPSILON)
    return field * inverse, inverse


def dot(left, right, over):
    return lax.dot_general(left, right, ((over[:1], over[1:]), ((), ())), preferred_element_type=F32)


def attend(
    first, count, at_own, at_x, at_near, at_far, segments, queries, out_grad, own, across_x, arrived_near, arrived_far,
    across_k, across_v,    query_gain, key_gain, *rest,
):
    attended, query_grad, part_own, part_near, part_far, third_k, third_v, part_next, gains = rest
    position = lax.axis_index("ctx")
    rows = queries.shape[1]
    band = (GREACH + 1) * rows
    gain_q = query_gain[...]
    gain_k = key_gain[...]

    def segment(distance):
        block = position - distance
        first = pl.multiple_of(jnp.maximum(block, 0) * rows, rows)
        return jnp.where(block >= 0, segments[:, pl.ds(first, rows)], -1)

    key_seg = jnp.concatenate([segment(distance) for distance in range(GREACH, -1, -1)], 1)
    query_seg = jnp.broadcast_to(segment(0), (rows, rows)).T[:, :1]
    back = (
        lax.broadcasted_iota(jnp.int32, (rows, band), 0)
        - lax.broadcasted_iota(jnp.int32, (rows, band), 1)
        + GREACH * rows
    )
    live = (query_seg == key_seg) & (back >= 0) & (back < WINDOW)
    live = jnp.concatenate([live] * GROUPS, 0)

    query_gains = jnp.zeros((1, HEAD_DIM), F32)
    key_gains = jnp.zeros((1, HEAD_DIM), F32)

    def band_of(index):
        third = (across_k, 0) if index < count else (across_v, -count * HEAD_DIM)
        blocks = ((arrived_far, at_far), third, (arrived_near, at_near), (across_x, at_x), (own, at_own))
        return jnp.concatenate(
            [field[:, at + index * HEAD_DIM : at + (index + 1) * HEAD_DIM] for field, at in blocks], 0
        )

    for head in range(count):
        at_k = slice(head * HEAD_DIM, (head + 1) * HEAD_DIM)
        at_v = slice((count + head) * HEAD_DIM, (count + head + 1) * HEAD_DIM)
        at_q = [slice((head * GROUPS + g) * HEAD_DIM, (head * GROUPS + g + 1) * HEAD_DIM) for g in range(GROUPS)]
        from_q = [slice(at.start + first * GROUPS * HEAD_DIM, at.stop + first * GROUPS * HEAD_DIM) for at in at_q]
        band_v = band_of(count + head)
        k_normed, _ = normalize(band_of(head).astype(F32))
        k_rounded = (k_normed * gain_k).astype(BF16)
        q_normed, q_inverse = normalize(jnp.concatenate([queries[0, :, at] for at in from_q], 0).astype(F32))
        q_scaled = (q_normed * gain_q * HEAD_DIM ** (-0.5)).astype(BF16)
        grads = jnp.concatenate([out_grad[0, :, at] for at in from_q], 0)

        scores = dot(q_scaled, k_rounded, (1, 1))
        weights = jnp.where(live, jnp.exp(scores), 0.0)
        probs = weights * (1.0 / jnp.sum(weights, -1, keepdims=True))
        probs_low = probs.astype(BF16)
        dprob = dot(grads, band_v, (1, 1))
        centre = jnp.sum(probs * dprob, -1, keepdims=True)
        dscore = (probs * (dprob - centre)).astype(BF16)
        key_parts = dot(dscore, q_scaled, (0, 0))
        value_parts = dot(probs_low, grads, (0, 0))
        for at, parts, third in ((at_k, key_parts, third_k), (at_v, value_parts, third_v)):
            part_far[:, at] = parts[:rows]
            third[:, at_k] = parts[rows : 2 * rows].astype(BF16)
            part_near[:, at] = parts[2 * rows : 3 * rows]
            part_next[:, at] = parts[3 * rows : 4 * rows].astype(BF16)
            part_own[:, at] = parts[4 * rows :]

        output = dot(probs_low, band_v, (1, 0)).astype(BF16)
        dq = dot(dscore, k_rounded, (1, 0)) * HEAD_DIM ** (-0.5)
        scaled = dq * gain_q
        grad = q_inverse * (scaled - q_normed * jnp.mean(scaled * q_normed, -1, keepdims=True))
        grad = grad.astype(BF16)
        for g, at in enumerate(at_q):
            attended[:, at] = output[g * rows : (g + 1) * rows]
            query_grad[:, at] = grad[g * rows : (g + 1) * rows]
        query_gains = query_gains + jnp.sum(dq * q_normed, 0, keepdims=True)
        key_gains = key_gains + jnp.sum(key_parts * k_normed, 0, keepdims=True)
    gains[0:1, :] = query_gains
    gains[1:2, :] = key_gains


def assemble(*refs):
    amount = len(CHUNKS)
    for index, out in enumerate(refs[-2:]):
        for (first, count), part in zip(CHUNKS, refs[index * amount : (index + 1) * amount]):
            out[0, :, first * GROUPS * HEAD_DIM : (first + count) * GROUPS * HEAD_DIM] = part[...]


def add(*refs):
    refs[-1][...] = sum(ref[...] for ref in refs[1:-1]) + refs[0][...]


def scale(factor, total, query_gains, key_gains):
    query_gains[...] = total[0:1, :] * factor
    key_gains[...] = total[1:2, :] * factor


def finish(count, at, keys, key_gain, part_own, swapped, arrived, *rest):
    key_grad, value_grad = rest[-2:]
    rows = part_own.shape[0]
    gain_k = key_gain[...]
    for head in range(count):

        def total(index):
            here = slice(index * HEAD_DIM, (index + 1) * HEAD_DIM)
            there = slice(at + index * HEAD_DIM, at + (index + 1) * HEAD_DIM)
            extra = jnp.where(core_index() == 0, swapped[:, here].astype(F32), 0.0)
            return part_own[:, here] + extra + arrived[:, there].astype(F32)

        out = slice(head * HEAD_DIM, (head + 1) * HEAD_DIM)
        normed, inverse = normalize(keys[0, :, out].astype(F32))
        scaled = total(head) * gain_k
        grad = inverse * (scaled - normed * jnp.mean(scaled * normed, -1, keepdims=True))
        key_grad[0, :, out] = grad.astype(BF16)
        value_grad[0, :, out] = total(count + head).astype(BF16)


def columns(rows, width, first):
    return pl.BlockSpec((1, rows, width), lambda i: (0, 0, first // width))


def move(field, axis, target):
    size = lax.axis_size(axis)
    return lax.ppermute(field, axis, [(i, target(i)) for i in range(size) if 0 <= target(i) < size])


def up(field):
    return move(field, "ctx", lambda i: i + 2)


def down(field):
    return move(field, "ctx", lambda i: i - 2)


def swap(field):
    return move(field, "ctx", lambda i: i ^ 1)


def total_over(field, axis, unit, end, most, after=()):
    end = min(end, lax.axis_size(axis))
    while unit < end:
        group = min(most, end // unit)
        others = [move(field, axis, lambda i: i ^ (by * unit)) for by in range(1, group)]
        (field,) = call(add, "add", dict(enumerate([field, *others])), dict(o=shape(*field.shape, F32)), after)
        unit *= group
    return field


def shards(segment_ids, queries, keys, values, query_gain, key_gain, out_grad):
    rows = queries.shape[1]
    gain_q = query_gain.reshape(1, HEAD_DIM)
    gain_k = key_gain.reshape(1, HEAD_DIM)
    amount = len(CHUNKS)
    width = [2 * count * HEAD_DIM for _, count in CHUNKS] + [0] * LAG
    def gather(chunks, small=(), after=()):
        sources = [pltpu.with_memory_space_constraint(field, pltpu.HBM) for field in (keys, values, *small)]
        made = call(
            functools.partial(payload, chunks),
            "payload",
            dict(enumerate(sources)),
            dict(
                enumerate(
                    [shape(rows, 2 * count * HEAD_DIM) for _, count in chunks]
                    + [jax.ShapeDtypeStruct(field.shape, field.dtype) for field in small]
                )
            ),
            after,
            in_specs=dict.fromkeys(range(len(sources)), ANY),
            scratch_shapes=[pltpu.SemaphoreType.DMA((2 * len(chunks) * PIECES + len(small),))],
        )
        return made[: len(chunks)], made[len(chunks) :]

    own, _ = gather(CHUNKS[:1])
    near = {0: (up(own[0]), 0)}
    more, (segments, gain_q, gain_k) = gather(CHUNKS[1:], (segment_ids, gain_q, gain_k), own)
    own = [(field, 0) for field in (*own, *more)]
    for chunk in range(1, LAG):
        near[chunk] = (up(own[chunk][0]), 0)
    far, next_behind, third_behind = {}, {}, {}

    def climb(steps, after=()):
        ins, outs, jobs = {}, {}, []

        def use(place, chunk):
            field, at = place
            key = next((key for key, value in ins.items() if value is field), f"in{len(ins)}")
            ins[key] = field
            return key, slice(at, at + width[chunk])

        def exchange(to, chunk, first, second, halves=1):
            part = width[chunk] // halves
            for half in range(halves):
                pick = [(key, slice(at.start + half * part, at.start + (half + 1) * part)) for key, at in (use(first[chunk], chunk), use(second[chunk], chunk))]
                jobs.append((f"{to}{half}", 0, *pick))
                outs[f"{to}{half}"] = shape(rows, part)

        for step in steps:
            rise = 0
            if step + LAG < amount:
                jobs.append((f"rise{step}", rise, use(own[step + LAG], step + LAG), None))
                rise += width[step + LAG]
            if step < amount:
                jobs.append((f"rise{step}", rise, use(near[step], step), None))
                outs[f"rise{step}"] = shape(rows, rise + width[step])
                exchange("next", step, own, near)
            if step >= LAG:
                exchange("third", step - LAG, near, far, 2)

        def body(*refs):
            ref = dict(zip(list(ins) + list(outs), refs))
            for to, at, (key, here), other in jobs:
                value = ref[key][:, here]
                if other is not None:
                    value = jnp.where(core_index() == 0, value, ref[other[0]][:, other[1]])
                ref[to][:, at : at + value.shape[1]] = value

        made = dict(zip(outs, call(body, "climb", ins, outs, after, cost=10**9 * steps[0])))
        for step in steps:
            if step < amount:
                arrived = up(made[f"rise{step}"])
                ahead = 0
                if step + LAG < amount:
                    near[step + LAG] = (arrived, 0)
                    ahead = width[step + LAG]
                far[step] = (arrived, ahead)
                next_behind[step] = (swap(made["next0"]), 0)
            if step >= LAG:
                third_behind[step - LAG] = [swap(made["third0"]), swap(made["third1"])]
        return [next(iter(made.values()))]

    parts, sunk = [], {}

    def sink(step, after=()):
        fresh, older = step < amount, step >= LAG
        mine, below = width[step], width[step - LAG] if older else 0
        ins = {}
        if fresh:
            ins.update(far=parts[step]["far"], third_k=parts[step]["third_k"], third_v=parts[step]["third_v"])
        if older:
            chunk = step - LAG
            ins.update(near=parts[chunk]["near"], arrived=sunk[chunk])
            ins.update(old_k=parts[chunk]["third_k"], old_v=parts[chunk]["third_v"], next_old=parts[chunk]["next"])

        def body(*refs):
            ref = dict(zip(list(ins) + ["out"], refs))
            first = core_index() == 0
            if fresh:
                for half, extra in ((slice(0, mine // 2), ref["third_k"]), (slice(mine // 2, mine), ref["third_v"])):
                    extra = jnp.where(first, 0.0, extra[...].astype(F32))
                    ref["out"][:, half] = (ref["far"][:, half] + extra).astype(BF16)
            if older:
                for half, extra in ((slice(0, below // 2), ref["old_k"]), (slice(below // 2, below), ref["old_v"])):
                    extra = jnp.where(first, extra[...], ref["next_old"][:, half]).astype(F32)
                    total = ref["near"][:, half] + extra + ref["arrived"][:, half].astype(F32)
                    ref["out"][:, mine + half.start : mine + half.stop] = total.astype(BF16)

        (total,) = call(body, "sink", ins, dict(out=shape(rows, mine + below)), after)
        sunk[step] = down(total)
        return total

    made, gains, last, token = [], [], [], []
    order = []
    for step in range(LAG):
        order = climb([step], order)
    for chunk, (first, count) in enumerate(CHUNKS):
        order = climb([chunk + LAG], order + token)
        held = (own, next_behind, near, far)
        wide = shape(rows, GROUPS * count * HEAD_DIM)
        whole, low, half = shape(rows, width[chunk], F32), shape(rows, width[chunk]), shape(rows, width[chunk] // 2)
        result = call(
            functools.partial(attend, first, count, *(place[chunk][1] for place in held)),
            "attend",
            dict(
                segments=segments, queries=queries, out_grad=out_grad, own=own[chunk][0],
                **{f"behind{i}": place[chunk][0] for i, place in enumerate(held[1:])},
                third_k=third_behind[chunk][0], third_v=third_behind[chunk][1], gain_q=gain_q, gain_k=gain_k,
            ),
            dict(
                attended=wide, query_grad=wide, own=whole, near=whole, far=whole,
                third_k=half, third_v=half, next=low,
                gains=shape(2, HEAD_DIM, F32),
            ),
            last,
        )
        made.append(result[:2])
        gains.append(result[8])
        token = [result[8]]
        parts.append(dict(zip(("own", "near", "far"), result[2:5])))
        parts[-1].update(third_k=swap(result[5]), third_v=swap(result[6]), next=swap(result[7]))
        if chunk == amount - 1:
            (total,) = call(add, "add", dict(enumerate(gains)), dict(o=shape(2, HEAD_DIM, F32)))
            total = total_over(total, "ctx", 1, 2, 2)
            last = [*last, total]
        last = [sink(chunk, last)]

    total = total_over(total, "dp", 1, 2, 2)
    for step in range(amount, amount + LAG):
        last = [sink(step, [*last, total])]
    key_outputs = []
    for chunk, (first, count) in enumerate(CHUNKS):
        narrow = columns(rows, count * HEAD_DIM, first * HEAD_DIM)
        key_outputs = call(
            functools.partial(finish, count, width[chunk + LAG]),
            "finish",
            dict(
                keys=keys, gain=gain_k, own=parts[chunk]["own"], next=parts[chunk]["next"], arrived=sunk[chunk + LAG]
            ),
            dict(
                key_grad=jax.ShapeDtypeStruct(keys.shape, BF16), value_grad=jax.ShapeDtypeStruct(keys.shape, BF16)
            ),
            key_outputs,
            cost=2**31 * (1 + chunk),
            grid=(1,),
            in_specs=dict(keys=narrow),
            out_specs=dict(key_grad=narrow, value_grad=narrow),
            input_output_aliases={5 + i: i for i in range(len(key_outputs))},
        )
    attended, query_grad = call(
        assemble,
        "assemble",
        {(i, chunk): made[chunk][i] for i in range(2) for chunk in range(amount)},
        dict(a=jax.ShapeDtypeStruct(queries.shape, BF16), b=jax.ShapeDtypeStruct(queries.shape, BF16)),
        last,
    )

    total = total_over(total, "dp", 2, lax.axis_size("dp"), 2)
    total = total_over(total, "ctx", 2, lax.axis_size("ctx"), 4, last)
    factor = (lax.axis_size("dp") * queries.shape[0] * lax.axis_size("ctx") * rows) ** (-0.5)
    row = shape(1, HEAD_DIM, F32)
    query_gains, key_gains = call(functools.partial(scale, factor), "scale", dict(t=total), dict(a=row, b=row))
    return attended, query_grad, *key_outputs, query_gains[0], key_gains[0]


def solution(mesh):
    block = P("dp", "ctx", None)
    return jax.shard_map(
        shards,
        mesh=mesh,
        in_specs=(P("dp", None), block, block, block, P(), P(), block),
        out_specs=(block, block, block, block, P(), P()),
        check_vma=False,
    )
```

```python
import functools

import jax
import jax.numpy as jnp
from jax import lax
from jax.experimental import pallas as pl
from jax.experimental.pallas import tpu as pltpu
from jax.sharding import PartitionSpec as P

HEADS = 8
KV_HEADS = 4
HEAD_DIM = 256
WINDOW = 512
GREACH = 4
GROUPS = HEADS // KV_HEADS
EPSILON = 1e-06
BF16 = jnp.bfloat16
F32 = jnp.float32
CHUNKS = ((0, 2), (2, 2))
LAG = 2

PIECES = 4

VMEM = pl.BlockSpec(memory_space=pltpu.VMEM)
ANY = pl.BlockSpec(memory_space=pl.ANY)


def call(body, name, ins, outs, after=(), cost=0, in_specs=None, out_specs=None, **more):
    names = list(ins)

    def kernel(*refs):
        used = len(names) + len(after)
        body(*refs[: len(names)], *refs[used:])

    specs = [(in_specs or {}).get(key, VMEM) for key in names] + [ANY] * len(after)
    return pl.pallas_call(
        kernel,
        out_shape=list(outs.values()),
        in_specs=specs,
        out_specs=[(out_specs or {}).get(key, VMEM) for key in outs],
        compiler_params=pltpu.CompilerParams(vmem_limit_bytes=40 * 2**20),
        cost_estimate=pl.CostEstimate(flops=cost, bytes_accessed=1, transcendentals=0),
        name=name,
        **more,
    )(*ins.values(), *after)


def shape(rows, cols, dtype=BF16):
    return jax.ShapeDtypeStruct((rows, cols), dtype)


def core_index():
    return lax.axis_index("ctx") % 2


def payload(chunks, keys, values, *rest):
    extra = len(rest[:-1]) - len(chunks)
    small, outs, kept, sems = rest[: extra // 2], rest[extra // 2 : -1 - extra // 2], rest[-1 - extra // 2 : -1], rest[-1]
    copies = [pltpu.make_async_copy(old, new, sems.at[i]) for i, (old, new) in enumerate(zip(small, kept))]
    for (first, count), out in zip(chunks, outs):
        here = pl.ds(first * HEAD_DIM, count * HEAD_DIM)
        for side, field in enumerate((keys, values)):
            to = pl.ds(side * count * HEAD_DIM, count * HEAD_DIM)
            for piece in range(PIECES):
                share = field.shape[1] // PIECES
                rows = pl.ds(piece * share, share)
                sem = sems.at[len(copies)]
                copies.append(pltpu.make_async_copy(field.at[0, rows, here], out.at[rows, to], sem))
    for copy in copies:
        copy.start()
    for copy in copies:
        copy.wait()


def normalize(field):
    inverse = lax.rsqrt(jnp.mean(field * field, -1, keepdims=True) + EPSILON)
    return field * inverse, inverse


def dot(left, right, over):
    return lax.dot_general(left, right, ((over[:1], over[1:]), ((), ())), preferred_element_type=F32)


def attend(
    first, count, at_own, at_x, at_near, at_far, segments, queries, out_grad, own, across_x, arrived_near, arrived_far,
    across_k, across_v,    query_gain, key_gain, *rest,
):
    attended, query_grad, part_own, part_near, part_far, third_k, third_v, part_next, gains = rest
    position = lax.axis_index("ctx")
    rows = queries.shape[1]
    band = (GREACH + 1) * rows
    gain_q = query_gain[...]
    gain_k = key_gain[...]

    def segment(distance):
        block = position - distance
        first = pl.multiple_of(jnp.maximum(block, 0) * rows, rows)
        return jnp.where(block >= 0, segments[:, pl.ds(first, rows)], -1)

    key_seg = jnp.concatenate([segment(distance) for distance in range(GREACH, -1, -1)], 1)
    query_seg = jnp.broadcast_to(segment(0), (rows, rows)).T[:, :1]
    back = (
        lax.broadcasted_iota(jnp.int32, (rows, band), 0)
        - lax.broadcasted_iota(jnp.int32, (rows, band), 1)
        + GREACH * rows
    )
    live = (query_seg == key_seg) & (back >= 0) & (back < WINDOW)
    live = jnp.concatenate([live] * GROUPS, 0)

    query_gains = jnp.zeros((1, HEAD_DIM), F32)
    key_gains = jnp.zeros((1, HEAD_DIM), F32)

    def band_of(index):
        third = (across_k, 0) if index < count else (across_v, -count * HEAD_DIM)
        blocks = ((arrived_far, at_far), third, (arrived_near, at_near), (across_x, at_x), (own, at_own))
        return jnp.concatenate(
            [field[:, at + index * HEAD_DIM : at + (index + 1) * HEAD_DIM] for field, at in blocks], 0
        )

    for head in range(count):
        at_k = slice(head * HEAD_DIM, (head + 1) * HEAD_DIM)
        at_v = slice((count + head) * HEAD_DIM, (count + head + 1) * HEAD_DIM)
        at_q = [slice((head * GROUPS + g) * HEAD_DIM, (head * GROUPS + g + 1) * HEAD_DIM) for g in range(GROUPS)]
        from_q = [slice(at.start + first * GROUPS * HEAD_DIM, at.stop + first * GROUPS * HEAD_DIM) for at in at_q]
        band_v = band_of(count + head)
        k_normed, _ = normalize(band_of(head).astype(F32))
        k_rounded = (k_normed * gain_k).astype(BF16)
        q_normed, q_inverse = normalize(jnp.concatenate([queries[0, :, at] for at in from_q], 0).astype(F32))
        q_scaled = (q_normed * gain_q * HEAD_DIM ** (-0.5)).astype(BF16)
        grads = jnp.concatenate([out_grad[0, :, at] for at in from_q], 0)

        scores = dot(q_scaled, k_rounded, (1, 1))
        weights = jnp.where(live, jnp.exp(scores), 0.0)
        probs = weights * (1.0 / jnp.sum(weights, -1, keepdims=True))
        probs_low = probs.astype(BF16)
        dprob = dot(grads, band_v, (1, 1))
        centre = jnp.sum(probs * dprob, -1, keepdims=True)
        dscore = (probs * (dprob - centre)).astype(BF16)
        key_parts = dot(dscore, q_scaled, (0, 0))
        value_parts = dot(probs_low, grads, (0, 0))
        for at, parts, third in ((at_k, key_parts, third_k), (at_v, value_parts, third_v)):
            part_far[:, at] = parts[:rows]
            third[:, at_k] = parts[rows : 2 * rows].astype(BF16)
            part_near[:, at] = parts[2 * rows : 3 * rows]
            part_next[:, at] = parts[3 * rows : 4 * rows].astype(BF16)
            part_own[:, at] = parts[4 * rows :]

        output = dot(probs_low, band_v, (1, 0)).astype(BF16)
        dq = dot(dscore, k_rounded, (1, 0)) * HEAD_DIM ** (-0.5)
        scaled = dq * gain_q
        grad = q_inverse * (scaled - q_normed * jnp.mean(scaled * q_normed, -1, keepdims=True))
        grad = grad.astype(BF16)
        for g, at in enumerate(at_q):
            attended[:, at] = output[g * rows : (g + 1) * rows]
            query_grad[:, at] = grad[g * rows : (g + 1) * rows]
        query_gains = query_gains + jnp.sum(dq * q_normed, 0, keepdims=True)
        key_gains = key_gains + jnp.sum(key_parts * k_normed, 0, keepdims=True)
    gains[0:1, :] = query_gains
    gains[1:2, :] = key_gains


def assemble(*refs):
    amount = len(CHUNKS)
    for index, out in enumerate(refs[-2:]):
        for (first, count), part in zip(CHUNKS, refs[index * amount : (index + 1) * amount]):
            out[0, :, first * GROUPS * HEAD_DIM : (first + count) * GROUPS * HEAD_DIM] = part[...]


def add(*refs):
    refs[-1][...] = sum(ref[...] for ref in refs[1:-1]) + refs[0][...]


def scale(factor, *refs):
    total = sum(ref[...] for ref in refs[1:-2]) + refs[0][...]
    refs[-2][...] = total[0:1, :] * factor
    refs[-1][...] = total[1:2, :] * factor


def finish(count, at, keys, key_gain, part_own, swapped, arrived, *rest):
    key_grad, value_grad = rest[-2:]
    rows = part_own.shape[0]
    gain_k = key_gain[...]
    for head in range(count):

        def total(index):
            here = slice(index * HEAD_DIM, (index + 1) * HEAD_DIM)
            there = slice(at + index * HEAD_DIM, at + (index + 1) * HEAD_DIM)
            extra = jnp.where(core_index() == 0, swapped[:, here].astype(F32), 0.0)
            return part_own[:, here] + extra + arrived[:, there].astype(F32)

        out = slice(head * HEAD_DIM, (head + 1) * HEAD_DIM)
        normed, inverse = normalize(keys[0, :, out].astype(F32))
        scaled = total(head) * gain_k
        grad = inverse * (scaled - normed * jnp.mean(scaled * normed, -1, keepdims=True))
        key_grad[0, :, out] = grad.astype(BF16)
        value_grad[0, :, out] = total(count + head).astype(BF16)


def columns(rows, width, first):
    return pl.BlockSpec((1, rows, width), lambda i: (0, 0, first // width))


def move(field, axis, target):
    size = lax.axis_size(axis)
    return lax.ppermute(field, axis, [(i, target(i)) for i in range(size) if 0 <= target(i) < size])


def up(field):
    return move(field, "ctx", lambda i: i + 2)


def down(field):
    return move(field, "ctx", lambda i: i - 2)


def swap(field):
    return move(field, "ctx", lambda i: i ^ 1)


def total_over(field, axis, unit, end, most, after=()):
    end = min(end, lax.axis_size(axis))
    while unit < end:
        group = min(most, end // unit)
        others = [move(field, axis, lambda i: i ^ (by * unit)) for by in range(1, group)]
        (field,) = call(add, "add", dict(enumerate([field, *others])), dict(o=shape(*field.shape, F32)), after)
        unit *= group
    return field


def shards(segment_ids, queries, keys, values, query_gain, key_gain, out_grad):
    rows = queries.shape[1]
    gain_q = query_gain.reshape(1, HEAD_DIM)
    gain_k = key_gain.reshape(1, HEAD_DIM)
    amount = len(CHUNKS)
    width = [2 * count * HEAD_DIM for _, count in CHUNKS] + [0] * LAG
    def gather(chunks, small=(), after=()):
        sources = [pltpu.with_memory_space_constraint(field, pltpu.HBM) for field in (keys, values, *small)]
        made = call(
            functools.partial(payload, chunks),
            "payload",
            dict(enumerate(sources)),
            dict(
                enumerate(
                    [shape(rows, 2 * count * HEAD_DIM) for _, count in chunks]
                    + [jax.ShapeDtypeStruct(field.shape, field.dtype) for field in small]
                )
            ),
            after,
            in_specs=dict.fromkeys(range(len(sources)), ANY),
            scratch_shapes=[pltpu.SemaphoreType.DMA((2 * len(chunks) * PIECES + len(small),))],
        )
        return made[: len(chunks)], made[len(chunks) :]

    own, _ = gather(CHUNKS[:1])
    near = {0: (up(own[0]), 0)}
    more, (segments, gain_q, gain_k) = gather(CHUNKS[1:], (segment_ids, gain_q, gain_k), own)
    own = [(field, 0) for field in (*own, *more)]
    for chunk in range(1, LAG):
        near[chunk] = (up(own[chunk][0]), 0)
    far, next_behind, third_behind = {}, {}, {}

    def climb(steps, after=()):
        ins, outs, jobs = {}, {}, []

        def use(place, chunk):
            field, at = place
            key = next((key for key, value in ins.items() if value is field), f"in{len(ins)}")
            ins[key] = field
            return key, slice(at, at + width[chunk])

        def exchange(to, chunk, first, second, halves=1):
            part = width[chunk] // halves
            for half in range(halves):
                pick = [(key, slice(at.start + half * part, at.start + (half + 1) * part)) for key, at in (use(first[chunk], chunk), use(second[chunk], chunk))]
                jobs.append((f"{to}{half}", 0, *pick))
                outs[f"{to}{half}"] = shape(rows, part)

        for step in steps:
            rise = 0
            if step + LAG < amount:
                jobs.append((f"rise{step}", rise, use(own[step + LAG], step + LAG), None))
                rise += width[step + LAG]
            if step < amount:
                jobs.append((f"rise{step}", rise, use(near[step], step), None))
                outs[f"rise{step}"] = shape(rows, rise + width[step])
                exchange("next", step, own, near)
            if step >= LAG:
                exchange("third", step - LAG, near, far, 2)

        def body(*refs):
            ref = dict(zip(list(ins) + list(outs), refs))
            for to, at, (key, here), other in jobs:
                value = ref[key][:, here]
                if other is not None:
                    value = jnp.where(core_index() == 0, value, ref[other[0]][:, other[1]])
                ref[to][:, at : at + value.shape[1]] = value

        made = dict(zip(outs, call(body, "climb", ins, outs, after, cost=10**9 * steps[0])))
        for step in steps:
            if step < amount:
                arrived = up(made[f"rise{step}"])
                ahead = 0
                if step + LAG < amount:
                    near[step + LAG] = (arrived, 0)
                    ahead = width[step + LAG]
                far[step] = (arrived, ahead)
                next_behind[step] = (swap(made["next0"]), 0)
            if step >= LAG:
                third_behind[step - LAG] = [swap(made["third0"]), swap(made["third1"])]
        return [next(iter(made.values()))]

    parts, sunk = [], {}

    def sink(step, after=()):
        fresh, older = step < amount, step >= LAG
        mine, below = width[step], width[step - LAG] if older else 0
        ins = {}
        if fresh:
            ins.update(far=parts[step]["far"], third_k=parts[step]["third_k"], third_v=parts[step]["third_v"])
        if older:
            chunk = step - LAG
            ins.update(near=parts[chunk]["near"], arrived=sunk[chunk])
            ins.update(old_k=parts[chunk]["third_k"], old_v=parts[chunk]["third_v"], next_old=parts[chunk]["next"])

        def body(*refs):
            ref = dict(zip(list(ins) + ["out"], refs))
            first = core_index() == 0
            if fresh:
                for half, extra in ((slice(0, mine // 2), ref["third_k"]), (slice(mine // 2, mine), ref["third_v"])):
                    extra = jnp.where(first, 0.0, extra[...].astype(F32))
                    ref["out"][:, half] = (ref["far"][:, half] + extra).astype(BF16)
            if older:
                for half, extra in ((slice(0, below // 2), ref["old_k"]), (slice(below // 2, below), ref["old_v"])):
                    extra = jnp.where(first, extra[...], ref["next_old"][:, half]).astype(F32)
                    total = ref["near"][:, half] + extra + ref["arrived"][:, half].astype(F32)
                    ref["out"][:, mine + half.start : mine + half.stop] = total.astype(BF16)

        (total,) = call(body, "sink", ins, dict(out=shape(rows, mine + below)), after)
        sunk[step] = down(total)
        return total

    made, gains, last, token = [], [], [], []
    order = []
    for step in range(LAG):
        order = climb([step], order)
    for chunk, (first, count) in enumerate(CHUNKS):
        order = climb([chunk + LAG], order + token)
        held = (own, next_behind, near, far)
        wide = shape(rows, GROUPS * count * HEAD_DIM)
        whole, low, half = shape(rows, width[chunk], F32), shape(rows, width[chunk]), shape(rows, width[chunk] // 2)
        result = call(
            functools.partial(attend, first, count, *(place[chunk][1] for place in held)),
            "attend",
            dict(
                segments=segments, queries=queries, out_grad=out_grad, own=own[chunk][0],
                **{f"behind{i}": place[chunk][0] for i, place in enumerate(held[1:])},
                third_k=third_behind[chunk][0], third_v=third_behind[chunk][1], gain_q=gain_q, gain_k=gain_k,
            ),
            dict(
                attended=wide, query_grad=wide, own=whole, near=whole, far=whole,
                third_k=half, third_v=half, next=low,
                gains=shape(2, HEAD_DIM, F32),
            ),
            last,
        )
        made.append(result[:2])
        gains.append(result[8])
        token = [result[8]]
        parts.append(dict(zip(("own", "near", "far"), result[2:5])))
        parts[-1].update(third_k=swap(result[5]), third_v=swap(result[6]), next=swap(result[7]))
        if chunk == amount - 1:
            (total,) = call(add, "add", dict(enumerate(gains)), dict(o=shape(2, HEAD_DIM, F32)))
            total = total_over(total, "ctx", 1, 2, 2)
            last = [*last, total]
        last = [sink(chunk, last)]

    unit = 1
    for step in range(amount, amount + LAG):
        end = unit * 2 if step + 1 < amount + LAG else lax.axis_size("dp")
        total = total_over(total, "dp", unit, end, 2)
        unit = end
        last = [sink(step, [*last, total])]
    key_outputs = []
    for chunk, (first, count) in enumerate(CHUNKS):
        narrow = columns(rows, count * HEAD_DIM, first * HEAD_DIM)
        key_outputs = call(
            functools.partial(finish, count, width[chunk + LAG]),
            "finish",
            dict(
                keys=keys, gain=gain_k, own=parts[chunk]["own"], next=parts[chunk]["next"], arrived=sunk[chunk + LAG]
            ),
            dict(
                key_grad=jax.ShapeDtypeStruct(keys.shape, BF16), value_grad=jax.ShapeDtypeStruct(keys.shape, BF16)
            ),
            key_outputs,
            cost=2**31 * (1 + chunk),
            grid=(1,),
            in_specs=dict(keys=narrow),
            out_specs=dict(key_grad=narrow, value_grad=narrow),
            input_output_aliases={5 + i: i for i in range(len(key_outputs))},
        )
    attended, query_grad = call(
        assemble,
        "assemble",
        {(i, chunk): made[chunk][i] for i in range(2) for chunk in range(amount)},
        dict(a=jax.ShapeDtypeStruct(queries.shape, BF16), b=jax.ShapeDtypeStruct(queries.shape, BF16)),
        last,
    )

    factor = (lax.axis_size("dp") * queries.shape[0] * lax.axis_size("ctx") * rows) ** (-0.5)
    row = shape(1, HEAD_DIM, F32)
    chips = lax.axis_size("ctx") // 2
    while chips > 4:
        total = total_over(total, "ctx", chips, 2 * chips, 2)
        chips //= 2
    others = [move(total, "ctx", lambda i: i ^ (2 * by)) for by in range(1, chips)]
    query_gains, key_gains = call(
        functools.partial(scale, factor),
        "scale",
        dict(enumerate([total, *others])),
        dict(a=row, b=row),
        [pltpu.with_memory_space_constraint(field, pltpu.HBM) for field in (attended, *key_outputs)],
    )
    return attended, query_grad, *key_outputs, query_gains[0], key_gains[0]


def solution(mesh):
    block = P("dp", "ctx", None)
    return jax.shard_map(
        shards,
        mesh=mesh,
        in_specs=(P("dp", None), block, block, block, P(), P(), block),
        out_specs=(block, block, block, block, P(), P()),
        check_vma=False,
    )
```

```python
import functools

import jax
import jax.numpy as jnp
from jax import lax
from jax.experimental import pallas as pl
from jax.experimental.pallas import tpu as pltpu
from jax.sharding import PartitionSpec as P

HEADS = 8
KV_HEADS = 4
HEAD_DIM = 256
WINDOW = 512
GREACH = 4
GROUPS = HEADS // KV_HEADS
EPSILON = 1e-06
BF16 = jnp.bfloat16
F32 = jnp.float32
CHUNKS = ((0, 2), (2, 2))
LAG = 2

PIECES = 4

Z_COST, S_COST, F_COST, G_COST = 2**30, 0, 2**31, 2**32

VMEM = pl.BlockSpec(memory_space=pltpu.VMEM)
ANY = pl.BlockSpec(memory_space=pl.ANY)


def call(body, name, ins, outs, after=(), cost=0, in_specs=None, out_specs=None, **more):
    names = list(ins)

    def kernel(*refs):
        used = len(names) + len(after)
        body(*refs[: len(names)], *refs[used:])

    specs = [(in_specs or {}).get(key, VMEM) for key in names] + [ANY] * len(after)
    return pl.pallas_call(
        kernel,
        out_shape=list(outs.values()),
        in_specs=specs,
        out_specs=[(out_specs or {}).get(key, VMEM) for key in outs],
        compiler_params=pltpu.CompilerParams(vmem_limit_bytes=40 * 2**20),
        cost_estimate=pl.CostEstimate(flops=cost, bytes_accessed=1, transcendentals=0),
        name=name,
        **more,
    )(*ins.values(), *after)


def shape(rows, cols, dtype=BF16):
    return jax.ShapeDtypeStruct((rows, cols), dtype)


def core_index():
    return lax.axis_index("ctx") % 2


def payload(chunks, keys, values, *rest):
    extra = len(rest[:-1]) - len(chunks)
    small, outs, kept, sems = rest[: extra // 2], rest[extra // 2 : -1 - extra // 2], rest[-1 - extra // 2 : -1], rest[-1]
    copies = [pltpu.make_async_copy(old, new, sems.at[i]) for i, (old, new) in enumerate(zip(small, kept))]
    for (first, count), out in zip(chunks, outs):
        here = pl.ds(first * HEAD_DIM, count * HEAD_DIM)
        for side, field in enumerate((keys, values)):
            to = pl.ds(side * count * HEAD_DIM, count * HEAD_DIM)
            for piece in range(PIECES):
                share = field.shape[1] // PIECES
                rows = pl.ds(piece * share, share)
                sem = sems.at[len(copies)]
                copies.append(pltpu.make_async_copy(field.at[0, rows, here], out.at[rows, to], sem))
    for copy in copies:
        copy.start()
    for copy in copies:
        copy.wait()


def normalize(field):
    inverse = lax.rsqrt(jnp.mean(field * field, -1, keepdims=True) + EPSILON)
    return field * inverse, inverse


def dot(left, right, over):
    return lax.dot_general(left, right, ((over[:1], over[1:]), ((), ())), preferred_element_type=F32)


def attend(
    first, count, at_own, at_x, at_near, at_far, segments, queries, out_grad, own, across_x, arrived_near, arrived_far,
    across_k, across_v,    query_gain, key_gain, *rest,
):
    attended, query_grad, part_own, part_near, part_far, third_k, third_v, part_next, gains = rest
    position = lax.axis_index("ctx")
    rows = queries.shape[1]
    band = (GREACH + 1) * rows
    gain_q = query_gain[...]
    gain_k = key_gain[...]

    def segment(distance):
        block = position - distance
        first = pl.multiple_of(jnp.maximum(block, 0) * rows, rows)
        return jnp.where(block >= 0, segments[:, pl.ds(first, rows)], -1)

    key_seg = jnp.concatenate([segment(distance) for distance in range(GREACH, -1, -1)], 1)
    query_seg = jnp.broadcast_to(segment(0), (rows, rows)).T[:, :1]
    back = (
        lax.broadcasted_iota(jnp.int32, (rows, band), 0)
        - lax.broadcasted_iota(jnp.int32, (rows, band), 1)
        + GREACH * rows
    )
    live = (query_seg == key_seg) & (back >= 0) & (back < WINDOW)
    live = jnp.concatenate([live] * GROUPS, 0)

    query_gains = jnp.zeros((1, HEAD_DIM), F32)
    key_gains = jnp.zeros((1, HEAD_DIM), F32)

    def band_of(index):
        third = (across_k, 0) if index < count else (across_v, -count * HEAD_DIM)
        blocks = ((arrived_far, at_far), third, (arrived_near, at_near), (across_x, at_x), (own, at_own))
        return jnp.concatenate(
            [field[:, at + index * HEAD_DIM : at + (index + 1) * HEAD_DIM] for field, at in blocks], 0
        )

    for head in range(count):
        at_k = slice(head * HEAD_DIM, (head + 1) * HEAD_DIM)
        at_v = slice((count + head) * HEAD_DIM, (count + head + 1) * HEAD_DIM)
        at_q = [slice((head * GROUPS + g) * HEAD_DIM, (head * GROUPS + g + 1) * HEAD_DIM) for g in range(GROUPS)]
        from_q = [slice(at.start + first * GROUPS * HEAD_DIM, at.stop + first * GROUPS * HEAD_DIM) for at in at_q]
        band_v = band_of(count + head)
        k_normed, _ = normalize(band_of(head).astype(F32))
        k_rounded = (k_normed * gain_k).astype(BF16)
        q_normed, q_inverse = normalize(jnp.concatenate([queries[0, :, at] for at in from_q], 0).astype(F32))
        q_scaled = (q_normed * gain_q * HEAD_DIM ** (-0.5)).astype(BF16)
        grads = jnp.concatenate([out_grad[0, :, at] for at in from_q], 0)

        scores = dot(q_scaled, k_rounded, (1, 1))
        weights = jnp.where(live, jnp.exp(scores), 0.0)
        probs = weights * (1.0 / jnp.sum(weights, -1, keepdims=True))
        probs_low = probs.astype(BF16)
        dprob = dot(grads, band_v, (1, 1))
        centre = jnp.sum(probs * dprob, -1, keepdims=True)
        dscore = (probs * (dprob - centre)).astype(BF16)
        key_parts = dot(dscore, q_scaled, (0, 0))
        value_parts = dot(probs_low, grads, (0, 0))
        for at, parts, third in ((at_k, key_parts, third_k), (at_v, value_parts, third_v)):
            part_far[:, at] = parts[:rows]
            third[:, at_k] = parts[rows : 2 * rows].astype(BF16)
            part_near[:, at] = parts[2 * rows : 3 * rows]
            part_next[:, at] = parts[3 * rows : 4 * rows].astype(BF16)
            part_own[:, at] = parts[4 * rows :]

        output = dot(probs_low, band_v, (1, 0)).astype(BF16)
        dq = dot(dscore, k_rounded, (1, 0)) * HEAD_DIM ** (-0.5)
        scaled = dq * gain_q
        grad = q_inverse * (scaled - q_normed * jnp.mean(scaled * q_normed, -1, keepdims=True))
        grad = grad.astype(BF16)
        for g, at in enumerate(at_q):
            attended[:, at] = output[g * rows : (g + 1) * rows]
            query_grad[:, at] = grad[g * rows : (g + 1) * rows]
        query_gains = query_gains + jnp.sum(dq * q_normed, 0, keepdims=True)
        key_gains = key_gains + jnp.sum(key_parts * k_normed, 0, keepdims=True)
    gains[0:1, :] = query_gains
    gains[1:2, :] = key_gains


def assemble(*refs):
    amount = len(CHUNKS)
    for index, out in enumerate(refs[-2:]):
        for (first, count), part in zip(CHUNKS, refs[index * amount : (index + 1) * amount]):
            out[0, :, first * GROUPS * HEAD_DIM : (first + count) * GROUPS * HEAD_DIM] = part[...]


def add(*refs):
    refs[-1][...] = sum(ref[...] for ref in refs[1:-1]) + refs[0][...]


def scale(factor, *refs):
    total = sum(ref[...] for ref in refs[1:-2]) + refs[0][...]
    refs[-2][...] = total[0:1, :] * factor
    refs[-1][...] = total[1:2, :] * factor


def finish(count, at, keys, key_gain, part_own, swapped, arrived, *rest):
    key_grad, value_grad = rest[-2:]
    rows = part_own.shape[0]
    gain_k = key_gain[...]
    for head in range(count):

        def total(index):
            here = slice(index * HEAD_DIM, (index + 1) * HEAD_DIM)
            there = slice(at + index * HEAD_DIM, at + (index + 1) * HEAD_DIM)
            extra = jnp.where(core_index() == 0, swapped[:, here].astype(F32), 0.0)
            return part_own[:, here] + extra + arrived[:, there].astype(F32)

        out = slice(head * HEAD_DIM, (head + 1) * HEAD_DIM)
        normed, inverse = normalize(keys[0, :, out].astype(F32))
        scaled = total(head) * gain_k
        grad = inverse * (scaled - normed * jnp.mean(scaled * normed, -1, keepdims=True))
        key_grad[0, :, out] = grad.astype(BF16)
        value_grad[0, :, out] = total(count + head).astype(BF16)


def columns(rows, width, first):
    return pl.BlockSpec((1, rows, width), lambda i: (0, 0, first // width))


def move(field, axis, target):
    size = lax.axis_size(axis)
    return lax.ppermute(field, axis, [(i, target(i)) for i in range(size) if 0 <= target(i) < size])


def up(field):
    return move(field, "ctx", lambda i: i + 2)


def down(field):
    return move(field, "ctx", lambda i: i - 2)


def swap(field):
    return move(field, "ctx", lambda i: i ^ 1)


def total_over(field, axis, unit, end, most, cost=0):
    end = min(end, lax.axis_size(axis))
    while unit < end:
        group = min(most, end // unit)
        others = [move(field, axis, lambda i: i ^ (by * unit)) for by in range(1, group)]
        (field,) = call(add, "add", dict(enumerate([field, *others])), dict(o=shape(*field.shape, F32)), cost=cost)
        unit *= group
    return field


def shards(segment_ids, queries, keys, values, query_gain, key_gain, out_grad):
    rows = queries.shape[1]
    gain_q = query_gain.reshape(1, HEAD_DIM)
    gain_k = key_gain.reshape(1, HEAD_DIM)
    amount = len(CHUNKS)
    width = [2 * count * HEAD_DIM for _, count in CHUNKS] + [0] * LAG
    def gather(chunks, small=(), after=()):
        sources = [pltpu.with_memory_space_constraint(field, pltpu.HBM) for field in (keys, values, *small)]
        made = call(
            functools.partial(payload, chunks),
            "payload",
            dict(enumerate(sources)),
            dict(
                enumerate(
                    [shape(rows, 2 * count * HEAD_DIM) for _, count in chunks]
                    + [jax.ShapeDtypeStruct(field.shape, field.dtype) for field in small]
                )
            ),
            after,
            in_specs=dict.fromkeys(range(len(sources)), ANY),
            scratch_shapes=[pltpu.SemaphoreType.DMA((2 * len(chunks) * PIECES + len(small),))],
        )
        return made[: len(chunks)], made[len(chunks) :]

    own, _ = gather(CHUNKS[:1])
    near = {0: (up(own[0]), 0)}
    more, (segments, gain_q, gain_k) = gather(CHUNKS[1:], (segment_ids, gain_q, gain_k), own)
    own = [(field, 0) for field in (*own, *more)]
    for chunk in range(1, LAG):
        near[chunk] = (up(own[chunk][0]), 0)
    far, next_behind, third_behind = {}, {}, {}

    def climb(steps, after=()):
        ins, outs, jobs = {}, {}, []

        def use(place, chunk):
            field, at = place
            key = next((key for key, value in ins.items() if value is field), f"in{len(ins)}")
            ins[key] = field
            return key, slice(at, at + width[chunk])

        def exchange(to, chunk, first, second, halves=1):
            part = width[chunk] // halves
            for half in range(halves):
                pick = [(key, slice(at.start + half * part, at.start + (half + 1) * part)) for key, at in (use(first[chunk], chunk), use(second[chunk], chunk))]
                jobs.append((f"{to}{half}", 0, *pick))
                outs[f"{to}{half}"] = shape(rows, part)

        for step in steps:
            rise = 0
            if step + LAG < amount:
                jobs.append((f"rise{step}", rise, use(own[step + LAG], step + LAG), None))
                rise += width[step + LAG]
            if step < amount:
                jobs.append((f"rise{step}", rise, use(near[step], step), None))
                outs[f"rise{step}"] = shape(rows, rise + width[step])
                exchange("next", step, own, near)
            if step >= LAG:
                exchange("third", step - LAG, near, far, 2)

        def body(*refs):
            ref = dict(zip(list(ins) + list(outs), refs))
            for to, at, (key, here), other in jobs:
                value = ref[key][:, here]
                if other is not None:
                    value = jnp.where(core_index() == 0, value, ref[other[0]][:, other[1]])
                ref[to][:, at : at + value.shape[1]] = value

        made = dict(zip(outs, call(body, "climb", ins, outs, after, cost=10**9 * steps[0])))
        for step in steps:
            if step < amount:
                arrived = up(made[f"rise{step}"])
                ahead = 0
                if step + LAG < amount:
                    near[step + LAG] = (arrived, 0)
                    ahead = width[step + LAG]
                far[step] = (arrived, ahead)
                next_behind[step] = (swap(made["next0"]), 0)
            if step >= LAG:
                third_behind[step - LAG] = [swap(made["third0"]), swap(made["third1"])]
        return [next(iter(made.values()))]

    parts, sunk = [], {}

    def sink(step, after=()):
        fresh, older = step < amount, step >= LAG
        mine, below = width[step], width[step - LAG] if older else 0
        ins = {}
        if fresh:
            ins.update(far=parts[step]["far"], third_k=parts[step]["third_k"], third_v=parts[step]["third_v"])
        if older:
            chunk = step - LAG
            ins.update(near=parts[chunk]["near"], arrived=sunk[chunk])
            ins.update(old_k=parts[chunk]["third_k"], old_v=parts[chunk]["third_v"], next_old=parts[chunk]["next"])

        def body(*refs):
            ref = dict(zip(list(ins) + ["out"], refs))
            first = core_index() == 0
            if fresh:
                for half, extra in ((slice(0, mine // 2), ref["third_k"]), (slice(mine // 2, mine), ref["third_v"])):
                    extra = jnp.where(first, 0.0, extra[...].astype(F32))
                    ref["out"][:, half] = (ref["far"][:, half] + extra).astype(BF16)
            if older:
                for half, extra in ((slice(0, below // 2), ref["old_k"]), (slice(below // 2, below), ref["old_v"])):
                    extra = jnp.where(first, extra[...], ref["next_old"][:, half]).astype(F32)
                    total = ref["near"][:, half] + extra + ref["arrived"][:, half].astype(F32)
                    ref["out"][:, mine + half.start : mine + half.stop] = total.astype(BF16)

        (total,) = call(body, "sink", ins, dict(out=shape(rows, mine + below)), after)
        sunk[step] = down(total)
        return total

    made, gains, last, token = [], [], [], []
    order = []
    for step in range(LAG):
        order = climb([step], order)
    for chunk, (first, count) in enumerate(CHUNKS):
        order = climb([chunk + LAG], order + token)
        held = (own, next_behind, near, far)
        wide = shape(rows, GROUPS * count * HEAD_DIM)
        whole, low, half = shape(rows, width[chunk], F32), shape(rows, width[chunk]), shape(rows, width[chunk] // 2)
        result = call(
            functools.partial(attend, first, count, *(place[chunk][1] for place in held)),
            "attend",
            dict(
                segments=segments, queries=queries, out_grad=out_grad, own=own[chunk][0],
                **{f"behind{i}": place[chunk][0] for i, place in enumerate(held[1:])},
                third_k=third_behind[chunk][0], third_v=third_behind[chunk][1], gain_q=gain_q, gain_k=gain_k,
            ),
            dict(
                attended=wide, query_grad=wide, own=whole, near=whole, far=whole,
                third_k=half, third_v=half, next=low,
                gains=shape(2, HEAD_DIM, F32),
            ),
            last,
        )
        made.append(result[:2])
        gains.append(result[8])
        token = [result[8]]
        parts.append(dict(zip(("own", "near", "far"), result[2:5])))
        parts[-1].update(third_k=swap(result[5]), third_v=swap(result[6]), next=swap(result[7]))
        if chunk == amount - 1:
            (total,) = call(add, "add", dict(enumerate(gains)), dict(o=shape(2, HEAD_DIM, F32)))
            total = total_over(total, "ctx", 1, 2, 2)
            last = [*last, total]
        last = [sink(chunk, last)]

    for step in range(amount, amount + LAG):
        if step == amount:
            total = total_over(total, "dp", 1, 2, 2)
        last = [sink(step, [*last, total])]
    key_outputs = []
    for chunk, (first, count) in enumerate(CHUNKS):
        narrow = columns(rows, count * HEAD_DIM, first * HEAD_DIM)
        key_outputs = call(
            functools.partial(finish, count, width[chunk + LAG]),
            "finish",
            dict(
                keys=keys, gain=gain_k, own=parts[chunk]["own"], next=parts[chunk]["next"], arrived=sunk[chunk + LAG]
            ),
            dict(
                key_grad=jax.ShapeDtypeStruct(keys.shape, BF16), value_grad=jax.ShapeDtypeStruct(keys.shape, BF16)
            ),
            key_outputs,
            cost=(F_COST, G_COST)[chunk],
            grid=(1,),
            in_specs=dict(keys=narrow),
            out_specs=dict(key_grad=narrow, value_grad=narrow),
            input_output_aliases={5 + i: i for i in range(len(key_outputs))},
        )
    attended, query_grad = call(
        assemble,
        "assemble",
        {(i, chunk): made[chunk][i] for i in range(2) for chunk in range(amount)},
        dict(a=jax.ShapeDtypeStruct(queries.shape, BF16), b=jax.ShapeDtypeStruct(queries.shape, BF16)),
        last,
    )

    factor = (lax.axis_size("dp") * queries.shape[0] * lax.axis_size("ctx") * rows) ** (-0.5)
    row = shape(1, HEAD_DIM, F32)
    chips = lax.axis_size("ctx") // 2
    while chips > 4:
        total = total_over(total, "ctx", chips, 2 * chips, 2)
        chips //= 2
    total = total_over(total, "ctx", 2, 2 * chips, 4, cost=Z_COST)
    half = lax.axis_size("dp") // 2
    total = total_over(total, "dp", 2, half, 2)
    others = [move(total, "dp", lambda i: i ^ half)] if half > 1 else []
    query_gains, key_gains = call(
        functools.partial(scale, factor), "scale", dict(enumerate([total, *others])), dict(a=row, b=row), cost=S_COST
    )
    return attended, query_grad, *key_outputs, query_gains[0], key_gains[0]


def solution(mesh):
    block = P("dp", "ctx", None)
    return jax.shard_map(
        shards,
        mesh=mesh,
        in_specs=(P("dp", None), block, block, block, P(), P(), block),
        out_specs=(block, block, block, block, P(), P()),
        check_vma=False,
    )
```

```python
import functools

import jax
import jax.numpy as jnp
from jax import lax
from jax.experimental import pallas as pl
from jax.experimental.pallas import tpu as pltpu
from jax.sharding import PartitionSpec as P

HEADS = 8
KV_HEADS = 4
HEAD_DIM = 256
WINDOW = 512
GREACH = 4
GROUPS = HEADS // KV_HEADS
EPSILON = 1e-06
BF16 = jnp.bfloat16
F32 = jnp.float32
CHUNKS = ((0, 2), (2, 2))
LAG = 2

PIECES = 4

GAIN_ROWS = 32

VMEM = pl.BlockSpec(memory_space=pltpu.VMEM)
ANY = pl.BlockSpec(memory_space=pl.ANY)


def call(body, name, ins, outs, after=(), cost=0, in_specs=None, out_specs=None, **more):
    names = list(ins)

    def kernel(*refs):
        used = len(names) + len(after)
        body(*refs[: len(names)], *refs[used:])

    specs = [(in_specs or {}).get(key, VMEM) for key in names] + [ANY] * len(after)
    return pl.pallas_call(
        kernel,
        out_shape=list(outs.values()),
        in_specs=specs,
        out_specs=[(out_specs or {}).get(key, VMEM) for key in outs],
        compiler_params=pltpu.CompilerParams(vmem_limit_bytes=40 * 2**20),
        cost_estimate=pl.CostEstimate(flops=cost, bytes_accessed=1, transcendentals=0),
        name=name,
        **more,
    )(*ins.values(), *after)


def shape(rows, cols, dtype=BF16):
    return jax.ShapeDtypeStruct((rows, cols), dtype)


def core_index():
    return lax.axis_index("ctx") % 2


def payload(chunks, keys, values, *rest):
    extra = len(rest[:-1]) - len(chunks)
    small, outs, kept, sems = rest[: extra // 2], rest[extra // 2 : -1 - extra // 2], rest[-1 - extra // 2 : -1], rest[-1]
    copies = [pltpu.make_async_copy(old, new, sems.at[i]) for i, (old, new) in enumerate(zip(small, kept))]
    for (first, count), out in zip(chunks, outs):
        here = pl.ds(first * HEAD_DIM, count * HEAD_DIM)
        for side, field in enumerate((keys, values)):
            to = pl.ds(side * count * HEAD_DIM, count * HEAD_DIM)
            for piece in range(PIECES):
                share = field.shape[1] // PIECES
                rows = pl.ds(piece * share, share)
                sem = sems.at[len(copies)]
                copies.append(pltpu.make_async_copy(field.at[0, rows, here], out.at[rows, to], sem))
    for copy in copies:
        copy.start()
    for copy in copies:
        copy.wait()


def normalize(field):
    inverse = lax.rsqrt(jnp.mean(field * field, -1, keepdims=True) + EPSILON)
    return field * inverse, inverse


def dot(left, right, over):
    return lax.dot_general(left, right, ((over[:1], over[1:]), ((), ())), preferred_element_type=F32)


def attend(
    first, count, at_own, at_x, at_near, at_far, segments, queries, out_grad, own, across_x, arrived_near, arrived_far,
    across_k, across_v,    query_gain, key_gain, *rest,
):
    attended, query_grad, part_own, part_near, part_far, third_k, third_v, part_next, gains = rest[-9:]
    earlier = rest[0] if len(rest) > 9 else None
    position = lax.axis_index("ctx")
    rows = queries.shape[1]
    band = (GREACH + 1) * rows
    gain_q = query_gain[...]
    gain_k = key_gain[...]

    def segment(distance):
        block = position - distance
        first = pl.multiple_of(jnp.maximum(block, 0) * rows, rows)
        return jnp.where(block >= 0, segments[:, pl.ds(first, rows)], -1)

    key_seg = jnp.concatenate([segment(distance) for distance in range(GREACH, -1, -1)], 1)
    query_seg = jnp.broadcast_to(segment(0), (rows, rows)).T[:, :1]
    back = (
        lax.broadcasted_iota(jnp.int32, (rows, band), 0)
        - lax.broadcasted_iota(jnp.int32, (rows, band), 1)
        + GREACH * rows
    )
    live = (query_seg == key_seg) & (back >= 0) & (back < WINDOW)
    live = jnp.concatenate([live] * GROUPS, 0)

    def folded(field):
        return jnp.sum(field.reshape(-1, GAIN_ROWS, HEAD_DIM), 0)

    query_gains = 0.0 if earlier is None else earlier[:GAIN_ROWS, :]
    key_gains = 0.0 if earlier is None else earlier[GAIN_ROWS:, :]

    def band_of(index):
        third = (across_k, 0) if index < count else (across_v, -count * HEAD_DIM)
        blocks = ((arrived_far, at_far), third, (arrived_near, at_near), (across_x, at_x), (own, at_own))
        return jnp.concatenate(
            [field[:, at + index * HEAD_DIM : at + (index + 1) * HEAD_DIM] for field, at in blocks], 0
        )

    for head in range(count):
        at_k = slice(head * HEAD_DIM, (head + 1) * HEAD_DIM)
        at_v = slice((count + head) * HEAD_DIM, (count + head + 1) * HEAD_DIM)
        at_q = [slice((head * GROUPS + g) * HEAD_DIM, (head * GROUPS + g + 1) * HEAD_DIM) for g in range(GROUPS)]
        from_q = [slice(at.start + first * GROUPS * HEAD_DIM, at.stop + first * GROUPS * HEAD_DIM) for at in at_q]
        band_v = band_of(count + head)
        k_normed, _ = normalize(band_of(head).astype(F32))
        k_rounded = (k_normed * gain_k).astype(BF16)
        q_normed, q_inverse = normalize(jnp.concatenate([queries[0, :, at] for at in from_q], 0).astype(F32))
        q_scaled = (q_normed * gain_q * HEAD_DIM ** (-0.5)).astype(BF16)
        grads = jnp.concatenate([out_grad[0, :, at] for at in from_q], 0)

        scores = dot(q_scaled, k_rounded, (1, 1))
        weights = jnp.where(live, jnp.exp(scores), 0.0)
        probs = weights * (1.0 / jnp.sum(weights, -1, keepdims=True))
        probs_low = probs.astype(BF16)
        dprob = dot(grads, band_v, (1, 1))
        centre = jnp.sum(probs * dprob, -1, keepdims=True)
        dscore = (probs * (dprob - centre)).astype(BF16)
        key_parts = dot(dscore, q_scaled, (0, 0))
        value_parts = dot(probs_low, grads, (0, 0))
        for at, parts, third in ((at_k, key_parts, third_k), (at_v, value_parts, third_v)):
            part_far[:, at] = parts[:rows]
            third[:, at_k] = parts[rows : 2 * rows].astype(BF16)
            part_near[:, at] = parts[2 * rows : 3 * rows]
            part_next[:, at] = parts[3 * rows : 4 * rows].astype(BF16)
            part_own[:, at] = parts[4 * rows :]

        output = dot(probs_low, band_v, (1, 0)).astype(BF16)
        dq = dot(dscore, k_rounded, (1, 0)) * HEAD_DIM ** (-0.5)
        scaled = dq * gain_q
        grad = q_inverse * (scaled - q_normed * jnp.mean(scaled * q_normed, -1, keepdims=True))
        grad = grad.astype(BF16)
        for g, at in enumerate(at_q):
            attended[:, at] = output[g * rows : (g + 1) * rows]
            query_grad[:, at] = grad[g * rows : (g + 1) * rows]
        query_gains = query_gains + folded(dq * q_normed)
        key_gains = key_gains + folded(key_parts * k_normed)
    gains[:GAIN_ROWS, :] = query_gains
    gains[GAIN_ROWS:, :] = key_gains


def assemble(*refs):
    amount = len(CHUNKS)
    for index, out in enumerate(refs[-2:]):
        for (first, count), part in zip(CHUNKS, refs[index * amount : (index + 1) * amount]):
            out[0, :, first * GROUPS * HEAD_DIM : (first + count) * GROUPS * HEAD_DIM] = part[...]


def scale(factor, total, query_gains, key_gains):
    query_gains[...] = jnp.sum(total[:GAIN_ROWS, :], 0, keepdims=True) * factor
    key_gains[...] = jnp.sum(total[GAIN_ROWS:, :], 0, keepdims=True) * factor


def finish(count, at, keys, key_gain, part_own, swapped, arrived, *rest):
    key_grad, value_grad = rest[-2:]
    rows = part_own.shape[0]
    gain_k = key_gain[...]
    for head in range(count):

        def total(index):
            here = slice(index * HEAD_DIM, (index + 1) * HEAD_DIM)
            there = slice(at + index * HEAD_DIM, at + (index + 1) * HEAD_DIM)
            extra = jnp.where(core_index() == 0, swapped[:, here].astype(F32), 0.0)
            return part_own[:, here] + extra + arrived[:, there].astype(F32)

        out = slice(head * HEAD_DIM, (head + 1) * HEAD_DIM)
        normed, inverse = normalize(keys[0, :, out].astype(F32))
        scaled = total(head) * gain_k
        grad = inverse * (scaled - normed * jnp.mean(scaled * normed, -1, keepdims=True))
        key_grad[0, :, out] = grad.astype(BF16)
        value_grad[0, :, out] = total(count + head).astype(BF16)


def columns(rows, width, first):
    return pl.BlockSpec((1, rows, width), lambda i: (0, 0, first // width))


def move(field, axis, target):
    size = lax.axis_size(axis)
    return lax.ppermute(field, axis, [(i, target(i)) for i in range(size) if 0 <= target(i) < size])


def up(field):
    return move(field, "ctx", lambda i: i + 2)


def down(field):
    return move(field, "ctx", lambda i: i - 2)


def swap(field):
    return move(field, "ctx", lambda i: i ^ 1)


def shards(segment_ids, queries, keys, values, query_gain, key_gain, out_grad):
    rows = queries.shape[1]
    gain_q = query_gain.reshape(1, HEAD_DIM)
    gain_k = key_gain.reshape(1, HEAD_DIM)
    amount = len(CHUNKS)
    width = [2 * count * HEAD_DIM for _, count in CHUNKS] + [0] * LAG
    def gather(chunks, small=(), after=()):
        sources = [pltpu.with_memory_space_constraint(field, pltpu.HBM) for field in (keys, values, *small)]
        made = call(
            functools.partial(payload, chunks),
            "payload",
            dict(enumerate(sources)),
            dict(
                enumerate(
                    [shape(rows, 2 * count * HEAD_DIM) for _, count in chunks]
                    + [jax.ShapeDtypeStruct(field.shape, field.dtype) for field in small]
                )
            ),
            after,
            in_specs=dict.fromkeys(range(len(sources)), ANY),
            scratch_shapes=[pltpu.SemaphoreType.DMA((2 * len(chunks) * PIECES + len(small),))],
        )
        return made[: len(chunks)], made[len(chunks) :]

    own, _ = gather(CHUNKS[:1])
    near = {0: (up(own[0]), 0)}
    more, (segments, gain_q, gain_k) = gather(CHUNKS[1:], (segment_ids, gain_q, gain_k), own)
    own = [(field, 0) for field in (*own, *more)]
    for chunk in range(1, LAG):
        near[chunk] = (up(own[chunk][0]), 0)
    far, next_behind, third_behind = {}, {}, {}

    def climb(steps, after=()):
        ins, outs, jobs = {}, {}, []

        def use(place, chunk):
            field, at = place
            key = next((key for key, value in ins.items() if value is field), f"in{len(ins)}")
            ins[key] = field
            return key, slice(at, at + width[chunk])

        def exchange(to, chunk, first, second, halves=1):
            part = width[chunk] // halves
            for half in range(halves):
                pick = [(key, slice(at.start + half * part, at.start + (half + 1) * part)) for key, at in (use(first[chunk], chunk), use(second[chunk], chunk))]
                jobs.append((f"{to}{half}", 0, *pick))
                outs[f"{to}{half}"] = shape(rows, part)

        for step in steps:
            rise = 0
            if step + LAG < amount:
                jobs.append((f"rise{step}", rise, use(own[step + LAG], step + LAG), None))
                rise += width[step + LAG]
            if step < amount:
                jobs.append((f"rise{step}", rise, use(near[step], step), None))
                outs[f"rise{step}"] = shape(rows, rise + width[step])
                exchange("next", step, own, near)
            if step >= LAG:
                exchange("third", step - LAG, near, far, 2)

        def body(*refs):
            ref = dict(zip(list(ins) + list(outs), refs))
            for to, at, (key, here), other in jobs:
                value = ref[key][:, here]
                if other is not None:
                    value = jnp.where(core_index() == 0, value, ref[other[0]][:, other[1]])
                ref[to][:, at : at + value.shape[1]] = value

        made = dict(zip(outs, call(body, "climb", ins, outs, after, cost=10**9 * steps[0])))
        for step in steps:
            if step < amount:
                arrived = up(made[f"rise{step}"])
                ahead = 0
                if step + LAG < amount:
                    near[step + LAG] = (arrived, 0)
                    ahead = width[step + LAG]
                far[step] = (arrived, ahead)
                next_behind[step] = (swap(made["next0"]), 0)
            if step >= LAG:
                third_behind[step - LAG] = [swap(made["third0"]), swap(made["third1"])]
        return [next(iter(made.values()))]

    parts, sunk = [], {}

    def sink(step, after=()):
        fresh, older = step < amount, step >= LAG
        mine, below = width[step], width[step - LAG] if older else 0
        ins = {}
        if fresh:
            ins.update(far=parts[step]["far"], third_k=parts[step]["third_k"], third_v=parts[step]["third_v"])
        if older:
            chunk = step - LAG
            ins.update(near=parts[chunk]["near"], arrived=sunk[chunk])
            ins.update(old_k=parts[chunk]["third_k"], old_v=parts[chunk]["third_v"], next_old=parts[chunk]["next"])

        def body(*refs):
            ref = dict(zip(list(ins) + ["out"], refs))
            first = core_index() == 0
            if fresh:
                for half, extra in ((slice(0, mine // 2), ref["third_k"]), (slice(mine // 2, mine), ref["third_v"])):
                    extra = jnp.where(first, 0.0, extra[...].astype(F32))
                    ref["out"][:, half] = (ref["far"][:, half] + extra).astype(BF16)
            if older:
                for half, extra in ((slice(0, below // 2), ref["old_k"]), (slice(below // 2, below), ref["old_v"])):
                    extra = jnp.where(first, extra[...], ref["next_old"][:, half]).astype(F32)
                    total = ref["near"][:, half] + extra + ref["arrived"][:, half].astype(F32)
                    ref["out"][:, mine + half.start : mine + half.stop] = total.astype(BF16)

        (total,) = call(body, "sink", ins, dict(out=shape(rows, mine + below)), after)
        sunk[step] = down(total)
        return total

    made, gains, last, token = [], [], [], []
    order = []
    for step in range(LAG):
        order = climb([step], order)
    for chunk, (first, count) in enumerate(CHUNKS):
        order = climb([chunk + LAG], order + token)
        held = (own, next_behind, near, far)
        wide = shape(rows, GROUPS * count * HEAD_DIM)
        whole, low, half = shape(rows, width[chunk], F32), shape(rows, width[chunk]), shape(rows, width[chunk] // 2)
        result = call(
            functools.partial(attend, first, count, *(place[chunk][1] for place in held)),
            "attend",
            dict(
                segments=segments, queries=queries, out_grad=out_grad, own=own[chunk][0],
                **{f"behind{i}": place[chunk][0] for i, place in enumerate(held[1:])},
                third_k=third_behind[chunk][0], third_v=third_behind[chunk][1], gain_q=gain_q, gain_k=gain_k,
                **({"earlier": gains[0]} if gains else {}),
            ),
            dict(
                attended=wide, query_grad=wide, own=whole, near=whole, far=whole,
                third_k=half, third_v=half, next=low,
                gains=shape(2 * GAIN_ROWS, HEAD_DIM, F32),
            ),
            last,
        )
        made.append(result[:2])
        gains = [result[8]]
        token = [result[8]]
        parts.append(dict(zip(("own", "near", "far"), result[2:5])))
        parts[-1].update(third_k=swap(result[5]), third_v=swap(result[6]), next=swap(result[7]))
        last = [sink(chunk, last)]

    total = lax.psum(gains[0], ("dp", "ctx"))
    for step in range(amount, amount + LAG):
        last = [sink(step, last)]
    key_outputs = []
    for chunk, (first, count) in enumerate(CHUNKS):
        narrow = columns(rows, count * HEAD_DIM, first * HEAD_DIM)
        key_outputs = call(
            functools.partial(finish, count, width[chunk + LAG]),
            "finish",
            dict(
                keys=keys, gain=gain_k, own=parts[chunk]["own"], next=parts[chunk]["next"], arrived=sunk[chunk + LAG]
            ),
            dict(
                key_grad=jax.ShapeDtypeStruct(keys.shape, BF16), value_grad=jax.ShapeDtypeStruct(keys.shape, BF16)
            ),
            key_outputs,
            cost=2**31 * (1 + chunk),
            grid=(1,),
            in_specs=dict(keys=narrow),
            out_specs=dict(key_grad=narrow, value_grad=narrow),
            input_output_aliases={5 + i: i for i in range(len(key_outputs))},
        )
    attended, query_grad = call(
        assemble,
        "assemble",
        {(i, chunk): made[chunk][i] for i in range(2) for chunk in range(amount)},
        dict(a=jax.ShapeDtypeStruct(queries.shape, BF16), b=jax.ShapeDtypeStruct(queries.shape, BF16)),
        last,
    )

    factor = (lax.axis_size("dp") * queries.shape[0] * lax.axis_size("ctx") * rows) ** (-0.5)
    row = shape(1, HEAD_DIM, F32)
    query_gains, key_gains = call(
        functools.partial(scale, factor),
        "scale",
        dict(total=total),
        dict(a=row, b=row),
        [pltpu.with_memory_space_constraint(field, pltpu.HBM) for field in (attended, *key_outputs)],
    )
    return attended, query_grad, *key_outputs, query_gains[0], key_gains[0]


def solution(mesh):
    block = P("dp", "ctx", None)
    return jax.shard_map(
        shards,
        mesh=mesh,
        in_specs=(P("dp", None), block, block, block, P(), P(), block),
        out_specs=(block, block, block, block, P(), P()),
        check_vma=False,
    )
```

```python
import functools

import jax
import jax.numpy as jnp
from jax import lax
from jax.experimental import pallas as pl
from jax.experimental.pallas import tpu as pltpu
from jax.sharding import PartitionSpec as P

HEADS = 8
KV_HEADS = 4
HEAD_DIM = 256
WINDOW = 512
GREACH = 4
GROUPS = HEADS // KV_HEADS
EPSILON = 1e-06
BF16 = jnp.bfloat16
F32 = jnp.float32
CHUNKS = ((0, 2), (2, 2))
LAG = 2

PIECES = 4

COSTS = 2**32, 0, 0, 2**31, 2**32, 2**32

VMEM = pl.BlockSpec(memory_space=pltpu.VMEM)
ANY = pl.BlockSpec(memory_space=pl.ANY)


def call(body, name, ins, outs, after=(), cost=0, in_specs=None, out_specs=None, **more):
    names = list(ins)

    def kernel(*refs):
        used = len(names) + len(after)
        body(*refs[: len(names)], *refs[used:])

    specs = [(in_specs or {}).get(key, VMEM) for key in names] + [ANY] * len(after)
    return pl.pallas_call(
        kernel,
        out_shape=list(outs.values()),
        in_specs=specs,
        out_specs=[(out_specs or {}).get(key, VMEM) for key in outs],
        compiler_params=pltpu.CompilerParams(vmem_limit_bytes=40 * 2**20),
        cost_estimate=pl.CostEstimate(flops=cost, bytes_accessed=1, transcendentals=0),
        name=name,
        **more,
    )(*ins.values(), *after)


def shape(rows, cols, dtype=BF16):
    return jax.ShapeDtypeStruct((rows, cols), dtype)


def core_index():
    return lax.axis_index("ctx") % 2


def payload(chunks, keys, values, *rest):
    extra = len(rest[:-1]) - len(chunks)
    small, outs, kept, sems = rest[: extra // 2], rest[extra // 2 : -1 - extra // 2], rest[-1 - extra // 2 : -1], rest[-1]
    copies = [pltpu.make_async_copy(old, new, sems.at[i]) for i, (old, new) in enumerate(zip(small, kept))]
    for (first, count), out in zip(chunks, outs):
        here = pl.ds(first * HEAD_DIM, count * HEAD_DIM)
        for side, field in enumerate((keys, values)):
            to = pl.ds(side * count * HEAD_DIM, count * HEAD_DIM)
            for piece in range(PIECES):
                share = field.shape[1] // PIECES
                rows = pl.ds(piece * share, share)
                sem = sems.at[len(copies)]
                copies.append(pltpu.make_async_copy(field.at[0, rows, here], out.at[rows, to], sem))
    for copy in copies:
        copy.start()
    for copy in copies:
        copy.wait()


def normalize(field):
    inverse = lax.rsqrt(jnp.mean(field * field, -1, keepdims=True) + EPSILON)
    return field * inverse, inverse


def dot(left, right, over):
    return lax.dot_general(left, right, ((over[:1], over[1:]), ((), ())), preferred_element_type=F32)


def attend(
    first, count, at_own, at_x, at_near, at_far, segments, queries, out_grad, own, across_x, arrived_near, arrived_far,
    across_k, across_v,    query_gain, key_gain, *rest,
):
    attended, query_grad, part_own, part_near, part_far, third_k, third_v, part_next, gains = rest
    position = lax.axis_index("ctx")
    rows = queries.shape[1]
    band = (GREACH + 1) * rows
    gain_q = query_gain[...]
    gain_k = key_gain[...]

    def segment(distance):
        block = position - distance
        first = pl.multiple_of(jnp.maximum(block, 0) * rows, rows)
        return jnp.where(block >= 0, segments[:, pl.ds(first, rows)], -1)

    key_seg = jnp.concatenate([segment(distance) for distance in range(GREACH, -1, -1)], 1)
    query_seg = jnp.broadcast_to(segment(0), (rows, rows)).T[:, :1]
    back = (
        lax.broadcasted_iota(jnp.int32, (rows, band), 0)
        - lax.broadcasted_iota(jnp.int32, (rows, band), 1)
        + GREACH * rows
    )
    live = (query_seg == key_seg) & (back >= 0) & (back < WINDOW)
    live = jnp.concatenate([live] * GROUPS, 0)

    query_gains = jnp.zeros((1, HEAD_DIM), F32)
    key_gains = jnp.zeros((1, HEAD_DIM), F32)

    def band_of(index):
        third = (across_k, 0) if index < count else (across_v, -count * HEAD_DIM)
        blocks = ((arrived_far, at_far), third, (arrived_near, at_near), (across_x, at_x), (own, at_own))
        return jnp.concatenate(
            [field[:, at + index * HEAD_DIM : at + (index + 1) * HEAD_DIM] for field, at in blocks], 0
        )

    for head in range(count):
        at_k = slice(head * HEAD_DIM, (head + 1) * HEAD_DIM)
        at_v = slice((count + head) * HEAD_DIM, (count + head + 1) * HEAD_DIM)
        at_q = [slice((head * GROUPS + g) * HEAD_DIM, (head * GROUPS + g + 1) * HEAD_DIM) for g in range(GROUPS)]
        from_q = [slice(at.start + first * GROUPS * HEAD_DIM, at.stop + first * GROUPS * HEAD_DIM) for at in at_q]
        band_v = band_of(count + head)
        k_normed, _ = normalize(band_of(head).astype(F32))
        k_rounded = (k_normed * gain_k).astype(BF16)
        q_normed, q_inverse = normalize(jnp.concatenate([queries[0, :, at] for at in from_q], 0).astype(F32))
        q_scaled = (q_normed * gain_q * HEAD_DIM ** (-0.5)).astype(BF16)
        grads = jnp.concatenate([out_grad[0, :, at] for at in from_q], 0)

        scores = dot(q_scaled, k_rounded, (1, 1))
        weights = jnp.where(live, jnp.exp(scores), 0.0)
        probs = weights * (1.0 / jnp.sum(weights, -1, keepdims=True))
        probs_low = probs.astype(BF16)
        dprob = dot(grads, band_v, (1, 1))
        centre = jnp.sum(probs * dprob, -1, keepdims=True)
        dscore = (probs * (dprob - centre)).astype(BF16)
        key_parts = dot(dscore, q_scaled, (0, 0))
        value_parts = dot(probs_low, grads, (0, 0))
        for at, parts, third in ((at_k, key_parts, third_k), (at_v, value_parts, third_v)):
            part_far[:, at] = parts[:rows]
            third[:, at_k] = parts[rows : 2 * rows].astype(BF16)
            part_near[:, at] = parts[2 * rows : 3 * rows]
            part_next[:, at] = parts[3 * rows : 4 * rows].astype(BF16)
            part_own[:, at] = parts[4 * rows :]

        output = dot(probs_low, band_v, (1, 0)).astype(BF16)
        dq = dot(dscore, k_rounded, (1, 0)) * HEAD_DIM ** (-0.5)
        scaled = dq * gain_q
        grad = q_inverse * (scaled - q_normed * jnp.mean(scaled * q_normed, -1, keepdims=True))
        grad = grad.astype(BF16)
        for g, at in enumerate(at_q):
            attended[:, at] = output[g * rows : (g + 1) * rows]
            query_grad[:, at] = grad[g * rows : (g + 1) * rows]
        query_gains = query_gains + jnp.sum(dq * q_normed, 0, keepdims=True)
        key_gains = key_gains + jnp.sum(key_parts * k_normed, 0, keepdims=True)
    gains[0:1, :] = query_gains
    gains[1:2, :] = key_gains


def assemble(*refs):
    amount = len(CHUNKS)
    for index, out in enumerate(refs[-2:]):
        for (first, count), part in zip(CHUNKS, refs[index * amount : (index + 1) * amount]):
            out[0, :, first * GROUPS * HEAD_DIM : (first + count) * GROUPS * HEAD_DIM] = part[...]


def add(*refs):
    refs[-1][...] = sum(ref[...] for ref in refs[1:-1]) + refs[0][...]


def scale(factor, *refs):
    total = sum(ref[...] for ref in refs[1:-2]) + refs[0][...]
    refs[-2][...] = total[0:1, :] * factor
    refs[-1][...] = total[1:2, :] * factor


def finish(count, at, keys, key_gain, part_own, swapped, arrived, *rest):
    key_grad, value_grad = rest[-2:]
    rows = part_own.shape[0]
    gain_k = key_gain[...]
    for head in range(count):

        def total(index):
            here = slice(index * HEAD_DIM, (index + 1) * HEAD_DIM)
            there = slice(at + index * HEAD_DIM, at + (index + 1) * HEAD_DIM)
            extra = jnp.where(core_index() == 0, swapped[:, here].astype(F32), 0.0)
            return part_own[:, here] + extra + arrived[:, there].astype(F32)

        out = slice(head * HEAD_DIM, (head + 1) * HEAD_DIM)
        normed, inverse = normalize(keys[0, :, out].astype(F32))
        scaled = total(head) * gain_k
        grad = inverse * (scaled - normed * jnp.mean(scaled * normed, -1, keepdims=True))
        key_grad[0, :, out] = grad.astype(BF16)
        value_grad[0, :, out] = total(count + head).astype(BF16)


def columns(rows, width, first):
    return pl.BlockSpec((1, rows, width), lambda i: (0, 0, first // width))


def move(field, axis, target):
    size = lax.axis_size(axis)
    return lax.ppermute(field, axis, [(i, target(i)) for i in range(size) if 0 <= target(i) < size])


def up(field):
    return move(field, "ctx", lambda i: i + 2)


def down(field):
    return move(field, "ctx", lambda i: i - 2)


def swap(field):
    return move(field, "ctx", lambda i: i ^ 1)


def total_over(field, axis, unit, end, most, cost=0, after=()):
    end = min(end, lax.axis_size(axis))
    while unit < end:
        group = min(most, end // unit)
        others = [move(field, axis, lambda i: i ^ (by * unit)) for by in range(1, group)]
        (field,) = call(add, "add", dict(enumerate([field, *others])), dict(o=shape(*field.shape, F32)), after, cost=cost)
        unit *= group
    return field


def shards(segment_ids, queries, keys, values, query_gain, key_gain, out_grad):
    rows = queries.shape[1]
    gain_q = query_gain.reshape(1, HEAD_DIM)
    gain_k = key_gain.reshape(1, HEAD_DIM)
    amount = len(CHUNKS)
    width = [2 * count * HEAD_DIM for _, count in CHUNKS] + [0] * LAG
    def gather(chunks, small=(), after=()):
        sources = [pltpu.with_memory_space_constraint(field, pltpu.HBM) for field in (keys, values, *small)]
        made = call(
            functools.partial(payload, chunks),
            "payload",
            dict(enumerate(sources)),
            dict(
                enumerate(
                    [shape(rows, 2 * count * HEAD_DIM) for _, count in chunks]
                    + [jax.ShapeDtypeStruct(field.shape, field.dtype) for field in small]
                )
            ),
            after,
            in_specs=dict.fromkeys(range(len(sources)), ANY),
            scratch_shapes=[pltpu.SemaphoreType.DMA((2 * len(chunks) * PIECES + len(small),))],
        )
        return made[: len(chunks)], made[len(chunks) :]

    own, _ = gather(CHUNKS[:1])
    near = {0: (up(own[0]), 0)}
    more, (segments, gain_q, gain_k) = gather(CHUNKS[1:], (segment_ids, gain_q, gain_k), own)
    own = [(field, 0) for field in (*own, *more)]
    for chunk in range(1, LAG):
        near[chunk] = (up(own[chunk][0]), 0)
    far, next_behind, third_behind = {}, {}, {}

    def climb(steps, after=()):
        ins, outs, jobs = {}, {}, []

        def use(place, chunk):
            field, at = place
            key = next((key for key, value in ins.items() if value is field), f"in{len(ins)}")
            ins[key] = field
            return key, slice(at, at + width[chunk])

        def exchange(to, chunk, first, second, halves=1):
            part = width[chunk] // halves
            for half in range(halves):
                pick = [(key, slice(at.start + half * part, at.start + (half + 1) * part)) for key, at in (use(first[chunk], chunk), use(second[chunk], chunk))]
                jobs.append((f"{to}{half}", 0, *pick))
                outs[f"{to}{half}"] = shape(rows, part)

        for step in steps:
            rise = 0
            if step + LAG < amount:
                jobs.append((f"rise{step}", rise, use(own[step + LAG], step + LAG), None))
                rise += width[step + LAG]
            if step < amount:
                jobs.append((f"rise{step}", rise, use(near[step], step), None))
                outs[f"rise{step}"] = shape(rows, rise + width[step])
                exchange("next", step, own, near)
            if step >= LAG:
                exchange("third", step - LAG, near, far, 2)

        def body(*refs):
            ref = dict(zip(list(ins) + list(outs), refs))
            for to, at, (key, here), other in jobs:
                value = ref[key][:, here]
                if other is not None:
                    value = jnp.where(core_index() == 0, value, ref[other[0]][:, other[1]])
                ref[to][:, at : at + value.shape[1]] = value

        made = dict(zip(outs, call(body, "climb", ins, outs, after, cost=10**9 * steps[0])))
        for step in steps:
            if step < amount:
                arrived = up(made[f"rise{step}"])
                ahead = 0
                if step + LAG < amount:
                    near[step + LAG] = (arrived, 0)
                    ahead = width[step + LAG]
                far[step] = (arrived, ahead)
                next_behind[step] = (swap(made["next0"]), 0)
            if step >= LAG:
                third_behind[step - LAG] = [swap(made["third0"]), swap(made["third1"])]
        return [next(iter(made.values()))]

    parts, sunk = [], {}

    def sink(step, after=()):
        fresh, older = step < amount, step >= LAG
        mine, below = width[step], width[step - LAG] if older else 0
        ins = {}
        if fresh:
            ins.update(far=parts[step]["far"], third_k=parts[step]["third_k"], third_v=parts[step]["third_v"])
        if older:
            chunk = step - LAG
            ins.update(near=parts[chunk]["near"], arrived=sunk[chunk])
            ins.update(old_k=parts[chunk]["third_k"], old_v=parts[chunk]["third_v"], next_old=parts[chunk]["next"])

        def body(*refs):
            ref = dict(zip(list(ins) + ["out"], refs))
            first = core_index() == 0
            if fresh:
                for half, extra in ((slice(0, mine // 2), ref["third_k"]), (slice(mine // 2, mine), ref["third_v"])):
                    extra = jnp.where(first, 0.0, extra[...].astype(F32))
                    ref["out"][:, half] = (ref["far"][:, half] + extra).astype(BF16)
            if older:
                for half, extra in ((slice(0, below // 2), ref["old_k"]), (slice(below // 2, below), ref["old_v"])):
                    extra = jnp.where(first, extra[...], ref["next_old"][:, half]).astype(F32)
                    total = ref["near"][:, half] + extra + ref["arrived"][:, half].astype(F32)
                    ref["out"][:, mine + half.start : mine + half.stop] = total.astype(BF16)

        (total,) = call(body, "sink", ins, dict(out=shape(rows, mine + below)), after)
        sunk[step] = down(total)
        return total

    made, gains, last, token = [], [], [], []
    order = []
    for step in range(LAG):
        order = climb([step], order)
    for chunk, (first, count) in enumerate(CHUNKS):
        order = climb([chunk + LAG], order + token)
        held = (own, next_behind, near, far)
        wide = shape(rows, GROUPS * count * HEAD_DIM)
        whole, low, half = shape(rows, width[chunk], F32), shape(rows, width[chunk]), shape(rows, width[chunk] // 2)
        result = call(
            functools.partial(attend, first, count, *(place[chunk][1] for place in held)),
            "attend",
            dict(
                segments=segments, queries=queries, out_grad=out_grad, own=own[chunk][0],
                **{f"behind{i}": place[chunk][0] for i, place in enumerate(held[1:])},
                third_k=third_behind[chunk][0], third_v=third_behind[chunk][1], gain_q=gain_q, gain_k=gain_k,
            ),
            dict(
                attended=wide, query_grad=wide, own=whole, near=whole, far=whole,
                third_k=half, third_v=half, next=low,
                gains=shape(2, HEAD_DIM, F32),
            ),
            last,
        )
        made.append(result[:2])
        gains.append(result[8])
        token = [result[8]]
        parts.append(dict(zip(("own", "near", "far"), result[2:5])))
        parts[-1].update(third_k=swap(result[5]), third_v=swap(result[6]), next=swap(result[7]))
        if chunk == amount - 1:
            (total,) = call(add, "add", dict(enumerate(gains)), dict(o=shape(2, HEAD_DIM, F32)))
            total = total_over(total, "ctx", 1, 2, 2)
            last = [*last, total]
        last = [sink(chunk, last)]

    for step in range(amount, amount + LAG):
        last = [sink(step, last)]

    factor = (lax.axis_size("dp") * queries.shape[0] * lax.axis_size("ctx") * rows) ** (-0.5)
    row = shape(1, HEAD_DIM, F32)
    chips = lax.axis_size("ctx") // 2
    (total,) = call(add, "add", dict(total=total), dict(o=shape(2, HEAD_DIM, F32)), [sunk[0]], cost=COSTS[5])
    while chips > 4:
        total = total_over(total, "ctx", chips, 2 * chips, 2)
        chips //= 2
    total = total_over(total, "ctx", 2, 2 * chips, 4, COSTS[0], [sunk[amount - 1]])
    half = lax.axis_size("dp") // 2
    total = total_over(total, "dp", 1, half, 2, COSTS[1])
    others = [move(total, "dp", lambda i: i ^ half)] if half else []
    query_gains, key_gains = call(
        functools.partial(scale, factor),
        "scale",
        dict(enumerate([total, *others])),
        dict(a=row, b=row),
        cost=COSTS[2],
    )
    attended, query_grad = call(
        assemble,
        "assemble",
        {(i, chunk): made[chunk][i] for i in range(2) for chunk in range(amount)},
        dict(a=jax.ShapeDtypeStruct(queries.shape, BF16), b=jax.ShapeDtypeStruct(queries.shape, BF16)),
        last,
    )
    before = [pltpu.with_memory_space_constraint(field, pltpu.HBM) for field in (attended, query_gains)]
    key_outputs = []
    for chunk, (first, count) in enumerate(CHUNKS):
        narrow = columns(rows, count * HEAD_DIM, first * HEAD_DIM)
        key_outputs = call(
            functools.partial(finish, count, width[chunk + LAG]),
            "finish",
            dict(
                keys=keys, gain=gain_k, own=parts[chunk]["own"], next=parts[chunk]["next"], arrived=sunk[chunk + LAG]
            ),
            dict(
                key_grad=jax.ShapeDtypeStruct(keys.shape, BF16), value_grad=jax.ShapeDtypeStruct(keys.shape, BF16)
            ),
            [*key_outputs, *(before if chunk == amount - 1 else [])],
            cost=COSTS[3 + chunk],
            grid=(1,),
            in_specs=dict(keys=narrow),
            out_specs=dict(key_grad=narrow, value_grad=narrow),
            input_output_aliases={5 + i: i for i in range(len(key_outputs))},
        )
    return attended, query_grad, *key_outputs, query_gains[0], key_gains[0]


def solution(mesh):
    block = P("dp", "ctx", None)
    return jax.shard_map(
        shards,
        mesh=mesh,
        in_specs=(P("dp", None), block, block, block, P(), P(), block),
        out_specs=(block, block, block, block, P(), P()),
        check_vma=False,
    )
```

```python
import functools

import jax
import jax.numpy as jnp
from jax import lax
from jax.experimental import pallas as pl
from jax.experimental.pallas import tpu as pltpu
from jax.sharding import PartitionSpec as P

HEADS = 8
KV_HEADS = 4
HEAD_DIM = 256
WINDOW = 512
GREACH = 4
GROUPS = HEADS // KV_HEADS
EPSILON = 1e-06
BF16 = jnp.bfloat16
F32 = jnp.float32
CHUNKS = ((0, 2), (2, 2))
LAG = 2

PIECES = 4

COSTS = 2**32, 0, 0, 2**31, 2**32, 2**31

VMEM = pl.BlockSpec(memory_space=pltpu.VMEM)
ANY = pl.BlockSpec(memory_space=pl.ANY)


def call(body, name, ins, outs, after=(), cost=0, in_specs=None, out_specs=None, **more):
    names = list(ins)

    def kernel(*refs):
        used = len(names) + len(after)
        body(*refs[: len(names)], *refs[used:])

    specs = [(in_specs or {}).get(key, VMEM) for key in names] + [ANY] * len(after)
    return pl.pallas_call(
        kernel,
        out_shape=list(outs.values()),
        in_specs=specs,
        out_specs=[(out_specs or {}).get(key, VMEM) for key in outs],
        compiler_params=pltpu.CompilerParams(vmem_limit_bytes=40 * 2**20),
        cost_estimate=pl.CostEstimate(flops=cost, bytes_accessed=1, transcendentals=0),
        name=name,
        **more,
    )(*ins.values(), *after)


def shape(rows, cols, dtype=BF16):
    return jax.ShapeDtypeStruct((rows, cols), dtype)


def core_index():
    return lax.axis_index("ctx") % 2


def payload(chunks, keys, values, *rest):
    extra = len(rest[:-1]) - len(chunks)
    small, outs, kept, sems = rest[: extra // 2], rest[extra // 2 : -1 - extra // 2], rest[-1 - extra // 2 : -1], rest[-1]
    copies = [pltpu.make_async_copy(old, new, sems.at[i]) for i, (old, new) in enumerate(zip(small, kept))]
    for (first, count), out in zip(chunks, outs):
        here = pl.ds(first * HEAD_DIM, count * HEAD_DIM)
        for side, field in enumerate((keys, values)):
            to = pl.ds(side * count * HEAD_DIM, count * HEAD_DIM)
            for piece in range(PIECES):
                share = field.shape[1] // PIECES
                rows = pl.ds(piece * share, share)
                sem = sems.at[len(copies)]
                copies.append(pltpu.make_async_copy(field.at[0, rows, here], out.at[rows, to], sem))
    for copy in copies:
        copy.start()
    for copy in copies:
        copy.wait()


def normalize(field):
    inverse = lax.rsqrt(jnp.mean(field * field, -1, keepdims=True) + EPSILON)
    return field * inverse, inverse


def dot(left, right, over):
    return lax.dot_general(left, right, ((over[:1], over[1:]), ((), ())), preferred_element_type=F32)


def attend(
    first, count, at_own, at_x, at_near, at_far, segments, queries, out_grad, own, across_x, arrived_near, arrived_far,
    across_k, across_v,    query_gain, key_gain, *rest,
):
    attended, query_grad, part_own, part_near, part_far, third_k, third_v, part_next, gains = rest
    position = lax.axis_index("ctx")
    rows = queries.shape[1]
    band = (GREACH + 1) * rows
    gain_q = query_gain[...]
    gain_k = key_gain[...]

    def segment(distance):
        block = position - distance
        first = pl.multiple_of(jnp.maximum(block, 0) * rows, rows)
        return jnp.where(block >= 0, segments[:, pl.ds(first, rows)], -1)

    key_seg = jnp.concatenate([segment(distance) for distance in range(GREACH, -1, -1)], 1)
    query_seg = jnp.broadcast_to(segment(0), (rows, rows)).T[:, :1]
    back = (
        lax.broadcasted_iota(jnp.int32, (rows, band), 0)
        - lax.broadcasted_iota(jnp.int32, (rows, band), 1)
        + GREACH * rows
    )
    live = (query_seg == key_seg) & (back >= 0) & (back < WINDOW)
    live = jnp.concatenate([live] * GROUPS, 0)

    query_gains = jnp.zeros((1, HEAD_DIM), F32)
    key_gains = jnp.zeros((1, HEAD_DIM), F32)

    def band_of(index):
        third = (across_k, 0) if index < count else (across_v, -count * HEAD_DIM)
        blocks = ((arrived_far, at_far), third, (arrived_near, at_near), (across_x, at_x), (own, at_own))
        return jnp.concatenate(
            [field[:, at + index * HEAD_DIM : at + (index + 1) * HEAD_DIM] for field, at in blocks], 0
        )

    for head in range(count):
        at_k = slice(head * HEAD_DIM, (head + 1) * HEAD_DIM)
        at_v = slice((count + head) * HEAD_DIM, (count + head + 1) * HEAD_DIM)
        at_q = [slice((head * GROUPS + g) * HEAD_DIM, (head * GROUPS + g + 1) * HEAD_DIM) for g in range(GROUPS)]
        from_q = [slice(at.start + first * GROUPS * HEAD_DIM, at.stop + first * GROUPS * HEAD_DIM) for at in at_q]
        band_v = band_of(count + head)
        k_normed, _ = normalize(band_of(head).astype(F32))
        k_rounded = (k_normed * gain_k).astype(BF16)
        q_normed, q_inverse = normalize(jnp.concatenate([queries[0, :, at] for at in from_q], 0).astype(F32))
        q_scaled = (q_normed * gain_q * HEAD_DIM ** (-0.5)).astype(BF16)
        grads = jnp.concatenate([out_grad[0, :, at] for at in from_q], 0)

        scores = dot(q_scaled, k_rounded, (1, 1))
        weights = jnp.where(live, jnp.exp(scores), 0.0)
        probs = weights * (1.0 / jnp.sum(weights, -1, keepdims=True))
        probs_low = probs.astype(BF16)
        dprob = dot(grads, band_v, (1, 1))
        centre = jnp.sum(probs * dprob, -1, keepdims=True)
        dscore = (probs * (dprob - centre)).astype(BF16)
        key_parts = dot(dscore, q_scaled, (0, 0))
        value_parts = dot(probs_low, grads, (0, 0))
        for at, parts, third in ((at_k, key_parts, third_k), (at_v, value_parts, third_v)):
            part_far[:, at] = parts[:rows]
            third[:, at_k] = parts[rows : 2 * rows].astype(BF16)
            part_near[:, at] = parts[2 * rows : 3 * rows]
            part_next[:, at] = parts[3 * rows : 4 * rows].astype(BF16)
            part_own[:, at] = parts[4 * rows :]

        output = dot(probs_low, band_v, (1, 0)).astype(BF16)
        dq = dot(dscore, k_rounded, (1, 0)) * HEAD_DIM ** (-0.5)
        scaled = dq * gain_q
        grad = q_inverse * (scaled - q_normed * jnp.mean(scaled * q_normed, -1, keepdims=True))
        grad = grad.astype(BF16)
        for g, at in enumerate(at_q):
            attended[:, at] = output[g * rows : (g + 1) * rows]
            query_grad[:, at] = grad[g * rows : (g + 1) * rows]
        query_gains = query_gains + jnp.sum(dq * q_normed, 0, keepdims=True)
        key_gains = key_gains + jnp.sum(key_parts * k_normed, 0, keepdims=True)
    gains[0:1, :] = query_gains
    gains[1:2, :] = key_gains


def assemble(*refs):
    amount = len(CHUNKS)
    for index, out in enumerate(refs[-2:]):
        for (first, count), part in zip(CHUNKS, refs[index * amount : (index + 1) * amount]):
            out[0, :, first * GROUPS * HEAD_DIM : (first + count) * GROUPS * HEAD_DIM] = part[...]


def add(*refs):
    refs[-1][...] = sum(ref[...] for ref in refs[1:-1]) + refs[0][...]


def scale(factor, *refs):
    total = sum(ref[...] for ref in refs[1:-2]) + refs[0][...]
    refs[-2][...] = total[0:1, :] * factor
    refs[-1][...] = total[1:2, :] * factor


def finish(count, at, keys, key_gain, part_own, swapped, arrived, *rest):
    key_grad, value_grad = rest[-2:]
    rows = part_own.shape[0]
    gain_k = key_gain[...]
    for head in range(count):

        def total(index):
            here = slice(index * HEAD_DIM, (index + 1) * HEAD_DIM)
            there = slice(at + index * HEAD_DIM, at + (index + 1) * HEAD_DIM)
            extra = jnp.where(core_index() == 0, swapped[:, here].astype(F32), 0.0)
            return part_own[:, here] + extra + arrived[:, there].astype(F32)

        out = slice(head * HEAD_DIM, (head + 1) * HEAD_DIM)
        normed, inverse = normalize(keys[0, :, out].astype(F32))
        scaled = total(head) * gain_k
        grad = inverse * (scaled - normed * jnp.mean(scaled * normed, -1, keepdims=True))
        key_grad[0, :, out] = grad.astype(BF16)
        value_grad[0, :, out] = total(count + head).astype(BF16)


def columns(rows, width, first):
    return pl.BlockSpec((1, rows, width), lambda i: (0, 0, first // width))


def move(field, axis, target):
    size = lax.axis_size(axis)
    return lax.ppermute(field, axis, [(i, target(i)) for i in range(size) if 0 <= target(i) < size])


def up(field):
    return move(field, "ctx", lambda i: i + 2)


def down(field):
    return move(field, "ctx", lambda i: i - 2)


def swap(field):
    return move(field, "ctx", lambda i: i ^ 1)


def total_over(field, axis, unit, end, most, cost=0, after=()):
    end = min(end, lax.axis_size(axis))
    while unit < end:
        group = min(most, end // unit)
        others = [move(field, axis, lambda i: i ^ (by * unit)) for by in range(1, group)]
        (field,) = call(add, "add", dict(enumerate([field, *others])), dict(o=shape(*field.shape, F32)), after, cost=cost)
        unit *= group
    return field


def shards(segment_ids, queries, keys, values, query_gain, key_gain, out_grad):
    rows = queries.shape[1]
    gain_q = query_gain.reshape(1, HEAD_DIM)
    gain_k = key_gain.reshape(1, HEAD_DIM)
    amount = len(CHUNKS)
    width = [2 * count * HEAD_DIM for _, count in CHUNKS] + [0] * LAG
    def gather(chunks, small=(), after=()):
        sources = [pltpu.with_memory_space_constraint(field, pltpu.HBM) for field in (keys, values, *small)]
        made = call(
            functools.partial(payload, chunks),
            "payload",
            dict(enumerate(sources)),
            dict(
                enumerate(
                    [shape(rows, 2 * count * HEAD_DIM) for _, count in chunks]
                    + [jax.ShapeDtypeStruct(field.shape, field.dtype) for field in small]
                )
            ),
            after,
            in_specs=dict.fromkeys(range(len(sources)), ANY),
            scratch_shapes=[pltpu.SemaphoreType.DMA((2 * len(chunks) * PIECES + len(small),))],
        )
        return made[: len(chunks)], made[len(chunks) :]

    own, _ = gather(CHUNKS[:1])
    near = {0: (up(own[0]), 0)}
    more, (segments, gain_q, gain_k) = gather(CHUNKS[1:], (segment_ids, gain_q, gain_k), own)
    own = [(field, 0) for field in (*own, *more)]
    for chunk in range(1, LAG):
        near[chunk] = (up(own[chunk][0]), 0)
    far, next_behind, third_behind = {}, {}, {}

    def climb(steps, after=()):
        ins, outs, jobs = {}, {}, []

        def use(place, chunk):
            field, at = place
            key = next((key for key, value in ins.items() if value is field), f"in{len(ins)}")
            ins[key] = field
            return key, slice(at, at + width[chunk])

        def exchange(to, chunk, first, second, halves=1):
            part = width[chunk] // halves
            for half in range(halves):
                pick = [(key, slice(at.start + half * part, at.start + (half + 1) * part)) for key, at in (use(first[chunk], chunk), use(second[chunk], chunk))]
                jobs.append((f"{to}{half}", 0, *pick))
                outs[f"{to}{half}"] = shape(rows, part)

        for step in steps:
            rise = 0
            if step + LAG < amount:
                jobs.append((f"rise{step}", rise, use(own[step + LAG], step + LAG), None))
                rise += width[step + LAG]
            if step < amount:
                jobs.append((f"rise{step}", rise, use(near[step], step), None))
                outs[f"rise{step}"] = shape(rows, rise + width[step])
                exchange("next", step, own, near)
            if step >= LAG:
                exchange("third", step - LAG, near, far, 2)

        def body(*refs):
            ref = dict(zip(list(ins) + list(outs), refs))
            for to, at, (key, here), other in jobs:
                value = ref[key][:, here]
                if other is not None:
                    value = jnp.where(core_index() == 0, value, ref[other[0]][:, other[1]])
                ref[to][:, at : at + value.shape[1]] = value

        made = dict(zip(outs, call(body, "climb", ins, outs, after, cost=10**9 * steps[0])))
        for step in steps:
            if step < amount:
                arrived = up(made[f"rise{step}"])
                ahead = 0
                if step + LAG < amount:
                    near[step + LAG] = (arrived, 0)
                    ahead = width[step + LAG]
                far[step] = (arrived, ahead)
                next_behind[step] = (swap(made["next0"]), 0)
            if step >= LAG:
                third_behind[step - LAG] = [swap(made["third0"]), swap(made["third1"])]
        return [next(iter(made.values()))]

    parts, sunk = [], {}

    def sink(step, after=()):
        fresh, older = step < amount, step >= LAG
        mine, below = width[step], width[step - LAG] if older else 0
        ins = {}
        if fresh:
            ins.update(far=parts[step]["far"], third_k=parts[step]["third_k"], third_v=parts[step]["third_v"])
        if older:
            chunk = step - LAG
            ins.update(near=parts[chunk]["near"], arrived=sunk[chunk])
            ins.update(old_k=parts[chunk]["third_k"], old_v=parts[chunk]["third_v"], next_old=parts[chunk]["next"])

        def body(*refs):
            ref = dict(zip(list(ins) + ["out"], refs))
            first = core_index() == 0
            if fresh:
                for half, extra in ((slice(0, mine // 2), ref["third_k"]), (slice(mine // 2, mine), ref["third_v"])):
                    extra = jnp.where(first, 0.0, extra[...].astype(F32))
                    ref["out"][:, half] = (ref["far"][:, half] + extra).astype(BF16)
            if older:
                for half, extra in ((slice(0, below // 2), ref["old_k"]), (slice(below // 2, below), ref["old_v"])):
                    extra = jnp.where(first, extra[...], ref["next_old"][:, half]).astype(F32)
                    total = ref["near"][:, half] + extra + ref["arrived"][:, half].astype(F32)
                    ref["out"][:, mine + half.start : mine + half.stop] = total.astype(BF16)

        (total,) = call(body, "sink", ins, dict(out=shape(rows, mine + below)), after)
        sunk[step] = down(total)
        return total

    made, gains, last, token = [], [], [], []
    order = []
    for step in range(LAG):
        order = climb([step], order)
    for chunk, (first, count) in enumerate(CHUNKS):
        order = climb([chunk + LAG], order + token)
        held = (own, next_behind, near, far)
        wide = shape(rows, GROUPS * count * HEAD_DIM)
        whole, low, half = shape(rows, width[chunk], F32), shape(rows, width[chunk]), shape(rows, width[chunk] // 2)
        result = call(
            functools.partial(attend, first, count, *(place[chunk][1] for place in held)),
            "attend",
            dict(
                segments=segments, queries=queries, out_grad=out_grad, own=own[chunk][0],
                **{f"behind{i}": place[chunk][0] for i, place in enumerate(held[1:])},
                third_k=third_behind[chunk][0], third_v=third_behind[chunk][1], gain_q=gain_q, gain_k=gain_k,
            ),
            dict(
                attended=wide, query_grad=wide, own=whole, near=whole, far=whole,
                third_k=half, third_v=half, next=low,
                gains=shape(2, HEAD_DIM, F32),
            ),
            last,
        )
        made.append(result[:2])
        gains.append(result[8])
        token = [result[8]]
        parts.append(dict(zip(("own", "near", "far"), result[2:5])))
        parts[-1].update(third_k=swap(result[5]), third_v=swap(result[6]), next=swap(result[7]))
        if chunk == amount - 1:
            (total,) = call(add, "add", dict(enumerate(gains)), dict(o=shape(2, HEAD_DIM, F32)))
            total = total_over(total, "ctx", 1, 2, 2)
            last = [*last, total]
        last = [sink(chunk, last)]

    first_sink = last
    for step in range(amount, amount + LAG):
        hold = call(add, "hold", dict(total=total), dict(o=shape(2, HEAD_DIM, F32)), [sunk[step - LAG]], cost=COSTS[5])
        last = [sink(step, [*last, *(hold if step == amount else [])])]

    factor = (lax.axis_size("dp") * queries.shape[0] * lax.axis_size("ctx") * rows) ** (-0.5)
    row = shape(1, HEAD_DIM, F32)
    chips = lax.axis_size("ctx") // 2
    (total,) = call(add, "add", dict(total=total), dict(o=shape(2, HEAD_DIM, F32)), first_sink)
    while chips > 4:
        total = total_over(total, "ctx", chips, 2 * chips, 2)
        chips //= 2
    total = total_over(total, "ctx", 2, 2 * chips, 4, COSTS[0], [sunk[amount - 1]])
    half = lax.axis_size("dp") // 2
    total = total_over(total, "dp", 1, half, 2, COSTS[1])
    others = [move(total, "dp", lambda i: i ^ half)] if half else []
    query_gains, key_gains = call(
        functools.partial(scale, factor),
        "scale",
        dict(enumerate([total, *others])),
        dict(a=row, b=row),
        cost=COSTS[2],
    )
    attended, query_grad = call(
        assemble,
        "assemble",
        {(i, chunk): made[chunk][i] for i in range(2) for chunk in range(amount)},
        dict(a=jax.ShapeDtypeStruct(queries.shape, BF16), b=jax.ShapeDtypeStruct(queries.shape, BF16)),
        last,
    )
    before = [pltpu.with_memory_space_constraint(field, pltpu.HBM) for field in (attended, query_gains)]
    key_outputs = []
    for chunk, (first, count) in enumerate(CHUNKS):
        narrow = columns(rows, count * HEAD_DIM, first * HEAD_DIM)
        key_outputs = call(
            functools.partial(finish, count, width[chunk + LAG]),
            "finish",
            dict(
                keys=keys, gain=gain_k, own=parts[chunk]["own"], next=parts[chunk]["next"], arrived=sunk[chunk + LAG]
            ),
            dict(
                key_grad=jax.ShapeDtypeStruct(keys.shape, BF16), value_grad=jax.ShapeDtypeStruct(keys.shape, BF16)
            ),
            [*key_outputs, *(before if chunk == amount - 1 else [])],
            cost=COSTS[3 + chunk],
            grid=(1,),
            in_specs=dict(keys=narrow),
            out_specs=dict(key_grad=narrow, value_grad=narrow),
            input_output_aliases={5 + i: i for i in range(len(key_outputs))},
        )
    return attended, query_grad, *key_outputs, query_gains[0], key_gains[0]


def solution(mesh):
    block = P("dp", "ctx", None)
    return jax.shard_map(
        shards,
        mesh=mesh,
        in_specs=(P("dp", None), block, block, block, P(), P(), block),
        out_specs=(block, block, block, block, P(), P()),
        check_vma=False,
    )
```

```python
import functools

import jax
import jax.numpy as jnp
from jax import lax
from jax.experimental import pallas as pl
from jax.experimental.pallas import tpu as pltpu
from jax.sharding import PartitionSpec as P

HEADS = 8
KV_HEADS = 4
HEAD_DIM = 256
WINDOW = 512
GREACH = 4
GROUPS = HEADS // KV_HEADS
EPSILON = 1e-06
BF16 = jnp.bfloat16
F32 = jnp.float32
CHUNKS = ((0, 2), (2, 2))
LAG = 2

PIECES = 4

COSTS = 2**32, 0, 0, 2**31, 2**32, 2**31

VMEM = pl.BlockSpec(memory_space=pltpu.VMEM)
ANY = pl.BlockSpec(memory_space=pl.ANY)


def call(body, name, ins, outs, after=(), cost=0, in_specs=None, out_specs=None, **more):
    names = list(ins)

    def kernel(*refs):
        used = len(names) + len(after)
        body(*refs[: len(names)], *refs[used:])

    specs = [(in_specs or {}).get(key, VMEM) for key in names] + [ANY] * len(after)
    return pl.pallas_call(
        kernel,
        out_shape=list(outs.values()),
        in_specs=specs,
        out_specs=[(out_specs or {}).get(key, VMEM) for key in outs],
        compiler_params=pltpu.CompilerParams(vmem_limit_bytes=40 * 2**20),
        cost_estimate=pl.CostEstimate(flops=cost, bytes_accessed=1, transcendentals=0),
        name=name,
        **more,
    )(*ins.values(), *after)


def shape(rows, cols, dtype=BF16):
    return jax.ShapeDtypeStruct((rows, cols), dtype)


def core_index():
    return lax.axis_index("ctx") % 2


def payload(chunks, keys, values, *rest):
    extra = len(rest[:-1]) - len(chunks)
    small, outs, kept, sems = rest[: extra // 2], rest[extra // 2 : -1 - extra // 2], rest[-1 - extra // 2 : -1], rest[-1]
    copies = [pltpu.make_async_copy(old, new, sems.at[i]) for i, (old, new) in enumerate(zip(small, kept))]
    for (first, count), out in zip(chunks, outs):
        here = pl.ds(first * HEAD_DIM, count * HEAD_DIM)
        for side, field in enumerate((keys, values)):
            to = pl.ds(side * count * HEAD_DIM, count * HEAD_DIM)
            for piece in range(PIECES):
                share = field.shape[1] // PIECES
                rows = pl.ds(piece * share, share)
                sem = sems.at[len(copies)]
                copies.append(pltpu.make_async_copy(field.at[0, rows, here], out.at[rows, to], sem))
    for copy in copies:
        copy.start()
    for copy in copies:
        copy.wait()


def normalize(field):
    inverse = lax.rsqrt(jnp.mean(field * field, -1, keepdims=True) + EPSILON)
    return field * inverse, inverse


def dot(left, right, over):
    return lax.dot_general(left, right, ((over[:1], over[1:]), ((), ())), preferred_element_type=F32)


def attend(
    first, count, at_own, at_x, at_near, at_far, segments, queries, out_grad, own, across_x, arrived_near, arrived_far,
    across_k, across_v,    query_gain, key_gain, *rest,
):
    attended, query_grad, part_own, part_near, part_far, third_k, third_v, part_next, gains = rest
    position = lax.axis_index("ctx")
    rows = queries.shape[1]
    band = (GREACH + 1) * rows
    gain_q = query_gain[...]
    gain_k = key_gain[...]

    def segment(distance):
        block = position - distance
        first = pl.multiple_of(jnp.maximum(block, 0) * rows, rows)
        return jnp.where(block >= 0, segments[:, pl.ds(first, rows)], -1)

    key_seg = jnp.concatenate([segment(distance) for distance in range(GREACH, -1, -1)], 1)
    query_seg = jnp.broadcast_to(segment(0), (rows, rows)).T[:, :1]
    back = (
        lax.broadcasted_iota(jnp.int32, (rows, band), 0)
        - lax.broadcasted_iota(jnp.int32, (rows, band), 1)
        + GREACH * rows
    )
    live = (query_seg == key_seg) & (back >= 0) & (back < WINDOW)
    live = jnp.concatenate([live] * GROUPS, 0)

    query_gains = jnp.zeros((1, HEAD_DIM), F32)
    key_gains = jnp.zeros((1, HEAD_DIM), F32)

    def band_of(index):
        third = (across_k, 0) if index < count else (across_v, -count * HEAD_DIM)
        blocks = ((arrived_far, at_far), third, (arrived_near, at_near), (across_x, at_x), (own, at_own))
        return jnp.concatenate(
            [field[:, at + index * HEAD_DIM : at + (index + 1) * HEAD_DIM] for field, at in blocks], 0
        )

    for head in range(count):
        at_k = slice(head * HEAD_DIM, (head + 1) * HEAD_DIM)
        at_v = slice((count + head) * HEAD_DIM, (count + head + 1) * HEAD_DIM)
        at_q = [slice((head * GROUPS + g) * HEAD_DIM, (head * GROUPS + g + 1) * HEAD_DIM) for g in range(GROUPS)]
        from_q = [slice(at.start + first * GROUPS * HEAD_DIM, at.stop + first * GROUPS * HEAD_DIM) for at in at_q]
        band_v = band_of(count + head)
        k_normed, _ = normalize(band_of(head).astype(F32))
        k_rounded = (k_normed * gain_k).astype(BF16)
        q_normed, q_inverse = normalize(jnp.concatenate([queries[0, :, at] for at in from_q], 0).astype(F32))
        q_scaled = (q_normed * gain_q * HEAD_DIM ** (-0.5)).astype(BF16)
        grads = jnp.concatenate([out_grad[0, :, at] for at in from_q], 0)

        scores = dot(q_scaled, k_rounded, (1, 1))
        weights = jnp.where(live, jnp.exp(scores), 0.0)
        probs = weights * (1.0 / jnp.sum(weights, -1, keepdims=True))
        probs_low = probs.astype(BF16)
        dprob = dot(grads, band_v, (1, 1))
        centre = jnp.sum(probs * dprob, -1, keepdims=True)
        dscore = (probs * (dprob - centre)).astype(BF16)
        key_parts = dot(dscore, q_scaled, (0, 0))
        value_parts = dot(probs_low, grads, (0, 0))
        for at, parts, third in ((at_k, key_parts, third_k), (at_v, value_parts, third_v)):
            part_far[:, at] = parts[:rows]
            third[:, at_k] = parts[rows : 2 * rows].astype(BF16)
            part_near[:, at] = parts[2 * rows : 3 * rows]
            part_next[:, at] = parts[3 * rows : 4 * rows].astype(BF16)
            part_own[:, at] = parts[4 * rows :]

        output = dot(probs_low, band_v, (1, 0)).astype(BF16)
        dq = dot(dscore, k_rounded, (1, 0)) * HEAD_DIM ** (-0.5)
        scaled = dq * gain_q
        grad = q_inverse * (scaled - q_normed * jnp.mean(scaled * q_normed, -1, keepdims=True))
        grad = grad.astype(BF16)
        for g, at in enumerate(at_q):
            attended[:, at] = output[g * rows : (g + 1) * rows]
            query_grad[:, at] = grad[g * rows : (g + 1) * rows]
        query_gains = query_gains + jnp.sum(dq * q_normed, 0, keepdims=True)
        key_gains = key_gains + jnp.sum(key_parts * k_normed, 0, keepdims=True)
    gains[0:1, :] = query_gains
    gains[1:2, :] = key_gains


def assemble(*refs):
    amount = len(CHUNKS)
    for index, out in enumerate(refs[-2:]):
        for (first, count), part in zip(CHUNKS, refs[index * amount : (index + 1) * amount]):
            out[0, :, first * GROUPS * HEAD_DIM : (first + count) * GROUPS * HEAD_DIM] = part[...]


def add(*refs):
    refs[-1][...] = sum(ref[...] for ref in refs[1:-1]) + refs[0][...]


def finish(count, at, factor, keys, key_gain, part_own, swapped, arrived, *rest):
    if factor is None:
        key_grad, value_grad = rest
    else:
        gains, (key_grad, value_grad, query_gains, key_gains) = rest[:-4], rest[-4:]
        total = sum(ref[...] for ref in gains[1:]) + gains[0][...]
        query_gains[...] = total[0:1, :] * factor
        key_gains[...] = total[1:2, :] * factor
    rows = part_own.shape[0]
    gain_k = key_gain[...]
    for head in range(count):

        def total(index):
            here = slice(index * HEAD_DIM, (index + 1) * HEAD_DIM)
            there = slice(at + index * HEAD_DIM, at + (index + 1) * HEAD_DIM)
            extra = jnp.where(core_index() == 0, swapped[:, here].astype(F32), 0.0)
            return part_own[:, here] + extra + arrived[:, there].astype(F32)

        out = slice(head * HEAD_DIM, (head + 1) * HEAD_DIM)
        normed, inverse = normalize(keys[0, :, out].astype(F32))
        scaled = total(head) * gain_k
        grad = inverse * (scaled - normed * jnp.mean(scaled * normed, -1, keepdims=True))
        key_grad[0, :, out] = grad.astype(BF16)
        value_grad[0, :, out] = total(count + head).astype(BF16)


def columns(rows, width, first):
    return pl.BlockSpec((1, rows, width), lambda i: (0, 0, first // width))


def move(field, axis, target):
    size = lax.axis_size(axis)
    return lax.ppermute(field, axis, [(i, target(i)) for i in range(size) if 0 <= target(i) < size])


def up(field):
    return move(field, "ctx", lambda i: i + 2)


def down(field):
    return move(field, "ctx", lambda i: i - 2)


def swap(field):
    return move(field, "ctx", lambda i: i ^ 1)


def total_over(field, axis, unit, end, most, cost=0, after=()):
    end = min(end, lax.axis_size(axis))
    while unit < end:
        group = min(most, end // unit)
        others = [move(field, axis, lambda i: i ^ (by * unit)) for by in range(1, group)]
        (field,) = call(add, "add", dict(enumerate([field, *others])), dict(o=shape(*field.shape, F32)), after, cost=cost)
        unit *= group
    return field


def shards(segment_ids, queries, keys, values, query_gain, key_gain, out_grad):
    rows = queries.shape[1]
    gain_q = query_gain.reshape(1, HEAD_DIM)
    gain_k = key_gain.reshape(1, HEAD_DIM)
    amount = len(CHUNKS)
    width = [2 * count * HEAD_DIM for _, count in CHUNKS] + [0] * LAG
    def gather(chunks, small=(), after=()):
        sources = [pltpu.with_memory_space_constraint(field, pltpu.HBM) for field in (keys, values, *small)]
        made = call(
            functools.partial(payload, chunks),
            "payload",
            dict(enumerate(sources)),
            dict(
                enumerate(
                    [shape(rows, 2 * count * HEAD_DIM) for _, count in chunks]
                    + [jax.ShapeDtypeStruct(field.shape, field.dtype) for field in small]
                )
            ),
            after,
            in_specs=dict.fromkeys(range(len(sources)), ANY),
            scratch_shapes=[pltpu.SemaphoreType.DMA((2 * len(chunks) * PIECES + len(small),))],
        )
        return made[: len(chunks)], made[len(chunks) :]

    own, _ = gather(CHUNKS[:1])
    near = {0: (up(own[0]), 0)}
    more, (segments, gain_q, gain_k) = gather(CHUNKS[1:], (segment_ids, gain_q, gain_k), own)
    own = [(field, 0) for field in (*own, *more)]
    for chunk in range(1, LAG):
        near[chunk] = (up(own[chunk][0]), 0)
    far, next_behind, third_behind = {}, {}, {}

    def climb(steps, after=()):
        ins, outs, jobs = {}, {}, []

        def use(place, chunk):
            field, at = place
            key = next((key for key, value in ins.items() if value is field), f"in{len(ins)}")
            ins[key] = field
            return key, slice(at, at + width[chunk])

        def exchange(to, chunk, first, second, halves=1):
            part = width[chunk] // halves
            for half in range(halves):
                pick = [(key, slice(at.start + half * part, at.start + (half + 1) * part)) for key, at in (use(first[chunk], chunk), use(second[chunk], chunk))]
                jobs.append((f"{to}{half}", 0, *pick))
                outs[f"{to}{half}"] = shape(rows, part)

        for step in steps:
            rise = 0
            if step + LAG < amount:
                jobs.append((f"rise{step}", rise, use(own[step + LAG], step + LAG), None))
                rise += width[step + LAG]
            if step < amount:
                jobs.append((f"rise{step}", rise, use(near[step], step), None))
                outs[f"rise{step}"] = shape(rows, rise + width[step])
                exchange("next", step, own, near)
            if step >= LAG:
                exchange("third", step - LAG, near, far, 2)

        def body(*refs):
            ref = dict(zip(list(ins) + list(outs), refs))
            for to, at, (key, here), other in jobs:
                value = ref[key][:, here]
                if other is not None:
                    value = jnp.where(core_index() == 0, value, ref[other[0]][:, other[1]])
                ref[to][:, at : at + value.shape[1]] = value

        made = dict(zip(outs, call(body, "climb", ins, outs, after, cost=10**9 * steps[0])))
        for step in steps:
            if step < amount:
                arrived = up(made[f"rise{step}"])
                ahead = 0
                if step + LAG < amount:
                    near[step + LAG] = (arrived, 0)
                    ahead = width[step + LAG]
                far[step] = (arrived, ahead)
                next_behind[step] = (swap(made["next0"]), 0)
            if step >= LAG:
                third_behind[step - LAG] = [swap(made["third0"]), swap(made["third1"])]
        return [next(iter(made.values()))]

    parts, sunk = [], {}

    def sink(step, after=()):
        fresh, older = step < amount, step >= LAG
        mine, below = width[step], width[step - LAG] if older else 0
        ins = {}
        if fresh:
            ins.update(far=parts[step]["far"], third_k=parts[step]["third_k"], third_v=parts[step]["third_v"])
        if older:
            chunk = step - LAG
            ins.update(near=parts[chunk]["near"], arrived=sunk[chunk])
            ins.update(old_k=parts[chunk]["third_k"], old_v=parts[chunk]["third_v"], next_old=parts[chunk]["next"])

        def body(*refs):
            ref = dict(zip(list(ins) + ["out"], refs))
            first = core_index() == 0
            if fresh:
                for half, extra in ((slice(0, mine // 2), ref["third_k"]), (slice(mine // 2, mine), ref["third_v"])):
                    extra = jnp.where(first, 0.0, extra[...].astype(F32))
                    ref["out"][:, half] = (ref["far"][:, half] + extra).astype(BF16)
            if older:
                for half, extra in ((slice(0, below // 2), ref["old_k"]), (slice(below // 2, below), ref["old_v"])):
                    extra = jnp.where(first, extra[...], ref["next_old"][:, half]).astype(F32)
                    total = ref["near"][:, half] + extra + ref["arrived"][:, half].astype(F32)
                    ref["out"][:, mine + half.start : mine + half.stop] = total.astype(BF16)

        (total,) = call(body, "sink", ins, dict(out=shape(rows, mine + below)), after)
        sunk[step] = down(total)
        return total

    made, gains, last, token = [], [], [], []
    order = []
    for step in range(LAG):
        order = climb([step], order)
    for chunk, (first, count) in enumerate(CHUNKS):
        order = climb([chunk + LAG], order + token)
        held = (own, next_behind, near, far)
        wide = shape(rows, GROUPS * count * HEAD_DIM)
        whole, low, half = shape(rows, width[chunk], F32), shape(rows, width[chunk]), shape(rows, width[chunk] // 2)
        result = call(
            functools.partial(attend, first, count, *(place[chunk][1] for place in held)),
            "attend",
            dict(
                segments=segments, queries=queries, out_grad=out_grad, own=own[chunk][0],
                **{f"behind{i}": place[chunk][0] for i, place in enumerate(held[1:])},
                third_k=third_behind[chunk][0], third_v=third_behind[chunk][1], gain_q=gain_q, gain_k=gain_k,
            ),
            dict(
                attended=wide, query_grad=wide, own=whole, near=whole, far=whole,
                third_k=half, third_v=half, next=low,
                gains=shape(2, HEAD_DIM, F32),
            ),
            last,
        )
        made.append(result[:2])
        gains.append(result[8])
        token = [result[8]]
        parts.append(dict(zip(("own", "near", "far"), result[2:5])))
        parts[-1].update(third_k=swap(result[5]), third_v=swap(result[6]), next=swap(result[7]))
        if chunk == amount - 1:
            (total,) = call(add, "add", dict(enumerate(gains)), dict(o=shape(2, HEAD_DIM, F32)))
            total = total_over(total, "ctx", 1, 2, 2)
            last = [*last, total]
        last = [sink(chunk, last)]

    first_sink = last
    for step in range(amount, amount + LAG):
        hold = call(add, "hold", dict(total=total), dict(o=shape(2, HEAD_DIM, F32)), [sunk[step - LAG]], cost=COSTS[5])
        last = [sink(step, [*last, *(hold if step == amount else [])])]

    attended, query_grad = call(
        assemble,
        "assemble",
        {(i, chunk): made[chunk][i] for i in range(2) for chunk in range(amount)},
        dict(a=jax.ShapeDtypeStruct(queries.shape, BF16), b=jax.ShapeDtypeStruct(queries.shape, BF16)),
        last,
    )

    factor = (lax.axis_size("dp") * queries.shape[0] * lax.axis_size("ctx") * rows) ** (-0.5)
    row = shape(1, HEAD_DIM, F32)
    chips = lax.axis_size("ctx") // 2
    (total,) = call(add, "add", dict(total=total), dict(o=shape(2, HEAD_DIM, F32)), first_sink)
    while chips > 4:
        total = total_over(total, "ctx", chips, 2 * chips, 2)
        chips //= 2
    total = total_over(total, "ctx", 2, 2 * chips, 4, COSTS[0], [sunk[amount - 1]])
    half = lax.axis_size("dp") // 2
    total = total_over(total, "dp", 1, half, 2, COSTS[1], [pltpu.with_memory_space_constraint(attended, pltpu.HBM)])
    others = [move(total, "dp", lambda i: i ^ half)] if half else []
    key_outputs = []
    for chunk, (first, count) in enumerate(CHUNKS):
        narrow = columns(rows, count * HEAD_DIM, first * HEAD_DIM)
        ins = dict(
            keys=keys, gain=gain_k, own=parts[chunk]["own"], next=parts[chunk]["next"], arrived=sunk[chunk + LAG]
        )
        outs = dict(
            key_grad=jax.ShapeDtypeStruct(keys.shape, BF16), value_grad=jax.ShapeDtypeStruct(keys.shape, BF16)
        )
        final = chunk == amount - 1
        if final:
            ins.update(enumerate([total, *others]))
            outs.update(query_gains=row, key_gains=row)
        key_outputs = call(
            functools.partial(finish, count, width[chunk + LAG], factor if final else None),
            "finish",
            ins,
            outs,
            key_outputs,
            cost=COSTS[3 + chunk],
            grid=(1,),
            in_specs=dict(keys=narrow),
            out_specs=dict(key_grad=narrow, value_grad=narrow),
            input_output_aliases={len(ins) + i: i for i in range(len(key_outputs))},
        )
    key_grad, value_grad, query_gains, key_gains = key_outputs
    return attended, query_grad, key_grad, value_grad, query_gains[0], key_gains[0]


def solution(mesh):
    block = P("dp", "ctx", None)
    return jax.shard_map(
        shards,
        mesh=mesh,
        in_specs=(P("dp", None), block, block, block, P(), P(), block),
        out_specs=(block, block, block, block, P(), P()),
        check_vma=False,
    )
```

```python
import functools

import jax
import jax.numpy as jnp
from jax import lax
from jax.experimental import pallas as pl
from jax.experimental.pallas import tpu as pltpu
from jax.sharding import PartitionSpec as P

HEADS = 8
KV_HEADS = 4
HEAD_DIM = 256
WINDOW = 512
GREACH = 4
GROUPS = HEADS // KV_HEADS
EPSILON = 1e-06
BF16 = jnp.bfloat16
F32 = jnp.float32
CHUNKS = ((0, 2), (2, 2))
LAG = 2

PIECES = 4

COSTS = 2**32, 0, 0, 2**31, 2**32, 2**31

VMEM = pl.BlockSpec(memory_space=pltpu.VMEM)
ANY = pl.BlockSpec(memory_space=pl.ANY)


def call(body, name, ins, outs, after=(), cost=0, in_specs=None, out_specs=None, **more):
    names = list(ins)

    def kernel(*refs):
        used = len(names) + len(after)
        body(*refs[: len(names)], *refs[used:])

    specs = [(in_specs or {}).get(key, VMEM) for key in names] + [ANY] * len(after)
    return pl.pallas_call(
        kernel,
        out_shape=list(outs.values()),
        in_specs=specs,
        out_specs=[(out_specs or {}).get(key, VMEM) for key in outs],
        compiler_params=pltpu.CompilerParams(vmem_limit_bytes=40 * 2**20),
        cost_estimate=pl.CostEstimate(flops=cost, bytes_accessed=1, transcendentals=0),
        name=name,
        **more,
    )(*ins.values(), *after)


def shape(rows, cols, dtype=BF16):
    return jax.ShapeDtypeStruct((rows, cols), dtype)


def core_index():
    return lax.axis_index("ctx") % 2


def payload(chunks, keys, values, *rest):
    extra = len(rest[:-1]) - len(chunks)
    small, outs, kept, sems = rest[: extra // 2], rest[extra // 2 : -1 - extra // 2], rest[-1 - extra // 2 : -1], rest[-1]
    copies = [pltpu.make_async_copy(old, new, sems.at[i]) for i, (old, new) in enumerate(zip(small, kept))]
    for (first, count), out in zip(chunks, outs):
        here = pl.ds(first * HEAD_DIM, count * HEAD_DIM)
        for side, field in enumerate((keys, values)):
            to = pl.ds(side * count * HEAD_DIM, count * HEAD_DIM)
            for piece in range(PIECES):
                share = field.shape[1] // PIECES
                rows = pl.ds(piece * share, share)
                sem = sems.at[len(copies)]
                copies.append(pltpu.make_async_copy(field.at[0, rows, here], out.at[rows, to], sem))
    for copy in copies:
        copy.start()
    for copy in copies:
        copy.wait()


def normalize(field):
    inverse = lax.rsqrt(jnp.mean(field * field, -1, keepdims=True) + EPSILON)
    return field * inverse, inverse


def dot(left, right, over):
    return lax.dot_general(left, right, ((over[:1], over[1:]), ((), ())), preferred_element_type=F32)


def attend(
    first, count, at_own, at_x, at_near, at_far, segments, queries, out_grad, own, across_x, arrived_near, arrived_far,
    across_k, across_v,    query_gain, key_gain, *rest,
):
    attended, query_grad, part_own, part_near, part_far, third_k, third_v, part_next, gains = rest
    position = lax.axis_index("ctx")
    rows = queries.shape[1]
    band = (GREACH + 1) * rows
    gain_q = query_gain[...]
    gain_k = key_gain[...]

    def segment(distance):
        block = position - distance
        first = pl.multiple_of(jnp.maximum(block, 0) * rows, rows)
        return jnp.where(block >= 0, segments[:, pl.ds(first, rows)], -1)

    key_seg = jnp.concatenate([segment(distance) for distance in range(GREACH, -1, -1)], 1)
    query_seg = jnp.broadcast_to(segment(0), (rows, rows)).T[:, :1]
    back = (
        lax.broadcasted_iota(jnp.int32, (rows, band), 0)
        - lax.broadcasted_iota(jnp.int32, (rows, band), 1)
        + GREACH * rows
    )
    live = (query_seg == key_seg) & (back >= 0) & (back < WINDOW)
    live = jnp.concatenate([live] * GROUPS, 0)

    def band_of(index):
        third = (across_k, 0) if index < count else (across_v, -count * HEAD_DIM)
        blocks = ((arrived_far, at_far), third, (arrived_near, at_near), (across_x, at_x), (own, at_own))
        return jnp.concatenate(
            [field[:, at + index * HEAD_DIM : at + (index + 1) * HEAD_DIM] for field, at in blocks], 0
        )

    def columns_of(index):
        return slice(index * HEAD_DIM, (index + 1) * HEAD_DIM)

    def query_rows(field, head):
        start = (first + head) * GROUPS
        return jnp.concatenate([field[0, :, columns_of(start + g)] for g in range(GROUPS)], 0)

    heads = range(count)
    grads = [query_rows(out_grad, head) for head in heads]
    band_v = [band_of(count + head) for head in heads]
    q_normed, q_inverse, q_scaled, k_normed, k_rounded, scores = [], [], [], [], [], []
    for head in heads:
        normed, inverse = normalize(query_rows(queries, head).astype(F32))
        q_normed.append(normed)
        q_inverse.append(inverse)
        q_scaled.append((normed * gain_q * HEAD_DIM ** (-0.5)).astype(BF16))
        k_normed.append(normalize(band_of(head).astype(F32))[0])
        k_rounded.append((k_normed[head] * gain_k).astype(BF16))
        scores.append(dot(q_scaled[head], k_rounded[head], (1, 1)))
    dprob = [dot(grads[head], band_v[head], (1, 1)) for head in heads]
    probs_low, dscore = [], []
    for head in heads:
        weights = jnp.where(live, jnp.exp(scores[head]), 0.0)
        probs = weights * (1.0 / jnp.sum(weights, -1, keepdims=True))
        probs_low.append(probs.astype(BF16))
        centre = jnp.sum(probs * dprob[head], -1, keepdims=True)
        dscore.append((probs * (dprob[head] - centre)).astype(BF16))

    def give(parts, at):
        part_far[:, at] = parts[:rows]
        part_near[:, at] = parts[2 * rows : 3 * rows]
        part_next[:, at] = parts[3 * rows : 4 * rows].astype(BF16)
        part_own[:, at] = parts[4 * rows :]
        return parts[rows : 2 * rows].astype(BF16)

    for head in heads:
        third_v[:, columns_of(head)] = give(dot(probs_low[head], grads[head], (0, 0)), columns_of(count + head))
        output = dot(probs_low[head], band_v[head], (1, 0)).astype(BF16)
        for g in range(GROUPS):
            attended[:, columns_of(head * GROUPS + g)] = output[g * rows : (g + 1) * rows]
    query_gains = jnp.zeros((1, HEAD_DIM), F32)
    key_gains = jnp.zeros((1, HEAD_DIM), F32)
    for head in heads:
        key_parts = dot(dscore[head], q_scaled[head], (0, 0))
        third_k[:, columns_of(head)] = give(key_parts, columns_of(head))
        key_gains = key_gains + jnp.sum(key_parts * k_normed[head], 0, keepdims=True)
        dq = dot(dscore[head], k_rounded[head], (1, 0)) * HEAD_DIM ** (-0.5)
        scaled = dq * gain_q
        grad = q_inverse[head] * (scaled - q_normed[head] * jnp.mean(scaled * q_normed[head], -1, keepdims=True))
        for g in range(GROUPS):
            query_grad[:, columns_of(head * GROUPS + g)] = grad[g * rows : (g + 1) * rows].astype(BF16)
        query_gains = query_gains + jnp.sum(dq * q_normed[head], 0, keepdims=True)
    gains[0:1, :] = query_gains
    gains[1:2, :] = key_gains


def assemble(*refs):
    amount = len(CHUNKS)
    for index, out in enumerate(refs[-2:]):
        for (first, count), part in zip(CHUNKS, refs[index * amount : (index + 1) * amount]):
            out[0, :, first * GROUPS * HEAD_DIM : (first + count) * GROUPS * HEAD_DIM] = part[...]


def add(*refs):
    refs[-1][...] = sum(ref[...] for ref in refs[1:-1]) + refs[0][...]


def finish(count, at, factor, keys, key_gain, part_own, swapped, arrived, *rest):
    if factor is None:
        key_grad, value_grad = rest
    else:
        gains, (key_grad, value_grad, query_gains, key_gains) = rest[:-4], rest[-4:]
        total = sum(ref[...] for ref in gains[1:]) + gains[0][...]
        query_gains[...] = total[0:1, :] * factor
        key_gains[...] = total[1:2, :] * factor
    rows = part_own.shape[0]
    gain_k = key_gain[...]
    for head in range(count):

        def total(index):
            here = slice(index * HEAD_DIM, (index + 1) * HEAD_DIM)
            there = slice(at + index * HEAD_DIM, at + (index + 1) * HEAD_DIM)
            extra = jnp.where(core_index() == 0, swapped[:, here].astype(F32), 0.0)
            return part_own[:, here] + extra + arrived[:, there].astype(F32)

        out = slice(head * HEAD_DIM, (head + 1) * HEAD_DIM)
        normed, inverse = normalize(keys[0, :, out].astype(F32))
        scaled = total(head) * gain_k
        grad = inverse * (scaled - normed * jnp.mean(scaled * normed, -1, keepdims=True))
        key_grad[0, :, out] = grad.astype(BF16)
        value_grad[0, :, out] = total(count + head).astype(BF16)


def columns(rows, width, first):
    return pl.BlockSpec((1, rows, width), lambda i: (0, 0, first // width))


def move(field, axis, target):
    size = lax.axis_size(axis)
    return lax.ppermute(field, axis, [(i, target(i)) for i in range(size) if 0 <= target(i) < size])


def up(field):
    return move(field, "ctx", lambda i: i + 2)


def down(field):
    return move(field, "ctx", lambda i: i - 2)


def swap(field):
    return move(field, "ctx", lambda i: i ^ 1)


def total_over(field, axis, unit, end, most, cost=0, after=()):
    end = min(end, lax.axis_size(axis))
    while unit < end:
        group = min(most, end // unit)
        others = [move(field, axis, lambda i: i ^ (by * unit)) for by in range(1, group)]
        (field,) = call(add, "add", dict(enumerate([field, *others])), dict(o=shape(*field.shape, F32)), after, cost=cost)
        unit *= group
    return field


def shards(segment_ids, queries, keys, values, query_gain, key_gain, out_grad):
    rows = queries.shape[1]
    gain_q = query_gain.reshape(1, HEAD_DIM)
    gain_k = key_gain.reshape(1, HEAD_DIM)
    amount = len(CHUNKS)
    width = [2 * count * HEAD_DIM for _, count in CHUNKS] + [0] * LAG
    def gather(chunks, small=(), after=()):
        sources = [pltpu.with_memory_space_constraint(field, pltpu.HBM) for field in (keys, values, *small)]
        made = call(
            functools.partial(payload, chunks),
            "payload",
            dict(enumerate(sources)),
            dict(
                enumerate(
                    [shape(rows, 2 * count * HEAD_DIM) for _, count in chunks]
                    + [jax.ShapeDtypeStruct(field.shape, field.dtype) for field in small]
                )
            ),
            after,
            in_specs=dict.fromkeys(range(len(sources)), ANY),
            scratch_shapes=[pltpu.SemaphoreType.DMA((2 * len(chunks) * PIECES + len(small),))],
        )
        return made[: len(chunks)], made[len(chunks) :]

    own, _ = gather(CHUNKS[:1])
    near = {0: (up(own[0]), 0)}
    more, (segments, gain_q, gain_k) = gather(CHUNKS[1:], (segment_ids, gain_q, gain_k), own)
    own = [(field, 0) for field in (*own, *more)]
    for chunk in range(1, LAG):
        near[chunk] = (up(own[chunk][0]), 0)
    far, next_behind, third_behind = {}, {}, {}

    def climb(steps, after=()):
        ins, outs, jobs = {}, {}, []

        def use(place, chunk):
            field, at = place
            key = next((key for key, value in ins.items() if value is field), f"in{len(ins)}")
            ins[key] = field
            return key, slice(at, at + width[chunk])

        def exchange(to, chunk, first, second, halves=1):
            part = width[chunk] // halves
            for half in range(halves):
                pick = [(key, slice(at.start + half * part, at.start + (half + 1) * part)) for key, at in (use(first[chunk], chunk), use(second[chunk], chunk))]
                jobs.append((f"{to}{half}", 0, *pick))
                outs[f"{to}{half}"] = shape(rows, part)

        for step in steps:
            rise = 0
            if step + LAG < amount:
                jobs.append((f"rise{step}", rise, use(own[step + LAG], step + LAG), None))
                rise += width[step + LAG]
            if step < amount:
                jobs.append((f"rise{step}", rise, use(near[step], step), None))
                outs[f"rise{step}"] = shape(rows, rise + width[step])
                exchange("next", step, own, near)
            if step >= LAG:
                exchange("third", step - LAG, near, far, 2)

        def body(*refs):
            ref = dict(zip(list(ins) + list(outs), refs))
            for to, at, (key, here), other in jobs:
                value = ref[key][:, here]
                if other is not None:
                    value = jnp.where(core_index() == 0, value, ref[other[0]][:, other[1]])
                ref[to][:, at : at + value.shape[1]] = value

        made = dict(zip(outs, call(body, "climb", ins, outs, after, cost=10**9 * steps[0])))
        for step in steps:
            if step < amount:
                arrived = up(made[f"rise{step}"])
                ahead = 0
                if step + LAG < amount:
                    near[step + LAG] = (arrived, 0)
                    ahead = width[step + LAG]
                far[step] = (arrived, ahead)
                next_behind[step] = (swap(made["next0"]), 0)
            if step >= LAG:
                third_behind[step - LAG] = [swap(made["third0"]), swap(made["third1"])]
        return [next(iter(made.values()))]

    parts, sunk = [], {}

    def sink(step, after=()):
        fresh, older = step < amount, step >= LAG
        mine, below = width[step], width[step - LAG] if older else 0
        ins = {}
        if fresh:
            ins.update(far=parts[step]["far"], third_k=parts[step]["third_k"], third_v=parts[step]["third_v"])
        if older:
            chunk = step - LAG
            ins.update(near=parts[chunk]["near"], arrived=sunk[chunk])
            ins.update(old_k=parts[chunk]["third_k"], old_v=parts[chunk]["third_v"], next_old=parts[chunk]["next"])

        def body(*refs):
            ref = dict(zip(list(ins) + ["out"], refs))
            first = core_index() == 0
            if fresh:
                for half, extra in ((slice(0, mine // 2), ref["third_k"]), (slice(mine // 2, mine), ref["third_v"])):
                    extra = jnp.where(first, 0.0, extra[...].astype(F32))
                    ref["out"][:, half] = (ref["far"][:, half] + extra).astype(BF16)
            if older:
                for half, extra in ((slice(0, below // 2), ref["old_k"]), (slice(below // 2, below), ref["old_v"])):
                    extra = jnp.where(first, extra[...], ref["next_old"][:, half]).astype(F32)
                    total = ref["near"][:, half] + extra + ref["arrived"][:, half].astype(F32)
                    ref["out"][:, mine + half.start : mine + half.stop] = total.astype(BF16)

        (total,) = call(body, "sink", ins, dict(out=shape(rows, mine + below)), after)
        sunk[step] = down(total)
        return total

    made, gains, last, token = [], [], [], []
    order = []
    for step in range(LAG):
        order = climb([step], order)
    for chunk, (first, count) in enumerate(CHUNKS):
        order = climb([chunk + LAG], order + token)
        held = (own, next_behind, near, far)
        wide = shape(rows, GROUPS * count * HEAD_DIM)
        whole, low, half = shape(rows, width[chunk], F32), shape(rows, width[chunk]), shape(rows, width[chunk] // 2)
        result = call(
            functools.partial(attend, first, count, *(place[chunk][1] for place in held)),
            "attend",
            dict(
                segments=segments, queries=queries, out_grad=out_grad, own=own[chunk][0],
                **{f"behind{i}": place[chunk][0] for i, place in enumerate(held[1:])},
                third_k=third_behind[chunk][0], third_v=third_behind[chunk][1], gain_q=gain_q, gain_k=gain_k,
            ),
            dict(
                attended=wide, query_grad=wide, own=whole, near=whole, far=whole,
                third_k=half, third_v=half, next=low,
                gains=shape(2, HEAD_DIM, F32),
            ),
            last,
        )
        made.append(result[:2])
        gains.append(result[8])
        token = [result[8]]
        parts.append(dict(zip(("own", "near", "far"), result[2:5])))
        parts[-1].update(third_k=swap(result[5]), third_v=swap(result[6]), next=swap(result[7]))
        if chunk == amount - 1:
            (total,) = call(add, "add", dict(enumerate(gains)), dict(o=shape(2, HEAD_DIM, F32)))
            total = total_over(total, "ctx", 1, 2, 2)
            last = [*last, total]
        last = [sink(chunk, last)]

    first_sink = last
    for step in range(amount, amount + LAG):
        hold = call(add, "hold", dict(total=total), dict(o=shape(2, HEAD_DIM, F32)), [sunk[step - LAG]], cost=COSTS[5])
        last = [sink(step, [*last, *(hold if step == amount else [])])]

    attended, query_grad = call(
        assemble,
        "assemble",
        {(i, chunk): made[chunk][i] for i in range(2) for chunk in range(amount)},
        dict(a=jax.ShapeDtypeStruct(queries.shape, BF16), b=jax.ShapeDtypeStruct(queries.shape, BF16)),
        last,
    )

    factor = (lax.axis_size("dp") * queries.shape[0] * lax.axis_size("ctx") * rows) ** (-0.5)
    row = shape(1, HEAD_DIM, F32)
    chips = lax.axis_size("ctx") // 2
    (total,) = call(add, "add", dict(total=total), dict(o=shape(2, HEAD_DIM, F32)), first_sink)
    while chips > 4:
        total = total_over(total, "ctx", chips, 2 * chips, 2)
        chips //= 2
    total = total_over(total, "ctx", 2, 2 * chips, 4, COSTS[0], [sunk[amount - 1]])
    half = lax.axis_size("dp") // 2
    total = total_over(total, "dp", 1, half, 2, COSTS[1], [pltpu.with_memory_space_constraint(attended, pltpu.HBM)])
    others = [move(total, "dp", lambda i: i ^ half)] if half else []
    key_outputs = []
    for chunk, (first, count) in enumerate(CHUNKS):
        narrow = columns(rows, count * HEAD_DIM, first * HEAD_DIM)
        ins = dict(
            keys=keys, gain=gain_k, own=parts[chunk]["own"], next=parts[chunk]["next"], arrived=sunk[chunk + LAG]
        )
        outs = dict(
            key_grad=jax.ShapeDtypeStruct(keys.shape, BF16), value_grad=jax.ShapeDtypeStruct(keys.shape, BF16)
        )
        final = chunk == amount - 1
        if final:
            ins.update(enumerate([total, *others]))
            outs.update(query_gains=row, key_gains=row)
        key_outputs = call(
            functools.partial(finish, count, width[chunk + LAG], factor if final else None),
            "finish",
            ins,
            outs,
            key_outputs,
            cost=COSTS[3 + chunk],
            grid=(1,),
            in_specs=dict(keys=narrow),
            out_specs=dict(key_grad=narrow, value_grad=narrow),
            input_output_aliases={len(ins) + i: i for i in range(len(key_outputs))},
        )
    key_grad, value_grad, query_gains, key_gains = key_outputs
    return attended, query_grad, key_grad, value_grad, query_gains[0], key_gains[0]


def solution(mesh):
    block = P("dp", "ctx", None)
    return jax.shard_map(
        shards,
        mesh=mesh,
        in_specs=(P("dp", None), block, block, block, P(), P(), block),
        out_specs=(block, block, block, block, P(), P()),
        check_vma=False,
    )
```

```python
import functools

import jax
import jax.numpy as jnp
from jax import lax
from jax.experimental import pallas as pl
from jax.experimental.pallas import tpu as pltpu
from jax.sharding import PartitionSpec as P

HEADS = 8
KV_HEADS = 4
HEAD_DIM = 256
WINDOW = 512
GREACH = 4
GROUPS = HEADS // KV_HEADS
EPSILON = 1e-06
BF16 = jnp.bfloat16
F32 = jnp.float32
CHUNKS = ((0, 2), (2, 2))
LAG = 2

PIECES = 4

COSTS = 2**32, 0, 0, 2**31, 2**32, 2**31

VMEM = pl.BlockSpec(memory_space=pltpu.VMEM)
ANY = pl.BlockSpec(memory_space=pl.ANY)


def call(body, name, ins, outs, after=(), cost=0, in_specs=None, out_specs=None, **more):
    names = list(ins)

    def kernel(*refs):
        used = len(names) + len(after)
        body(*refs[: len(names)], *refs[used:])

    specs = [(in_specs or {}).get(key, VMEM) for key in names] + [ANY] * len(after)
    return pl.pallas_call(
        kernel,
        out_shape=list(outs.values()),
        in_specs=specs,
        out_specs=[(out_specs or {}).get(key, VMEM) for key in outs],
        compiler_params=pltpu.CompilerParams(vmem_limit_bytes=40 * 2**20),
        cost_estimate=pl.CostEstimate(flops=cost, bytes_accessed=1, transcendentals=0),
        name=name,
        **more,
    )(*ins.values(), *after)


def shape(rows, cols, dtype=BF16):
    return jax.ShapeDtypeStruct((rows, cols), dtype)


def core_index():
    return lax.axis_index("ctx") % 2


def payload(chunks, keys, values, *rest):
    extra = len(rest[:-1]) - len(chunks)
    small, outs, kept, sems = rest[: extra // 2], rest[extra // 2 : -1 - extra // 2], rest[-1 - extra // 2 : -1], rest[-1]
    copies = [pltpu.make_async_copy(old, new, sems.at[i]) for i, (old, new) in enumerate(zip(small, kept))]
    for (first, count), out in zip(chunks, outs):
        here = pl.ds(first * HEAD_DIM, count * HEAD_DIM)
        for side, field in enumerate((keys, values)):
            to = pl.ds(side * count * HEAD_DIM, count * HEAD_DIM)
            for piece in range(PIECES):
                share = field.shape[1] // PIECES
                rows = pl.ds(piece * share, share)
                sem = sems.at[len(copies)]
                copies.append(pltpu.make_async_copy(field.at[0, rows, here], out.at[rows, to], sem))
    for copy in copies:
        copy.start()
    for copy in copies:
        copy.wait()


def normalize(field):
    inverse = lax.rsqrt(jnp.mean(field * field, -1, keepdims=True) + EPSILON)
    return field * inverse, inverse


def dot(left, right, over):
    return lax.dot_general(left, right, ((over[:1], over[1:]), ((), ())), preferred_element_type=F32)


def attend(
    first, count, at_own, at_x, at_near, at_far, segments, queries, out_grad, own, across_x, arrived_near, arrived_far,
    across_k, across_v,    query_gain, key_gain, *rest,
):
    attended, query_grad, part_own, part_near, part_far, third_k, third_v, part_next, gains = rest
    position = lax.axis_index("ctx")
    rows = queries.shape[1]
    band = (GREACH + 1) * rows
    gain_q = query_gain[...]
    gain_k = key_gain[...]

    def segment(distance):
        block = position - distance
        first = pl.multiple_of(jnp.maximum(block, 0) * rows, rows)
        return jnp.where(block >= 0, segments[:, pl.ds(first, rows)], -1)

    key_seg = jnp.concatenate([segment(distance) for distance in range(GREACH, -1, -1)], 1)
    query_seg = jnp.broadcast_to(segment(0), (rows, rows)).T[:, :1]
    back = (
        lax.broadcasted_iota(jnp.int32, (rows, band), 0)
        - lax.broadcasted_iota(jnp.int32, (rows, band), 1)
        + GREACH * rows
    )
    live = (query_seg == key_seg) & (back >= 0) & (back < WINDOW)
    live = jnp.concatenate([live] * GROUPS, 0)

    def band_of(index):
        third = (across_k, 0) if index < count else (across_v, -count * HEAD_DIM)
        blocks = ((arrived_far, at_far), third, (arrived_near, at_near), (across_x, at_x), (own, at_own))
        return jnp.concatenate(
            [field[:, at + index * HEAD_DIM : at + (index + 1) * HEAD_DIM] for field, at in blocks], 0
        )

    def columns_of(index):
        return slice(index * HEAD_DIM, (index + 1) * HEAD_DIM)

    def query_rows(field, head):
        start = (first + head) * GROUPS
        return jnp.concatenate([field[0, :, columns_of(start + g)] for g in range(GROUPS)], 0)

    heads = range(count)
    grads = [query_rows(out_grad, head) for head in heads]
    band_v = [band_of(count + head) for head in heads]
    q_normed, q_inverse, q_scaled, k_normed, k_rounded, scores = [], [], [], [], [], []
    for head in heads:
        normed, inverse = normalize(query_rows(queries, head).astype(F32))
        q_normed.append(normed)
        q_inverse.append(inverse)
        q_scaled.append((normed * gain_q * HEAD_DIM ** (-0.5)).astype(BF16))
        k_normed.append(normalize(band_of(head).astype(F32))[0])
        k_rounded.append((k_normed[head] * gain_k).astype(BF16))
        scores.append(dot(q_scaled[head], k_rounded[head], (1, 1)))
    dprob = [dot(grads[head], band_v[head], (1, 1)) for head in heads]

    def give(parts, at):
        part_far[:, at] = parts[:rows]
        part_near[:, at] = parts[2 * rows : 3 * rows]
        part_next[:, at] = parts[3 * rows : 4 * rows].astype(BF16)
        part_own[:, at] = parts[4 * rows :]
        return parts[rows : 2 * rows].astype(BF16)

    dscore = []
    for head in heads:
        weights = jnp.where(live, jnp.exp(scores[head]), 0.0)
        probs = weights * (1.0 / jnp.sum(weights, -1, keepdims=True))
        probs_low = probs.astype(BF16)
        centre = jnp.sum(probs * dprob[head], -1, keepdims=True)
        dscore.append((probs * (dprob[head] - centre)).astype(BF16))
        third_v[:, columns_of(head)] = give(dot(probs_low, grads[head], (0, 0)), columns_of(count + head))
        output = dot(probs_low, band_v[head], (1, 0)).astype(BF16)
        for g in range(GROUPS):
            attended[:, columns_of(head * GROUPS + g)] = output[g * rows : (g + 1) * rows]
    query_gains = jnp.zeros((1, HEAD_DIM), F32)
    key_gains = jnp.zeros((1, HEAD_DIM), F32)
    for head in heads:
        key_parts = dot(dscore[head], q_scaled[head], (0, 0))
        third_k[:, columns_of(head)] = give(key_parts, columns_of(head))
        key_gains = key_gains + jnp.sum(key_parts * k_normed[head], 0, keepdims=True)
        dq = dot(dscore[head], k_rounded[head], (1, 0)) * HEAD_DIM ** (-0.5)
        scaled = dq * gain_q
        grad = q_inverse[head] * (scaled - q_normed[head] * jnp.mean(scaled * q_normed[head], -1, keepdims=True))
        for g in range(GROUPS):
            query_grad[:, columns_of(head * GROUPS + g)] = grad[g * rows : (g + 1) * rows].astype(BF16)
        query_gains = query_gains + jnp.sum(dq * q_normed[head], 0, keepdims=True)
    gains[0:1, :] = query_gains
    gains[1:2, :] = key_gains


def assemble(*refs):
    amount = len(CHUNKS)
    for index, out in enumerate(refs[-2:]):
        for (first, count), part in zip(CHUNKS, refs[index * amount : (index + 1) * amount]):
            out[0, :, first * GROUPS * HEAD_DIM : (first + count) * GROUPS * HEAD_DIM] = part[...]


def add(*refs):
    refs[-1][...] = sum(ref[...] for ref in refs[1:-1]) + refs[0][...]


def finish(count, at, factor, own, key_gain, part_own, swapped, arrived, *rest):
    if factor is None:
        key_grad, value_grad = rest
    else:
        gains, (key_grad, value_grad, query_gains, key_gains) = rest[:-4], rest[-4:]
        total = sum(ref[...] for ref in gains[1:]) + gains[0][...]
        query_gains[...] = total[0:1, :] * factor
        key_gains[...] = total[1:2, :] * factor
    rows = part_own.shape[0]
    gain_k = key_gain[...]
    for head in range(count):

        def total(index):
            here = slice(index * HEAD_DIM, (index + 1) * HEAD_DIM)
            there = slice(at + index * HEAD_DIM, at + (index + 1) * HEAD_DIM)
            extra = jnp.where(core_index() == 0, swapped[:, here].astype(F32), 0.0)
            return part_own[:, here] + extra + arrived[:, there].astype(F32)

        out = slice(head * HEAD_DIM, (head + 1) * HEAD_DIM)
        normed, inverse = normalize(own[:, out].astype(F32))
        scaled = total(head) * gain_k
        grad = inverse * (scaled - normed * jnp.mean(scaled * normed, -1, keepdims=True))
        key_grad[0, :, out] = grad.astype(BF16)
        value_grad[0, :, out] = total(count + head).astype(BF16)


def columns(rows, width, first):
    return pl.BlockSpec((1, rows, width), lambda i: (0, 0, first // width))


def move(field, axis, target):
    size = lax.axis_size(axis)
    return lax.ppermute(field, axis, [(i, target(i)) for i in range(size) if 0 <= target(i) < size])


def up(field):
    return move(field, "ctx", lambda i: i + 2)


def down(field):
    return move(field, "ctx", lambda i: i - 2)


def swap(field):
    return move(field, "ctx", lambda i: i ^ 1)


def total_over(field, axis, unit, end, most, cost=0, after=()):
    end = min(end, lax.axis_size(axis))
    while unit < end:
        group = min(most, end // unit)
        others = [move(field, axis, lambda i: i ^ (by * unit)) for by in range(1, group)]
        (field,) = call(add, "add", dict(enumerate([field, *others])), dict(o=shape(*field.shape, F32)), after, cost=cost)
        unit *= group
    return field


def shards(segment_ids, queries, keys, values, query_gain, key_gain, out_grad):
    rows = queries.shape[1]
    gain_q = query_gain.reshape(1, HEAD_DIM)
    gain_k = key_gain.reshape(1, HEAD_DIM)
    amount = len(CHUNKS)
    width = [2 * count * HEAD_DIM for _, count in CHUNKS] + [0] * LAG
    def gather(chunks, small=(), after=()):
        sources = [pltpu.with_memory_space_constraint(field, pltpu.HBM) for field in (keys, values, *small)]
        made = call(
            functools.partial(payload, chunks),
            "payload",
            dict(enumerate(sources)),
            dict(
                enumerate(
                    [shape(rows, 2 * count * HEAD_DIM) for _, count in chunks]
                    + [jax.ShapeDtypeStruct(field.shape, field.dtype) for field in small]
                )
            ),
            after,
            in_specs=dict.fromkeys(range(len(sources)), ANY),
            scratch_shapes=[pltpu.SemaphoreType.DMA((2 * len(chunks) * PIECES + len(small),))],
        )
        return made[: len(chunks)], made[len(chunks) :]

    own, _ = gather(CHUNKS[:1])
    near = {0: (up(own[0]), 0)}
    more, (segments, gain_q, gain_k) = gather(CHUNKS[1:], (segment_ids, gain_q, gain_k), own)
    own = [(field, 0) for field in (*own, *more)]
    for chunk in range(1, LAG):
        near[chunk] = (up(own[chunk][0]), 0)
    far, next_behind, third_behind = {}, {}, {}

    def climb(steps, after=()):
        ins, outs, jobs = {}, {}, []

        def use(place, chunk):
            field, at = place
            key = next((key for key, value in ins.items() if value is field), f"in{len(ins)}")
            ins[key] = field
            return key, slice(at, at + width[chunk])

        def exchange(to, chunk, first, second, halves=1):
            part = width[chunk] // halves
            for half in range(halves):
                pick = [(key, slice(at.start + half * part, at.start + (half + 1) * part)) for key, at in (use(first[chunk], chunk), use(second[chunk], chunk))]
                jobs.append((f"{to}{half}", 0, *pick))
                outs[f"{to}{half}"] = shape(rows, part)

        for step in steps:
            rise = 0
            if step + LAG < amount:
                jobs.append((f"rise{step}", rise, use(own[step + LAG], step + LAG), None))
                rise += width[step + LAG]
            if step < amount:
                jobs.append((f"rise{step}", rise, use(near[step], step), None))
                outs[f"rise{step}"] = shape(rows, rise + width[step])
                exchange("next", step, own, near)
            if step >= LAG:
                exchange("third", step - LAG, near, far, 2)

        def body(*refs):
            ref = dict(zip(list(ins) + list(outs), refs))
            for to, at, (key, here), other in jobs:
                value = ref[key][:, here]
                if other is not None:
                    value = jnp.where(core_index() == 0, value, ref[other[0]][:, other[1]])
                ref[to][:, at : at + value.shape[1]] = value

        made = dict(zip(outs, call(body, "climb", ins, outs, after, cost=10**9 * steps[0])))
        for step in steps:
            if step < amount:
                arrived = up(made[f"rise{step}"])
                ahead = 0
                if step + LAG < amount:
                    near[step + LAG] = (arrived, 0)
                    ahead = width[step + LAG]
                far[step] = (arrived, ahead)
                next_behind[step] = (swap(made["next0"]), 0)
            if step >= LAG:
                third_behind[step - LAG] = [swap(made["third0"]), swap(made["third1"])]
        return [next(iter(made.values()))]

    parts, sunk = [], {}

    def sink(step, after=()):
        fresh, older = step < amount, step >= LAG
        mine, below = width[step], width[step - LAG] if older else 0
        ins = {}
        if fresh:
            ins.update(far=parts[step]["far"], third_k=parts[step]["third_k"], third_v=parts[step]["third_v"])
        if older:
            chunk = step - LAG
            ins.update(near=parts[chunk]["near"], arrived=sunk[chunk])
            ins.update(old_k=parts[chunk]["third_k"], old_v=parts[chunk]["third_v"], next_old=parts[chunk]["next"])

        def body(*refs):
            ref = dict(zip(list(ins) + ["out"], refs))
            first = core_index() == 0
            if fresh:
                for half, extra in ((slice(0, mine // 2), ref["third_k"]), (slice(mine // 2, mine), ref["third_v"])):
                    extra = jnp.where(first, 0.0, extra[...].astype(F32))
                    ref["out"][:, half] = (ref["far"][:, half] + extra).astype(BF16)
            if older:
                for half, extra in ((slice(0, below // 2), ref["old_k"]), (slice(below // 2, below), ref["old_v"])):
                    extra = jnp.where(first, extra[...], ref["next_old"][:, half]).astype(F32)
                    total = ref["near"][:, half] + extra + ref["arrived"][:, half].astype(F32)
                    ref["out"][:, mine + half.start : mine + half.stop] = total.astype(BF16)

        (total,) = call(body, "sink", ins, dict(out=shape(rows, mine + below)), after)
        sunk[step] = down(total)
        return total

    made, gains, last, token = [], [], [], []
    order = []
    for step in range(LAG):
        order = climb([step], order)
    for chunk, (first, count) in enumerate(CHUNKS):
        order = climb([chunk + LAG], order + token)
        held = (own, next_behind, near, far)
        wide = shape(rows, GROUPS * count * HEAD_DIM)
        whole, low, half = shape(rows, width[chunk], F32), shape(rows, width[chunk]), shape(rows, width[chunk] // 2)
        result = call(
            functools.partial(attend, first, count, *(place[chunk][1] for place in held)),
            "attend",
            dict(
                segments=segments, queries=queries, out_grad=out_grad, own=own[chunk][0],
                **{f"behind{i}": place[chunk][0] for i, place in enumerate(held[1:])},
                third_k=third_behind[chunk][0], third_v=third_behind[chunk][1], gain_q=gain_q, gain_k=gain_k,
            ),
            dict(
                attended=wide, query_grad=wide, own=whole, near=whole, far=whole,
                third_k=half, third_v=half, next=low,
                gains=shape(2, HEAD_DIM, F32),
            ),
            last,
        )
        made.append(result[:2])
        gains.append(result[8])
        token = [result[8]]
        parts.append(dict(zip(("own", "near", "far"), result[2:5])))
        parts[-1].update(third_k=swap(result[5]), third_v=swap(result[6]), next=swap(result[7]))
        if chunk == amount - 1:
            (total,) = call(add, "add", dict(enumerate(gains)), dict(o=shape(2, HEAD_DIM, F32)))
            total = total_over(total, "ctx", 1, 2, 2)
            last = [*last, total]
        last = [sink(chunk, last)]

    first_sink = last
    for step in range(amount, amount + LAG):
        hold = call(add, "hold", dict(total=total), dict(o=shape(2, HEAD_DIM, F32)), [sunk[step - LAG]], cost=COSTS[5])
        last = [sink(step, [*last, *(hold if step == amount else [])])]

    attended, query_grad = call(
        assemble,
        "assemble",
        {(i, chunk): made[chunk][i] for i in range(2) for chunk in range(amount)},
        dict(a=jax.ShapeDtypeStruct(queries.shape, BF16), b=jax.ShapeDtypeStruct(queries.shape, BF16)),
        last,
    )

    factor = (lax.axis_size("dp") * queries.shape[0] * lax.axis_size("ctx") * rows) ** (-0.5)
    row = shape(1, HEAD_DIM, F32)
    chips = lax.axis_size("ctx") // 2
    (total,) = call(add, "add", dict(total=total), dict(o=shape(2, HEAD_DIM, F32)), first_sink)
    while chips > 4:
        total = total_over(total, "ctx", chips, 2 * chips, 2)
        chips //= 2
    total = total_over(total, "ctx", 2, 2 * chips, 4, COSTS[0], [sunk[amount - 1]])
    half = lax.axis_size("dp") // 2
    total = total_over(total, "dp", 1, half, 2, COSTS[1], [pltpu.with_memory_space_constraint(attended, pltpu.HBM)])
    others = [move(total, "dp", lambda i: i ^ half)] if half else []
    key_outputs = []
    for chunk, (first, count) in enumerate(CHUNKS):
        narrow = columns(rows, count * HEAD_DIM, first * HEAD_DIM)
        ins = dict(
            keys=own[chunk][0], gain=gain_k, own=parts[chunk]["own"], next=parts[chunk]["next"], arrived=sunk[chunk + LAG]
        )
        outs = dict(
            key_grad=jax.ShapeDtypeStruct(keys.shape, BF16), value_grad=jax.ShapeDtypeStruct(keys.shape, BF16)
        )
        final = chunk == amount - 1
        if final:
            ins.update(enumerate([total, *others]))
            outs.update(query_gains=row, key_gains=row)
        key_outputs = call(
            functools.partial(finish, count, width[chunk + LAG], factor if final else None),
            "finish",
            ins,
            outs,
            key_outputs,
            cost=COSTS[3 + chunk],
            grid=(1,),
            out_specs=dict(key_grad=narrow, value_grad=narrow),
            input_output_aliases={len(ins) + i: i for i in range(len(key_outputs))},
        )
    key_grad, value_grad, query_gains, key_gains = key_outputs
    return attended, query_grad, key_grad, value_grad, query_gains[0], key_gains[0]


def solution(mesh):
    block = P("dp", "ctx", None)
    return jax.shard_map(
        shards,
        mesh=mesh,
        in_specs=(P("dp", None), block, block, block, P(), P(), block),
        out_specs=(block, block, block, block, P(), P()),
        check_vma=False,
    )
```

```python
import functools

import jax
import jax.numpy as jnp
from jax import lax
from jax.experimental import pallas as pl
from jax.experimental.pallas import tpu as pltpu
from jax.sharding import PartitionSpec as P

HEADS = 8
KV_HEADS = 4
HEAD_DIM = 256
WINDOW = 512
GREACH = 4
GROUPS = HEADS // KV_HEADS
EPSILON = 1e-06
BF16 = jnp.bfloat16
F32 = jnp.float32
CHUNKS = ((0, 2), (2, 2))
LAG = 2

PIECES = 4

COSTS = 2**32, 0, 0, 2**31, 2**32, 2**31

VMEM = pl.BlockSpec(memory_space=pltpu.VMEM)
ANY = pl.BlockSpec(memory_space=pl.ANY)


def call(body, name, ins, outs, after=(), cost=0, in_specs=None, out_specs=None, **more):
    names = list(ins)

    def kernel(*refs):
        used = len(names) + len(after)
        body(*refs[: len(names)], *refs[used:])

    specs = [(in_specs or {}).get(key, VMEM) for key in names] + [ANY] * len(after)
    return pl.pallas_call(
        kernel,
        out_shape=list(outs.values()),
        in_specs=specs,
        out_specs=[(out_specs or {}).get(key, VMEM) for key in outs],
        compiler_params=pltpu.CompilerParams(vmem_limit_bytes=40 * 2**20),
        cost_estimate=pl.CostEstimate(flops=cost, bytes_accessed=1, transcendentals=0),
        name=name,
        **more,
    )(*ins.values(), *after)


def shape(rows, cols, dtype=BF16):
    return jax.ShapeDtypeStruct((rows, cols), dtype)


def core_index():
    return lax.axis_index("ctx") % 2


def payload(chunks, keys, values, *rest):
    extra = len(rest[:-1]) - len(chunks)
    small, outs, kept, sems = rest[: extra // 2], rest[extra // 2 : -1 - extra // 2], rest[-1 - extra // 2 : -1], rest[-1]
    copies = [pltpu.make_async_copy(old, new, sems.at[i]) for i, (old, new) in enumerate(zip(small, kept))]
    for (first, count), out in zip(chunks, outs):
        here = pl.ds(first * HEAD_DIM, count * HEAD_DIM)
        for side, field in enumerate((keys, values)):
            to = pl.ds(side * count * HEAD_DIM, count * HEAD_DIM)
            for piece in range(PIECES):
                share = field.shape[1] // PIECES
                rows = pl.ds(piece * share, share)
                sem = sems.at[len(copies)]
                copies.append(pltpu.make_async_copy(field.at[0, rows, here], out.at[rows, to], sem))
    for copy in copies:
        copy.start()
    for copy in copies:
        copy.wait()


def normalize(field):
    inverse = lax.rsqrt(jnp.mean(field * field, -1, keepdims=True) + EPSILON)
    return field * inverse, inverse


def dot(left, right, over):
    return lax.dot_general(left, right, ((over[:1], over[1:]), ((), ())), preferred_element_type=F32)


def attend(
    first, count, at_own, at_x, at_near, at_far, segments, queries, out_grad, own, across_x, arrived_near, arrived_far,
    across_k, across_v,    query_gain, key_gain, *rest,
):
    attended, query_grad, part_own, part_near, part_far, third_k, third_v, part_next, gains = rest
    position = lax.axis_index("ctx")
    rows = queries.shape[1]
    band = (GREACH + 1) * rows
    gain_q = query_gain[...]
    gain_k = key_gain[...]

    def segment(distance):
        block = position - distance
        first = pl.multiple_of(jnp.maximum(block, 0) * rows, rows)
        return jnp.where(block >= 0, segments[:, pl.ds(first, rows)], -1)

    key_seg = jnp.concatenate([segment(distance) for distance in range(GREACH, -1, -1)], 1)
    query_seg = jnp.broadcast_to(segment(0), (rows, rows)).T[:, :1]
    back = (
        lax.broadcasted_iota(jnp.int32, (rows, band), 0)
        - lax.broadcasted_iota(jnp.int32, (rows, band), 1)
        + GREACH * rows
    )
    live = (query_seg == key_seg) & (back >= 0) & (back < WINDOW)
    live = jnp.concatenate([live] * GROUPS, 0)

    def band_of(index):
        third = (across_k, 0) if index < count else (across_v, -count * HEAD_DIM)
        blocks = ((arrived_far, at_far), third, (arrived_near, at_near), (across_x, at_x), (own, at_own))
        return jnp.concatenate(
            [field[:, at + index * HEAD_DIM : at + (index + 1) * HEAD_DIM] for field, at in blocks], 0
        )

    def columns_of(index):
        return slice(index * HEAD_DIM, (index + 1) * HEAD_DIM)

    def query_rows(field, head):
        start = (first + head) * GROUPS
        return jnp.concatenate([field[0, :, columns_of(start + g)] for g in range(GROUPS)], 0)

    heads = range(count)
    grads = [query_rows(out_grad, head) for head in heads]
    band_v = [band_of(count + head) for head in heads]
    q_normed, q_inverse, q_scaled, k_normed, k_rounded, scores = [], [], [], [], [], []
    for head in heads:
        normed, inverse = normalize(query_rows(queries, head).astype(F32))
        q_normed.append(normed)
        q_inverse.append(inverse)
        q_scaled.append((normed * gain_q * HEAD_DIM ** (-0.5)).astype(BF16))
        k_normed.append(normalize(band_of(head).astype(F32))[0])
        k_rounded.append((k_normed[head] * gain_k).astype(BF16))
        scores.append(dot(q_scaled[head], k_rounded[head], (1, 1)))
    dprob = [dot(grads[head], band_v[head], (1, 1)) for head in heads]

    def give(parts, at):
        part_far[:, at] = parts[:rows]
        part_near[:, at] = parts[2 * rows : 3 * rows]
        part_next[:, at] = parts[3 * rows : 4 * rows].astype(BF16)
        part_own[:, at] = parts[4 * rows :]
        return parts[rows : 2 * rows].astype(BF16)

    dscore = []
    for head in heads:
        weights = jnp.where(live, jnp.exp(scores[head]), 0.0)
        probs = weights * (1.0 / jnp.sum(weights, -1, keepdims=True))
        probs_low = probs.astype(BF16)
        centre = jnp.sum(probs * dprob[head], -1, keepdims=True)
        dscore.append((probs * (dprob[head] - centre)).astype(BF16))
        third_v[:, columns_of(head)] = give(dot(probs_low, grads[head], (0, 0)), columns_of(count + head))
        output = dot(probs_low, band_v[head], (1, 0)).astype(BF16)
        for g in range(GROUPS):
            attended[:, columns_of(head * GROUPS + g)] = output[g * rows : (g + 1) * rows]
    query_gains = jnp.zeros((1, HEAD_DIM), F32)
    key_gains = jnp.zeros((1, HEAD_DIM), F32)
    for head in heads:
        key_parts = dot(dscore[head], q_scaled[head], (0, 0))
        third_k[:, columns_of(head)] = give(key_parts, columns_of(head))
        key_gains = key_gains + jnp.sum(key_parts * k_normed[head], 0, keepdims=True)
        dq = dot(dscore[head], k_rounded[head], (1, 0)) * HEAD_DIM ** (-0.5)
        scaled = dq * gain_q
        grad = q_inverse[head] * (scaled - q_normed[head] * jnp.mean(scaled * q_normed[head], -1, keepdims=True))
        for g in range(GROUPS):
            query_grad[:, columns_of(head * GROUPS + g)] = grad[g * rows : (g + 1) * rows].astype(BF16)
        query_gains = query_gains + jnp.sum(dq * q_normed[head], 0, keepdims=True)
    gains[0:1, :] = query_gains
    gains[1:2, :] = key_gains


def assemble(*refs):
    amount = len(CHUNKS)
    for index, out in enumerate(refs[-2:]):
        for (first, count), part in zip(CHUNKS, refs[index * amount : (index + 1) * amount]):
            out[0, :, first * GROUPS * HEAD_DIM : (first + count) * GROUPS * HEAD_DIM] = part[...]


def add(*refs):
    refs[-1][...] = sum(ref[...] for ref in refs[1:-1]) + refs[0][...]


def finish(count, at, factor, own, key_gain, part_own, swapped, arrived, *rest):
    if factor is None:
        key_grad, value_grad = rest
    else:
        gains, (key_grad, value_grad, query_gains, key_gains) = rest[:-4], rest[-4:]
        total = sum(ref[...] for ref in gains[1:]) + gains[0][...]
        query_gains[...] = total[0:1, :] * factor
        key_gains[...] = total[1:2, :] * factor
    rows = part_own.shape[0]
    gain_k = key_gain[...]
    for head in range(count):

        def total(index):
            here = slice(index * HEAD_DIM, (index + 1) * HEAD_DIM)
            there = slice(at + index * HEAD_DIM, at + (index + 1) * HEAD_DIM)
            extra = jnp.where(core_index() == 0, swapped[:, here].astype(F32), 0.0)
            return part_own[:, here] + extra + arrived[:, there].astype(F32)

        out = slice(head * HEAD_DIM, (head + 1) * HEAD_DIM)
        normed, inverse = normalize(own[:, out].astype(F32))
        scaled = total(head) * gain_k
        grad = inverse * (scaled - normed * jnp.mean(scaled * normed, -1, keepdims=True))
        key_grad[0, :, out] = grad.astype(BF16)
        value_grad[0, :, out] = total(count + head).astype(BF16)


def columns(rows, width, first):
    return pl.BlockSpec((1, rows, width), lambda i: (0, 0, first // width))


def move(field, axis, target):
    size = lax.axis_size(axis)
    return lax.ppermute(field, axis, [(i, target(i)) for i in range(size) if 0 <= target(i) < size])


def up(field, lowest=0):
    return move(field, "ctx", lambda i: i + 2 if i >= 2 * lowest else -1)


def down(field, lowest=0):
    return move(field, "ctx", lambda i: i - 2 if i - 2 >= 2 * lowest else -1)


def swap(field):
    return move(field, "ctx", lambda i: i ^ 1)


def total_over(field, axis, unit, end, most, cost=0, after=()):
    end = min(end, lax.axis_size(axis))
    while unit < end:
        group = min(most, end // unit)
        others = [move(field, axis, lambda i: i ^ (by * unit)) for by in range(1, group)]
        (field,) = call(add, "add", dict(enumerate([field, *others])), dict(o=shape(*field.shape, F32)), after, cost=cost)
        unit *= group
    return field


def shards(segment_ids, queries, keys, values, query_gain, key_gain, out_grad):
    rows = queries.shape[1]
    gain_q = query_gain.reshape(1, HEAD_DIM)
    gain_k = key_gain.reshape(1, HEAD_DIM)
    amount = len(CHUNKS)
    width = [2 * count * HEAD_DIM for _, count in CHUNKS] + [0] * LAG
    def gather(chunks, small=(), after=()):
        sources = [pltpu.with_memory_space_constraint(field, pltpu.HBM) for field in (keys, values, *small)]
        made = call(
            functools.partial(payload, chunks),
            "payload",
            dict(enumerate(sources)),
            dict(
                enumerate(
                    [shape(rows, 2 * count * HEAD_DIM) for _, count in chunks]
                    + [jax.ShapeDtypeStruct(field.shape, field.dtype) for field in small]
                )
            ),
            after,
            in_specs=dict.fromkeys(range(len(sources)), ANY),
            scratch_shapes=[pltpu.SemaphoreType.DMA((2 * len(chunks) * PIECES + len(small),))],
        )
        return made[: len(chunks)], made[len(chunks) :]

    own, _ = gather(CHUNKS[:1])
    near = {0: (up(own[0]), 0)}
    more, (segments, gain_q, gain_k) = gather(CHUNKS[1:], (segment_ids, gain_q, gain_k), own)
    own = [(field, 0) for field in (*own, *more)]
    for chunk in range(1, LAG):
        near[chunk] = (up(own[chunk][0]), 0)
    far, next_behind, third_behind = {}, {}, {}

    def climb(steps, after=()):
        ins, outs, jobs = {}, {}, []

        def use(place, chunk):
            field, at = place
            key = next((key for key, value in ins.items() if value is field), f"in{len(ins)}")
            ins[key] = field
            return key, slice(at, at + width[chunk])

        def exchange(to, chunk, first, second, halves=1):
            part = width[chunk] // halves
            for half in range(halves):
                pick = [(key, slice(at.start + half * part, at.start + (half + 1) * part)) for key, at in (use(first[chunk], chunk), use(second[chunk], chunk))]
                jobs.append((f"{to}{half}", 0, *pick))
                outs[f"{to}{half}"] = shape(rows, part)

        for step in steps:
            rise = 0
            if step + LAG < amount:
                jobs.append((f"rise{step}", rise, use(own[step + LAG], step + LAG), None))
                rise += width[step + LAG]
            if step < amount:
                jobs.append((f"rise{step}", rise, use(near[step], step), None))
                outs[f"rise{step}"] = shape(rows, rise + width[step])
                exchange("next", step, own, near)
            if step >= LAG:
                exchange("third", step - LAG, near, far, 2)

        def body(*refs):
            ref = dict(zip(list(ins) + list(outs), refs))
            for to, at, (key, here), other in jobs:
                value = ref[key][:, here]
                if other is not None:
                    value = jnp.where(core_index() == 0, value, ref[other[0]][:, other[1]])
                ref[to][:, at : at + value.shape[1]] = value

        made = dict(zip(outs, call(body, "climb", ins, outs, after, cost=10**9 * steps[0])))
        for step in steps:
            if step < amount:
                arrived = up(made[f"rise{step}"], 0 if step + LAG < amount else 1)
                ahead = 0
                if step + LAG < amount:
                    near[step + LAG] = (arrived, 0)
                    ahead = width[step + LAG]
                far[step] = (arrived, ahead)
                next_behind[step] = (swap(made["next0"]), 0)
            if step >= LAG:
                third_behind[step - LAG] = [swap(made["third0"]), swap(made["third1"])]
        return [next(iter(made.values()))]

    parts, sunk = [], {}

    def sink(step, after=()):
        fresh, older = step < amount, step >= LAG
        mine, below = width[step], width[step - LAG] if older else 0
        ins = {}
        if fresh:
            ins.update(far=parts[step]["far"], third_k=parts[step]["third_k"], third_v=parts[step]["third_v"])
        if older:
            chunk = step - LAG
            ins.update(near=parts[chunk]["near"], arrived=sunk[chunk])
            ins.update(old_k=parts[chunk]["third_k"], old_v=parts[chunk]["third_v"], next_old=parts[chunk]["next"])

        def body(*refs):
            ref = dict(zip(list(ins) + ["out"], refs))
            first = core_index() == 0
            if fresh:
                for half, extra in ((slice(0, mine // 2), ref["third_k"]), (slice(mine // 2, mine), ref["third_v"])):
                    extra = jnp.where(first, 0.0, extra[...].astype(F32))
                    ref["out"][:, half] = (ref["far"][:, half] + extra).astype(BF16)
            if older:
                for half, extra in ((slice(0, below // 2), ref["old_k"]), (slice(below // 2, below), ref["old_v"])):
                    extra = jnp.where(first, extra[...], ref["next_old"][:, half]).astype(F32)
                    total = ref["near"][:, half] + extra + ref["arrived"][:, half].astype(F32)
                    ref["out"][:, mine + half.start : mine + half.stop] = total.astype(BF16)

        (total,) = call(body, "sink", ins, dict(out=shape(rows, mine + below)), after)
        sunk[step] = down(total, 0 if older else 1)
        return total

    made, gains, last, token = [], [], [], []
    order = []
    for step in range(LAG):
        order = climb([step], order)
    for chunk, (first, count) in enumerate(CHUNKS):
        order = climb([chunk + LAG], order + token)
        held = (own, next_behind, near, far)
        wide = shape(rows, GROUPS * count * HEAD_DIM)
        whole, low, half = shape(rows, width[chunk], F32), shape(rows, width[chunk]), shape(rows, width[chunk] // 2)
        result = call(
            functools.partial(attend, first, count, *(place[chunk][1] for place in held)),
            "attend",
            dict(
                segments=segments, queries=queries, out_grad=out_grad, own=own[chunk][0],
                **{f"behind{i}": place[chunk][0] for i, place in enumerate(held[1:])},
                third_k=third_behind[chunk][0], third_v=third_behind[chunk][1], gain_q=gain_q, gain_k=gain_k,
            ),
            dict(
                attended=wide, query_grad=wide, own=whole, near=whole, far=whole,
                third_k=half, third_v=half, next=low,
                gains=shape(2, HEAD_DIM, F32),
            ),
            last,
        )
        made.append(result[:2])
        gains.append(result[8])
        token = [result[8]]
        parts.append(dict(zip(("own", "near", "far"), result[2:5])))
        parts[-1].update(third_k=swap(result[5]), third_v=swap(result[6]), next=swap(result[7]))
        if chunk == amount - 1:
            (total,) = call(add, "add", dict(enumerate(gains)), dict(o=shape(2, HEAD_DIM, F32)))
            total = total_over(total, "ctx", 1, 2, 2)
            last = [*last, total]
        last = [sink(chunk, last)]

    first_sink = last
    for step in range(amount, amount + LAG):
        hold = call(add, "hold", dict(total=total), dict(o=shape(2, HEAD_DIM, F32)), [sunk[step - LAG]], cost=COSTS[5])
        last = [sink(step, [*last, *(hold if step == amount else [])])]

    attended, query_grad = call(
        assemble,
        "assemble",
        {(i, chunk): made[chunk][i] for i in range(2) for chunk in range(amount)},
        dict(a=jax.ShapeDtypeStruct(queries.shape, BF16), b=jax.ShapeDtypeStruct(queries.shape, BF16)),
        last,
    )

    factor = (lax.axis_size("dp") * queries.shape[0] * lax.axis_size("ctx") * rows) ** (-0.5)
    row = shape(1, HEAD_DIM, F32)
    chips = lax.axis_size("ctx") // 2
    (total,) = call(add, "add", dict(total=total), dict(o=shape(2, HEAD_DIM, F32)), first_sink)
    while chips > 4:
        total = total_over(total, "ctx", chips, 2 * chips, 2)
        chips //= 2
    total = total_over(total, "ctx", 2, 2 * chips, 4, COSTS[0], [sunk[amount - 1]])
    half = lax.axis_size("dp") // 2
    total = total_over(total, "dp", 1, half, 2, COSTS[1], [pltpu.with_memory_space_constraint(attended, pltpu.HBM)])
    others = [move(total, "dp", lambda i: i ^ half)] if half else []
    key_outputs = []
    for chunk, (first, count) in enumerate(CHUNKS):
        narrow = columns(rows, count * HEAD_DIM, first * HEAD_DIM)
        ins = dict(
            keys=own[chunk][0], gain=gain_k, own=parts[chunk]["own"], next=parts[chunk]["next"], arrived=sunk[chunk + LAG]
        )
        outs = dict(
            key_grad=jax.ShapeDtypeStruct(keys.shape, BF16), value_grad=jax.ShapeDtypeStruct(keys.shape, BF16)
        )
        final = chunk == amount - 1
        if final:
            ins.update(enumerate([total, *others]))
            outs.update(query_gains=row, key_gains=row)
        key_outputs = call(
            functools.partial(finish, count, width[chunk + LAG], factor if final else None),
            "finish",
            ins,
            outs,
            key_outputs,
            cost=COSTS[3 + chunk],
            grid=(1,),
            out_specs=dict(key_grad=narrow, value_grad=narrow),
            input_output_aliases={len(ins) + i: i for i in range(len(key_outputs))},
        )
    key_grad, value_grad, query_gains, key_gains = key_outputs
    return attended, query_grad, key_grad, value_grad, query_gains[0], key_gains[0]


def solution(mesh):
    block = P("dp", "ctx", None)
    return jax.shard_map(
        shards,
        mesh=mesh,
        in_specs=(P("dp", None), block, block, block, P(), P(), block),
        out_specs=(block, block, block, block, P(), P()),
        check_vma=False,
    )
```

```python
import functools

import jax
import jax.numpy as jnp
from jax import lax
from jax.experimental import pallas as pl
from jax.experimental.pallas import tpu as pltpu
from jax.sharding import PartitionSpec as P

HEADS = 8
KV_HEADS = 4
HEAD_DIM = 256
WINDOW = 512
GREACH = 4
GROUPS = HEADS // KV_HEADS
EPSILON = 1e-06
BF16 = jnp.bfloat16
F32 = jnp.float32
CHUNKS = ((0, 2), (2, 2))
LAG = 2

PIECES = 4

COSTS = 2**32, 0, 0, 2**31, 2**32, 2**31

VMEM = pl.BlockSpec(memory_space=pltpu.VMEM)
ANY = pl.BlockSpec(memory_space=pl.ANY)


def call(body, name, ins, outs, after=(), cost=0, in_specs=None, out_specs=None, **more):
    names = list(ins)

    def kernel(*refs):
        used = len(names) + len(after)
        body(*refs[: len(names)], *refs[used:])

    specs = [(in_specs or {}).get(key, VMEM) for key in names] + [ANY] * len(after)
    return pl.pallas_call(
        kernel,
        out_shape=list(outs.values()),
        in_specs=specs,
        out_specs=[(out_specs or {}).get(key, VMEM) for key in outs],
        compiler_params=pltpu.CompilerParams(vmem_limit_bytes=40 * 2**20),
        cost_estimate=pl.CostEstimate(flops=cost, bytes_accessed=1, transcendentals=0),
        name=name,
        **more,
    )(*ins.values(), *after)


def shape(rows, cols, dtype=BF16):
    return jax.ShapeDtypeStruct((rows, cols), dtype)


def core_index():
    return lax.axis_index("ctx") % 2


def payload(chunks, keys, values, *rest):
    extra = len(rest[:-1]) - len(chunks)
    small, outs, kept, sems = rest[: extra // 2], rest[extra // 2 : -1 - extra // 2], rest[-1 - extra // 2 : -1], rest[-1]
    copies = [pltpu.make_async_copy(old, new, sems.at[i]) for i, (old, new) in enumerate(zip(small, kept))]
    for (first, count), out in zip(chunks, outs):
        here = pl.ds(first * HEAD_DIM, count * HEAD_DIM)
        for side, field in enumerate((keys, values)):
            to = pl.ds(side * count * HEAD_DIM, count * HEAD_DIM)
            for piece in range(PIECES):
                share = field.shape[1] // PIECES
                rows = pl.ds(piece * share, share)
                sem = sems.at[len(copies)]
                copies.append(pltpu.make_async_copy(field.at[0, rows, here], out.at[rows, to], sem))
    for copy in copies:
        copy.start()
    for copy in copies:
        copy.wait()


def normalize(field):
    inverse = lax.rsqrt(jnp.mean(field * field, -1, keepdims=True) + EPSILON)
    return field * inverse, inverse


def dot(left, right, over):
    return lax.dot_general(left, right, ((over[:1], over[1:]), ((), ())), preferred_element_type=F32)


def columns_of(index):
    return slice(index * HEAD_DIM, (index + 1) * HEAD_DIM)


def live_pairs(segments, rows, distances):
    position = lax.axis_index("ctx")

    def segment(distance):
        block = position - distance
        first = pl.multiple_of(jnp.maximum(block, 0) * rows, rows)
        return jnp.where(block >= 0, segments[:, pl.ds(first, rows)], -1)

    key_seg = jnp.concatenate([segment(distance) for distance in distances], 1)
    query_seg = jnp.broadcast_to(segment(0), (rows, rows)).T[:, :1]
    span = (rows, len(distances) * rows)
    back = lax.broadcasted_iota(jnp.int32, span, 0) - lax.broadcasted_iota(jnp.int32, span, 1) + distances[0] * rows
    live = (query_seg == key_seg) & (back >= 0) & (back < WINDOW)
    return jnp.concatenate([live] * GROUPS, 0)


def query_rows(field, head):
    return jnp.concatenate([field[0, :, columns_of(head * GROUPS + g)] for g in range(GROUPS)], 0)


def scored(live, queries, grads, keys, values, gain_q, gain_k):
    k_normed = normalize(keys.astype(F32))[0]
    k_rounded = (k_normed * gain_k).astype(BF16)
    weights = jnp.where(live, jnp.exp(dot(queries, k_rounded, (1, 1))), 0.0)
    return k_normed, k_rounded, weights, dot(grads, values, (1, 1))


def normed_queries(queries, head, gain_q):
    q_normed, q_inverse = normalize(query_rows(queries, head).astype(F32))
    return q_normed, q_inverse, (q_normed * gain_q * HEAD_DIM ** (-0.5)).astype(BF16)


def begin(first, count, places, segments, queries, out_grad, own, across_x, arrived_near, query_gain, key_gain, *outs):
    live = live_pairs(segments, queries.shape[1], (2, 1, 0))
    gain_q, gain_k = query_gain[...], key_gain[...]
    blocks = list(zip((arrived_near, across_x, own), places))

    def band_of(index):
        return jnp.concatenate([field[:, at + index * HEAD_DIM : at + (index + 1) * HEAD_DIM] for field, at in blocks], 0)

    for head in range(count):
        q_scaled = normed_queries(queries, first + head, gain_q)[2]
        grads = query_rows(out_grad, first + head)
        made = scored(live, q_scaled, grads, band_of(head), band_of(count + head), gain_q, gain_k)
        for out, value in zip(outs, made):
            share = value.shape[0]
            out[head * share : (head + 1) * share, :] = value


def attend(
    first, count, places, at_far, segments, queries, out_grad, own, across_x, arrived_near, arrived_far, across_k,
    across_v, query_gain, key_gain, begun_normed, begun_rounded, begun_weights, begun_dprob, *rest,
):
    attended, query_grad, part_own, part_near, part_far, third_k, third_v, part_next, gains = rest
    rows = queries.shape[1]
    gain_q, gain_k = query_gain[...], key_gain[...]
    live = live_pairs(segments, rows, (4, 3))
    blocks = list(zip((arrived_near, across_x, own), places))

    def far_of(index):
        third = (across_k, 0) if index < count else (across_v, -count * HEAD_DIM)
        return [field[:, at + index * HEAD_DIM : at + (index + 1) * HEAD_DIM] for field, at in ((arrived_far, at_far), third)]

    def near_of(index):
        return [field[:, at + index * HEAD_DIM : at + (index + 1) * HEAD_DIM] for field, at in blocks]

    def begun(field, head):
        share = field.shape[0] // count
        return field[head * share : (head + 1) * share, :]

    heads = range(count)
    grads = [query_rows(out_grad, first + head) for head in heads]
    band_v = [jnp.concatenate(far_of(count + head) + near_of(count + head), 0) for head in heads]
    query = [normed_queries(queries, first + head, gain_q) for head in heads]
    k_normed, k_rounded, weights, dprob = [], [], [], []
    for head in heads:
        far_keys, far_values = (jnp.concatenate(far_of(index), 0) for index in (head, count + head))
        made = scored(live, query[head][2], grads[head], far_keys, far_values, gain_q, gain_k)
        k_normed.append(jnp.concatenate([made[0], begun(begun_normed, head)], 0))
        k_rounded.append(jnp.concatenate([made[1], begun(begun_rounded, head)], 0))
        weights.append(jnp.concatenate([made[2], begun(begun_weights, head)], 1))
        dprob.append(jnp.concatenate([made[3], begun(begun_dprob, head)], 1))

    def give(parts, at):
        part_far[:, at] = parts[:rows]
        part_near[:, at] = parts[2 * rows : 3 * rows]
        part_next[:, at] = parts[3 * rows : 4 * rows].astype(BF16)
        part_own[:, at] = parts[4 * rows :]
        return parts[rows : 2 * rows].astype(BF16)

    dscore = []
    for head in heads:
        probs = weights[head] * (1.0 / jnp.sum(weights[head], -1, keepdims=True))
        probs_low = probs.astype(BF16)
        centre = jnp.sum(probs * dprob[head], -1, keepdims=True)
        dscore.append((probs * (dprob[head] - centre)).astype(BF16))
        third_v[:, columns_of(head)] = give(dot(probs_low, grads[head], (0, 0)), columns_of(count + head))
        output = dot(probs_low, band_v[head], (1, 0)).astype(BF16)
        for g in range(GROUPS):
            attended[:, columns_of(head * GROUPS + g)] = output[g * rows : (g + 1) * rows]
    query_gains = jnp.zeros((1, HEAD_DIM), F32)
    key_gains = jnp.zeros((1, HEAD_DIM), F32)
    for head in heads:
        q_normed, q_inverse, q_scaled = query[head]
        key_parts = dot(dscore[head], q_scaled, (0, 0))
        third_k[:, columns_of(head)] = give(key_parts, columns_of(head))
        key_gains = key_gains + jnp.sum(key_parts * k_normed[head], 0, keepdims=True)
        dq = dot(dscore[head], k_rounded[head], (1, 0)) * HEAD_DIM ** (-0.5)
        scaled = dq * gain_q
        grad = q_inverse * (scaled - q_normed * jnp.mean(scaled * q_normed, -1, keepdims=True))
        for g in range(GROUPS):
            query_grad[:, columns_of(head * GROUPS + g)] = grad[g * rows : (g + 1) * rows].astype(BF16)
        query_gains = query_gains + jnp.sum(dq * q_normed, 0, keepdims=True)
    gains[0:1, :] = query_gains
    gains[1:2, :] = key_gains


def assemble(*refs):
    amount = len(CHUNKS)
    for index, out in enumerate(refs[-2:]):
        for (first, count), part in zip(CHUNKS, refs[index * amount : (index + 1) * amount]):
            out[0, :, first * GROUPS * HEAD_DIM : (first + count) * GROUPS * HEAD_DIM] = part[...]


def add(*refs):
    refs[-1][...] = sum(ref[...] for ref in refs[1:-1]) + refs[0][...]


def finish(count, at, factor, own, key_gain, part_own, swapped, arrived, *rest):
    if factor is None:
        key_grad, value_grad = rest
    else:
        gains, (key_grad, value_grad, query_gains, key_gains) = rest[:-4], rest[-4:]
        total = sum(ref[...] for ref in gains[1:]) + gains[0][...]
        query_gains[...] = total[0:1, :] * factor
        key_gains[...] = total[1:2, :] * factor
    rows = part_own.shape[0]
    gain_k = key_gain[...]
    for head in range(count):

        def total(index):
            here = slice(index * HEAD_DIM, (index + 1) * HEAD_DIM)
            there = slice(at + index * HEAD_DIM, at + (index + 1) * HEAD_DIM)
            extra = jnp.where(core_index() == 0, swapped[:, here].astype(F32), 0.0)
            return part_own[:, here] + extra + arrived[:, there].astype(F32)

        out = slice(head * HEAD_DIM, (head + 1) * HEAD_DIM)
        normed, inverse = normalize(own[:, out].astype(F32))
        scaled = total(head) * gain_k
        grad = inverse * (scaled - normed * jnp.mean(scaled * normed, -1, keepdims=True))
        key_grad[0, :, out] = grad.astype(BF16)
        value_grad[0, :, out] = total(count + head).astype(BF16)


def columns(rows, width, first):
    return pl.BlockSpec((1, rows, width), lambda i: (0, 0, first // width))


def move(field, axis, target):
    size = lax.axis_size(axis)
    return lax.ppermute(field, axis, [(i, target(i)) for i in range(size) if 0 <= target(i) < size])


def up(field, lowest=0):
    return move(field, "ctx", lambda i: i + 2 if i >= 2 * lowest else -1)


def down(field, lowest=0):
    return move(field, "ctx", lambda i: i - 2 if i - 2 >= 2 * lowest else -1)


def swap(field):
    return move(field, "ctx", lambda i: i ^ 1)


def total_over(field, axis, unit, end, most, cost=0, after=()):
    end = min(end, lax.axis_size(axis))
    while unit < end:
        group = min(most, end // unit)
        others = [move(field, axis, lambda i: i ^ (by * unit)) for by in range(1, group)]
        (field,) = call(add, "add", dict(enumerate([field, *others])), dict(o=shape(*field.shape, F32)), after, cost=cost)
        unit *= group
    return field


def shards(segment_ids, queries, keys, values, query_gain, key_gain, out_grad):
    rows = queries.shape[1]
    gain_q = query_gain.reshape(1, HEAD_DIM)
    gain_k = key_gain.reshape(1, HEAD_DIM)
    amount = len(CHUNKS)
    width = [2 * count * HEAD_DIM for _, count in CHUNKS] + [0] * LAG
    def gather(chunks, small=(), after=()):
        sources = [pltpu.with_memory_space_constraint(field, pltpu.HBM) for field in (keys, values, *small)]
        made = call(
            functools.partial(payload, chunks),
            "payload",
            dict(enumerate(sources)),
            dict(
                enumerate(
                    [shape(rows, 2 * count * HEAD_DIM) for _, count in chunks]
                    + [jax.ShapeDtypeStruct(field.shape, field.dtype) for field in small]
                )
            ),
            after,
            in_specs=dict.fromkeys(range(len(sources)), ANY),
            scratch_shapes=[pltpu.SemaphoreType.DMA((2 * len(chunks) * PIECES + len(small),))],
        )
        return made[: len(chunks)], made[len(chunks) :]

    own, _ = gather(CHUNKS[:1])
    near = {0: (up(own[0]), 0)}
    more, (segments, gain_q, gain_k) = gather(CHUNKS[1:], (segment_ids, gain_q, gain_k), own)
    own = [(field, 0) for field in (*own, *more)]
    for chunk in range(1, LAG):
        near[chunk] = (up(own[chunk][0]), 0)
    far, next_behind, third_behind = {}, {}, {}

    def climb(steps, after=()):
        ins, outs, jobs = {}, {}, []

        def use(place, chunk):
            field, at = place
            key = next((key for key, value in ins.items() if value is field), f"in{len(ins)}")
            ins[key] = field
            return key, slice(at, at + width[chunk])

        def exchange(to, chunk, first, second, halves=1):
            part = width[chunk] // halves
            for half in range(halves):
                pick = [(key, slice(at.start + half * part, at.start + (half + 1) * part)) for key, at in (use(first[chunk], chunk), use(second[chunk], chunk))]
                jobs.append((f"{to}{half}", 0, *pick))
                outs[f"{to}{half}"] = shape(rows, part)

        for step in steps:
            rise = 0
            if step + LAG < amount:
                jobs.append((f"rise{step}", rise, use(own[step + LAG], step + LAG), None))
                rise += width[step + LAG]
            if step < amount:
                jobs.append((f"rise{step}", rise, use(near[step], step), None))
                outs[f"rise{step}"] = shape(rows, rise + width[step])
                exchange("next", step, own, near)
            if step >= LAG:
                exchange("third", step - LAG, near, far, 2)

        def body(*refs):
            ref = dict(zip(list(ins) + list(outs), refs))
            for to, at, (key, here), other in jobs:
                value = ref[key][:, here]
                if other is not None:
                    value = jnp.where(core_index() == 0, value, ref[other[0]][:, other[1]])
                ref[to][:, at : at + value.shape[1]] = value

        made = dict(zip(outs, call(body, "climb", ins, outs, after, cost=10**9 * steps[0])))
        for step in steps:
            if step < amount:
                arrived = up(made[f"rise{step}"], 0 if step + LAG < amount else 1)
                ahead = 0
                if step + LAG < amount:
                    near[step + LAG] = (arrived, 0)
                    ahead = width[step + LAG]
                far[step] = (arrived, ahead)
                next_behind[step] = (swap(made["next0"]), 0)
            if step >= LAG:
                third_behind[step - LAG] = [swap(made["third0"]), swap(made["third1"])]
        return [next(iter(made.values()))]

    parts, sunk = [], {}

    def sink(step, after=()):
        fresh, older = step < amount, step >= LAG
        mine, below = width[step], width[step - LAG] if older else 0
        ins = {}
        if fresh:
            ins.update(far=parts[step]["far"], third_k=parts[step]["third_k"], third_v=parts[step]["third_v"])
        if older:
            chunk = step - LAG
            ins.update(near=parts[chunk]["near"], arrived=sunk[chunk])
            ins.update(old_k=parts[chunk]["third_k"], old_v=parts[chunk]["third_v"], next_old=parts[chunk]["next"])

        def body(*refs):
            ref = dict(zip(list(ins) + ["out"], refs))
            first = core_index() == 0
            if fresh:
                for half, extra in ((slice(0, mine // 2), ref["third_k"]), (slice(mine // 2, mine), ref["third_v"])):
                    extra = jnp.where(first, 0.0, extra[...].astype(F32))
                    ref["out"][:, half] = (ref["far"][:, half] + extra).astype(BF16)
            if older:
                for half, extra in ((slice(0, below // 2), ref["old_k"]), (slice(below // 2, below), ref["old_v"])):
                    extra = jnp.where(first, extra[...], ref["next_old"][:, half]).astype(F32)
                    total = ref["near"][:, half] + extra + ref["arrived"][:, half].astype(F32)
                    ref["out"][:, mine + half.start : mine + half.stop] = total.astype(BF16)

        (total,) = call(body, "sink", ins, dict(out=shape(rows, mine + below)), after)
        sunk[step] = down(total, 0 if older else 1)
        return total

    made, gains, last, token = [], [], [], []
    order = []
    for step in range(LAG):
        order = climb([step], order)
    for chunk, (first, count) in enumerate(CHUNKS):
        tall, square = count * (GREACH - 1) * rows, count * GROUPS * rows
        held = dict(own=own[chunk], across_x=next_behind[chunk], near=near[chunk])
        places = [held[key][1] for key in ("near", "across_x", "own")]
        common = dict(segments=segments, queries=queries, out_grad=out_grad, **{key: held[key][0] for key in held})
        begun = call(
            functools.partial(begin, first, count, places),
            "begin",
            dict(**common, gain_q=gain_q, gain_k=gain_k),
            dict(
                normed=shape(tall, HEAD_DIM, F32), rounded=shape(tall, HEAD_DIM),
                weights=shape(square, (GREACH - 1) * rows, F32), dprob=shape(square, (GREACH - 1) * rows, F32),
            ),
        )
        order = climb([chunk + LAG], order + token + list(begun[1:2]))
        wide = shape(rows, GROUPS * count * HEAD_DIM)
        whole, low, half = shape(rows, width[chunk], F32), shape(rows, width[chunk]), shape(rows, width[chunk] // 2)
        result = call(
            functools.partial(attend, first, count, places, far[chunk][1]),
            "attend",
            dict(
                **common, far=far[chunk][0], third_k=third_behind[chunk][0], third_v=third_behind[chunk][1],
                gain_q=gain_q, gain_k=gain_k, **dict(zip(("b0", "b1", "b2", "b3"), begun)),
            ),
            dict(
                attended=wide, query_grad=wide, own=whole, near=whole, far=whole,
                third_k=half, third_v=half, next=low,
                gains=shape(2, HEAD_DIM, F32),
            ),
            last,
        )
        made.append(result[:2])
        gains.append(result[8])
        token = [result[8]]
        parts.append(dict(zip(("own", "near", "far"), result[2:5])))
        parts[-1].update(third_k=swap(result[5]), third_v=swap(result[6]), next=swap(result[7]))
        if chunk == amount - 1:
            (total,) = call(add, "add", dict(enumerate(gains)), dict(o=shape(2, HEAD_DIM, F32)))
            total = total_over(total, "ctx", 1, 2, 2)
            last = [*last, total]
        last = [sink(chunk, last)]

    first_sink = last
    for step in range(amount, amount + LAG):
        hold = call(add, "hold", dict(total=total), dict(o=shape(2, HEAD_DIM, F32)), [sunk[step - LAG]], cost=COSTS[5])
        last = [sink(step, [*last, *(hold if step == amount else [])])]

    attended, query_grad = call(
        assemble,
        "assemble",
        {(i, chunk): made[chunk][i] for i in range(2) for chunk in range(amount)},
        dict(a=jax.ShapeDtypeStruct(queries.shape, BF16), b=jax.ShapeDtypeStruct(queries.shape, BF16)),
        last,
    )

    factor = (lax.axis_size("dp") * queries.shape[0] * lax.axis_size("ctx") * rows) ** (-0.5)
    row = shape(1, HEAD_DIM, F32)
    chips = lax.axis_size("ctx") // 2
    (total,) = call(add, "add", dict(total=total), dict(o=shape(2, HEAD_DIM, F32)), first_sink)
    while chips > 4:
        total = total_over(total, "ctx", chips, 2 * chips, 2)
        chips //= 2
    total = total_over(total, "ctx", 2, 2 * chips, 4, COSTS[0], [sunk[amount - 1]])
    half = lax.axis_size("dp") // 2
    total = total_over(total, "dp", 1, half, 2, COSTS[1], [pltpu.with_memory_space_constraint(attended, pltpu.HBM)])
    others = [move(total, "dp", lambda i: i ^ half)] if half else []
    key_outputs = []
    for chunk, (first, count) in enumerate(CHUNKS):
        narrow = columns(rows, count * HEAD_DIM, first * HEAD_DIM)
        ins = dict(
            keys=own[chunk][0], gain=gain_k, own=parts[chunk]["own"], next=parts[chunk]["next"], arrived=sunk[chunk + LAG]
        )
        outs = dict(
            key_grad=jax.ShapeDtypeStruct(keys.shape, BF16), value_grad=jax.ShapeDtypeStruct(keys.shape, BF16)
        )
        final = chunk == amount - 1
        if final:
            ins.update(enumerate([total, *others]))
            outs.update(query_gains=row, key_gains=row)
        key_outputs = call(
            functools.partial(finish, count, width[chunk + LAG], factor if final else None),
            "finish",
            ins,
            outs,
            key_outputs,
            cost=COSTS[3 + chunk],
            grid=(1,),
            out_specs=dict(key_grad=narrow, value_grad=narrow),
            input_output_aliases={len(ins) + i: i for i in range(len(key_outputs))},
        )
    key_grad, value_grad, query_gains, key_gains = key_outputs
    return attended, query_grad, key_grad, value_grad, query_gains[0], key_gains[0]


def solution(mesh):
    block = P("dp", "ctx", None)
    return jax.shard_map(
        shards,
        mesh=mesh,
        in_specs=(P("dp", None), block, block, block, P(), P(), block),
        out_specs=(block, block, block, block, P(), P()),
        check_vma=False,
    )
```

```python
import functools

import jax
import jax.numpy as jnp
from jax import lax
from jax.experimental import pallas as pl
from jax.experimental.pallas import tpu as pltpu
from jax.sharding import PartitionSpec as P

HEADS = 8
KV_HEADS = 4
HEAD_DIM = 256
WINDOW = 512
GREACH = 4
GROUPS = HEADS // KV_HEADS
EPSILON = 1e-06
BF16 = jnp.bfloat16
F32 = jnp.float32
CHUNKS = ((0, 2), (2, 2))
LAG = 2

PIECES = 4

COSTS = 2**32, 0, 0, 2**31, 2**32, 2**31

VMEM = pl.BlockSpec(memory_space=pltpu.VMEM)
ANY = pl.BlockSpec(memory_space=pl.ANY)


def call(body, name, ins, outs, after=(), cost=0, in_specs=None, out_specs=None, **more):
    names = list(ins)

    def kernel(*refs):
        used = len(names) + len(after)
        body(*refs[: len(names)], *refs[used:])

    specs = [(in_specs or {}).get(key, VMEM) for key in names] + [ANY] * len(after)
    return pl.pallas_call(
        kernel,
        out_shape=list(outs.values()),
        in_specs=specs,
        out_specs=[(out_specs or {}).get(key, VMEM) for key in outs],
        compiler_params=pltpu.CompilerParams(vmem_limit_bytes=40 * 2**20),
        cost_estimate=pl.CostEstimate(flops=cost, bytes_accessed=1, transcendentals=0),
        name=name,
        **more,
    )(*ins.values(), *after)


def shape(rows, cols, dtype=BF16):
    return jax.ShapeDtypeStruct((rows, cols), dtype)


def core_index():
    return lax.axis_index("ctx") % 2


def payload(chunks, keys, values, *rest):
    extra = len(rest[:-1]) - len(chunks)
    small, outs, kept, sems = rest[: extra // 2], rest[extra // 2 : -1 - extra // 2], rest[-1 - extra // 2 : -1], rest[-1]
    copies = [pltpu.make_async_copy(old, new, sems.at[i]) for i, (old, new) in enumerate(zip(small, kept))]
    for (first, count), out in zip(chunks, outs):
        here = pl.ds(first * HEAD_DIM, count * HEAD_DIM)
        for side, field in enumerate((keys, values)):
            to = pl.ds(side * count * HEAD_DIM, count * HEAD_DIM)
            for piece in range(PIECES):
                share = field.shape[1] // PIECES
                rows = pl.ds(piece * share, share)
                sem = sems.at[len(copies)]
                copies.append(pltpu.make_async_copy(field.at[0, rows, here], out.at[rows, to], sem))
    for copy in copies:
        copy.start()
    for copy in copies:
        copy.wait()


def normalize(field):
    inverse = lax.rsqrt(jnp.mean(field * field, -1, keepdims=True) + EPSILON)
    return field * inverse, inverse


def dot(left, right, over):
    return lax.dot_general(left, right, ((over[:1], over[1:]), ((), ())), preferred_element_type=F32)


def attend(
    first, count, at_own, at_x, at_near, at_far, segments, queries, out_grad, own, across_x, arrived_near, arrived_far,
    across_k, across_v,    query_gain, key_gain, *rest,
):
    attended, query_grad, part_own, part_near, part_far, third_k, third_v, part_next, gains = rest
    position = lax.axis_index("ctx")
    rows = queries.shape[1]
    band = (GREACH + 1) * rows
    gain_q = query_gain[...]
    gain_k = key_gain[...]

    def segment(distance):
        block = position - distance
        first = pl.multiple_of(jnp.maximum(block, 0) * rows, rows)
        return jnp.where(block >= 0, segments[:, pl.ds(first, rows)], -1)

    key_seg = jnp.concatenate([segment(distance) for distance in range(GREACH, -1, -1)], 1)
    query_seg = jnp.broadcast_to(segment(0), (rows, rows)).T[:, :1]
    back = (
        lax.broadcasted_iota(jnp.int32, (rows, band), 0)
        - lax.broadcasted_iota(jnp.int32, (rows, band), 1)
        + GREACH * rows
    )
    live = (query_seg == key_seg) & (back >= 0) & (back < WINDOW)
    live = jnp.concatenate([live] * GROUPS, 0)

    def band_of(index):
        third = (across_k, 0) if index < count else (across_v, -count * HEAD_DIM)
        blocks = ((arrived_far, at_far), third, (arrived_near, at_near), (across_x, at_x), (own, at_own))
        return jnp.concatenate(
            [field[:, at + index * HEAD_DIM : at + (index + 1) * HEAD_DIM] for field, at in blocks], 0
        )

    def columns_of(index):
        return slice(index * HEAD_DIM, (index + 1) * HEAD_DIM)

    def query_rows(field, head):
        start = (first + head) * GROUPS
        return jnp.concatenate([field[0, :, columns_of(start + g)] for g in range(GROUPS)], 0)

    heads = range(count)
    grads = [query_rows(out_grad, head) for head in heads]
    band_v = [band_of(count + head) for head in heads]
    q_normed, q_inverse, q_scaled, k_normed, k_rounded, scores = [], [], [], [], [], []
    for head in heads:
        normed, inverse = normalize(query_rows(queries, head).astype(F32))
        q_normed.append(normed)
        q_inverse.append(inverse)
        q_scaled.append((normed * gain_q * HEAD_DIM ** (-0.5)).astype(BF16))
        k_normed.append(normalize(band_of(head).astype(F32))[0])
        k_rounded.append((k_normed[head] * gain_k).astype(BF16))
        scores.append(dot(q_scaled[head], k_rounded[head], (1, 1)))
    dprob = [dot(grads[head], band_v[head], (1, 1)) for head in heads]

    def give(parts, at):
        part_far[:, at] = parts[:rows]
        part_near[:, at] = parts[2 * rows : 3 * rows]
        part_next[:, at] = parts[3 * rows : 4 * rows].astype(BF16)
        part_own[:, at] = parts[4 * rows :]
        return parts[rows : 2 * rows].astype(BF16)

    dscore = []
    for head in heads:
        weights = jnp.where(live, jnp.exp(scores[head]), 0.0)
        probs = weights * (1.0 / jnp.sum(weights, -1, keepdims=True))
        probs_low = probs.astype(BF16)
        centre = jnp.sum(probs * dprob[head], -1, keepdims=True)
        dscore.append((probs * (dprob[head] - centre)).astype(BF16))
        third_v[:, columns_of(head)] = give(dot(probs_low, grads[head], (0, 0)), columns_of(count + head))
        output = dot(probs_low, band_v[head], (1, 0)).astype(BF16)
        for g in range(GROUPS):
            attended[:, columns_of(head * GROUPS + g)] = output[g * rows : (g + 1) * rows]
    query_gains = jnp.zeros((1, HEAD_DIM), F32)
    key_gains = jnp.zeros((1, HEAD_DIM), F32)
    for head in heads:
        key_parts = dot(dscore[head], q_scaled[head], (0, 0))
        third_k[:, columns_of(head)] = give(key_parts, columns_of(head))
        key_gains = key_gains + jnp.sum(key_parts * k_normed[head], 0, keepdims=True)
        dq = dot(dscore[head], k_rounded[head], (1, 0)) * HEAD_DIM ** (-0.5)
        scaled = dq * gain_q
        grad = q_inverse[head] * (scaled - q_normed[head] * jnp.mean(scaled * q_normed[head], -1, keepdims=True))
        for g in range(GROUPS):
            query_grad[:, columns_of(head * GROUPS + g)] = grad[g * rows : (g + 1) * rows].astype(BF16)
        query_gains = query_gains + jnp.sum(dq * q_normed[head], 0, keepdims=True)
    gains[0:1, :] = query_gains
    gains[1:2, :] = key_gains


def assemble(*refs):
    amount = len(CHUNKS)
    for index, out in enumerate(refs[-2:]):
        for (first, count), part in zip(CHUNKS, refs[index * amount : (index + 1) * amount]):
            out[0, :, first * GROUPS * HEAD_DIM : (first + count) * GROUPS * HEAD_DIM] = part[...]


def add(*refs):
    refs[-1][...] = sum(ref[...] for ref in refs[1:-1]) + refs[0][...]


def finish(count, at, factor, own, key_gain, part_own, swapped, arrived, *rest):
    if factor is None:
        key_grad, value_grad = rest
    else:
        gains, (key_grad, value_grad, query_gains, key_gains) = rest[:-4], rest[-4:]
        total = sum(ref[...] for ref in gains[1:]) + gains[0][...]
        query_gains[...] = total[0:1, :] * factor
        key_gains[...] = total[1:2, :] * factor
    rows = part_own.shape[0]
    gain_k = key_gain[...]
    for head in range(count):

        def total(index):
            here = slice(index * HEAD_DIM, (index + 1) * HEAD_DIM)
            there = slice(at + index * HEAD_DIM, at + (index + 1) * HEAD_DIM)
            extra = jnp.where(core_index() == 0, swapped[:, here].astype(F32), 0.0)
            return part_own[:, here] + extra + arrived[:, there].astype(F32)

        out = slice(head * HEAD_DIM, (head + 1) * HEAD_DIM)
        normed, inverse = normalize(own[:, out].astype(F32))
        scaled = total(head) * gain_k
        grad = inverse * (scaled - normed * jnp.mean(scaled * normed, -1, keepdims=True))
        key_grad[0, :, out] = grad.astype(BF16)
        value_grad[0, :, out] = total(count + head).astype(BF16)


def columns(rows, width, first):
    return pl.BlockSpec((1, rows, width), lambda i: (0, 0, first // width))


def move(field, axis, target):
    size = lax.axis_size(axis)
    return lax.ppermute(field, axis, [(i, target(i)) for i in range(size) if 0 <= target(i) < size])


def up(field, lowest=0):
    return move(field, "ctx", lambda i: i + 2 if i >= 2 * lowest else -1)


def down(field, lowest=0):
    return move(field, "ctx", lambda i: i - 2 if i - 2 >= 2 * lowest else -1)


def swap(field):
    return move(field, "ctx", lambda i: i ^ 1)


def total_over(field, axis, unit, end, most, cost=0, after=()):
    end = min(end, lax.axis_size(axis))
    while unit < end:
        group = min(most, end // unit)
        others = [move(field, axis, lambda i: i ^ (by * unit)) for by in range(1, group)]
        (field,) = call(add, "add", dict(enumerate([field, *others])), dict(o=shape(*field.shape, F32)), after, cost=cost)
        unit *= group
    return field


def shards(segment_ids, queries, keys, values, query_gain, key_gain, out_grad):
    rows = queries.shape[1]
    gain_q = query_gain.reshape(1, HEAD_DIM)
    gain_k = key_gain.reshape(1, HEAD_DIM)
    amount = len(CHUNKS)
    width = [2 * count * HEAD_DIM for _, count in CHUNKS] + [0] * LAG
    def gather(chunks, small=(), after=()):
        sources = [pltpu.with_memory_space_constraint(field, pltpu.HBM) for field in (keys, values, *small)]
        made = call(
            functools.partial(payload, chunks),
            "payload",
            dict(enumerate(sources)),
            dict(
                enumerate(
                    [shape(rows, 2 * count * HEAD_DIM) for _, count in chunks]
                    + [jax.ShapeDtypeStruct(field.shape, field.dtype) for field in small]
                )
            ),
            after,
            in_specs=dict.fromkeys(range(len(sources)), ANY),
            scratch_shapes=[pltpu.SemaphoreType.DMA((2 * len(chunks) * PIECES + len(small),))],
        )
        return made[: len(chunks)], made[len(chunks) :]

    own, _ = gather(CHUNKS[:1])
    near = {0: (up(own[0]), 0)}
    more, (segments, gain_q, gain_k) = gather(CHUNKS[1:], (segment_ids, gain_q, gain_k), own)
    own = [(field, 0) for field in (*own, *more)]
    for chunk in range(1, LAG):
        near[chunk] = (up(own[chunk][0]), 0)
    far, next_behind, third_behind = {}, {}, {}

    def climb(steps, after=()):
        ins, outs, jobs = {}, {}, []

        def use(place, chunk):
            field, at = place
            key = next((key for key, value in ins.items() if value is field), f"in{len(ins)}")
            ins[key] = field
            return key, slice(at, at + width[chunk])

        def exchange(to, chunk, first, second, halves=1):
            part = width[chunk] // halves
            for half in range(halves):
                pick = [(key, slice(at.start + half * part, at.start + (half + 1) * part)) for key, at in (use(first[chunk], chunk), use(second[chunk], chunk))]
                jobs.append((f"{to}{half}", 0, *pick))
                outs[f"{to}{half}"] = shape(rows, part)

        for step in steps:
            rise = 0
            if step + LAG < amount:
                jobs.append((f"rise{step}", rise, use(own[step + LAG], step + LAG), None))
                rise += width[step + LAG]
            if step < amount:
                jobs.append((f"rise{step}", rise, use(near[step], step), None))
                outs[f"rise{step}"] = shape(rows, rise + width[step])
                exchange("next", step, own, near)
            if step >= LAG:
                exchange("third", step - LAG, near, far, 2)

        def body(*refs):
            ref = dict(zip(list(ins) + list(outs), refs))
            for to, at, (key, here), other in jobs:
                value = ref[key][:, here]
                if other is not None:
                    value = jnp.where(core_index() == 0, value, ref[other[0]][:, other[1]])
                ref[to][:, at : at + value.shape[1]] = value

        made = dict(zip(outs, call(body, "climb", ins, outs, after, cost=10**9 * steps[0])))
        for step in steps:
            if step < amount:
                arrived = up(made[f"rise{step}"], 0 if step + LAG < amount else 1)
                ahead = 0
                if step + LAG < amount:
                    near[step + LAG] = (arrived, 0)
                    ahead = width[step + LAG]
                far[step] = (arrived, ahead)
                next_behind[step] = (swap(made["next0"]), 0)
            if step >= LAG:
                third_behind[step - LAG] = [swap(made["third0"]), swap(made["third1"])]
        return [next(iter(made.values()))]

    parts, sunk = [], {}

    def sink(step, after=()):
        fresh, older = step < amount, step >= LAG
        mine, below = width[step], width[step - LAG] if older else 0
        ins = {}
        if fresh:
            ins.update(far=parts[step]["far"], third_k=parts[step]["third_k"], third_v=parts[step]["third_v"])
        if step == 0:
            ins.update(next=parts[step]["next"])
        if older:
            chunk = step - LAG
            ins.update(near=parts[chunk]["near"], arrived=sunk[chunk])
            ins.update(old_k=parts[chunk]["third_k"], old_v=parts[chunk]["third_v"], next_old=parts[chunk]["next"])

        def body(*refs):
            ref = dict(zip(list(ins) + list(outs), refs))
            first = core_index() == 0
            if fresh:
                if step == 0:
                    ref["give"][...] = ref["next"][...]
                for half, extra in ((slice(0, mine // 2), ref["third_k"]), (slice(mine // 2, mine), ref["third_v"])):
                    extra = jnp.where(first, 0.0, extra[...].astype(F32))
                    ref["out"][:, half] = (ref["far"][:, half] + extra).astype(BF16)
            if older:
                for half, extra in ((slice(0, below // 2), ref["old_k"]), (slice(below // 2, below), ref["old_v"])):
                    extra = jnp.where(first, extra[...], ref["next_old"][:, half]).astype(F32)
                    total = ref["near"][:, half] + extra + ref["arrived"][:, half].astype(F32)
                    ref["out"][:, mine + half.start : mine + half.stop] = total.astype(BF16)

        outs = dict(out=shape(rows, mine + below))
        if step == 0:
            outs.update(give=shape(rows, mine))
        total, *give = call(body, "sink", ins, outs, after)
        sunk[step] = down(total, 0 if older else 1)
        if step == 0:
            parts[step]["next"] = swap(give[0])
        return total

    made, gains, last, token = [], [], [], []
    order = []
    for step in range(LAG):
        order = climb([step], order)
    for chunk, (first, count) in enumerate(CHUNKS):
        order = climb([chunk + LAG], order + token)
        held = (own, next_behind, near, far)
        wide = shape(rows, GROUPS * count * HEAD_DIM)
        whole, low, half = shape(rows, width[chunk], F32), shape(rows, width[chunk]), shape(rows, width[chunk] // 2)
        result = call(
            functools.partial(attend, first, count, *(place[chunk][1] for place in held)),
            "attend",
            dict(
                segments=segments, queries=queries, out_grad=out_grad, own=own[chunk][0],
                **{f"behind{i}": place[chunk][0] for i, place in enumerate(held[1:])},
                third_k=third_behind[chunk][0], third_v=third_behind[chunk][1], gain_q=gain_q, gain_k=gain_k,
            ),
            dict(
                attended=wide, query_grad=wide, own=whole, near=whole, far=whole,
                third_k=half, third_v=half, next=low,
                gains=shape(2, HEAD_DIM, F32),
            ),
            last,
        )
        made.append(result[:2])
        gains.append(result[8])
        token = [result[8]]
        parts.append(dict(zip(("own", "near", "far"), result[2:5])))
        parts[-1].update(third_k=swap(result[5]), third_v=swap(result[6]), next=swap(result[7]) if chunk else result[7])
        if chunk == amount - 1:
            (total,) = call(add, "add", dict(enumerate(gains)), dict(o=shape(2, HEAD_DIM, F32)))
            total = total_over(total, "ctx", 1, 2, 2)
            last = [*last, total]
        last = [sink(chunk, last)]

    first_sink = last
    for step in range(amount, amount + LAG):
        hold = call(add, "hold", dict(total=total), dict(o=shape(2, HEAD_DIM, F32)), [sunk[step - LAG]], cost=COSTS[5])
        last = [sink(step, [*last, *(hold if step == amount else [])])]

    attended, query_grad = call(
        assemble,
        "assemble",
        {(i, chunk): made[chunk][i] for i in range(2) for chunk in range(amount)},
        dict(a=jax.ShapeDtypeStruct(queries.shape, BF16), b=jax.ShapeDtypeStruct(queries.shape, BF16)),
        last,
    )

    factor = (lax.axis_size("dp") * queries.shape[0] * lax.axis_size("ctx") * rows) ** (-0.5)
    row = shape(1, HEAD_DIM, F32)
    chips = lax.axis_size("ctx") // 2
    (total,) = call(add, "add", dict(total=total), dict(o=shape(2, HEAD_DIM, F32)), first_sink)
    while chips > 4:
        total = total_over(total, "ctx", chips, 2 * chips, 2)
        chips //= 2
    total = total_over(total, "ctx", 2, 2 * chips, 4, COSTS[0], [sunk[amount - 1]])
    half = lax.axis_size("dp") // 2
    total = total_over(total, "dp", 1, half, 2, COSTS[1], [pltpu.with_memory_space_constraint(attended, pltpu.HBM)])
    others = [move(total, "dp", lambda i: i ^ half)] if half else []
    key_outputs = []
    for chunk, (first, count) in enumerate(CHUNKS):
        narrow = columns(rows, count * HEAD_DIM, first * HEAD_DIM)
        ins = dict(
            keys=own[chunk][0], gain=gain_k, own=parts[chunk]["own"], next=parts[chunk]["next"], arrived=sunk[chunk + LAG]
        )
        outs = dict(
            key_grad=jax.ShapeDtypeStruct(keys.shape, BF16), value_grad=jax.ShapeDtypeStruct(keys.shape, BF16)
        )
        final = chunk == amount - 1
        if final:
            ins.update(enumerate([total, *others]))
            outs.update(query_gains=row, key_gains=row)
        key_outputs = call(
            functools.partial(finish, count, width[chunk + LAG], factor if final else None),
            "finish",
            ins,
            outs,
            key_outputs,
            cost=COSTS[3 + chunk],
            grid=(1,),
            out_specs=dict(key_grad=narrow, value_grad=narrow),
            input_output_aliases={len(ins) + i: i for i in range(len(key_outputs))},
        )
    key_grad, value_grad, query_gains, key_gains = key_outputs
    return attended, query_grad, key_grad, value_grad, query_gains[0], key_gains[0]


def solution(mesh):
    block = P("dp", "ctx", None)
    return jax.shard_map(
        shards,
        mesh=mesh,
        in_specs=(P("dp", None), block, block, block, P(), P(), block),
        out_specs=(block, block, block, block, P(), P()),
        check_vma=False,
    )
```

```python
import functools

import jax
import jax.numpy as jnp
from jax import lax
from jax.experimental import pallas as pl
from jax.experimental.pallas import tpu as pltpu
from jax.sharding import PartitionSpec as P

HEADS = 8
KV_HEADS = 4
HEAD_DIM = 256
WINDOW = 512
GREACH = 4
GROUPS = HEADS // KV_HEADS
EPSILON = 1e-06
BF16 = jnp.bfloat16
F32 = jnp.float32
CHUNKS = ((0, 2), (2, 2))
LAG = 2

PIECES = 4

COSTS = 2**32, 0, 0, 2**31, 2**32, 2**31

VMEM = pl.BlockSpec(memory_space=pltpu.VMEM)
ANY = pl.BlockSpec(memory_space=pl.ANY)


def call(body, name, ins, outs, after=(), cost=0, in_specs=None, out_specs=None, **more):
    names = list(ins)

    def kernel(*refs):
        used = len(names) + len(after)
        body(*refs[: len(names)], *refs[used:])

    specs = [(in_specs or {}).get(key, VMEM) for key in names] + [ANY] * len(after)
    return pl.pallas_call(
        kernel,
        out_shape=list(outs.values()),
        in_specs=specs,
        out_specs=[(out_specs or {}).get(key, VMEM) for key in outs],
        compiler_params=pltpu.CompilerParams(vmem_limit_bytes=40 * 2**20),
        cost_estimate=pl.CostEstimate(flops=cost, bytes_accessed=1, transcendentals=0),
        name=name,
        **more,
    )(*ins.values(), *after)


def shape(rows, cols, dtype=BF16):
    return jax.ShapeDtypeStruct((rows, cols), dtype)


def core_index():
    return lax.axis_index("ctx") % 2


def payload(chunks, keys, values, *rest):
    extra = len(rest[:-1]) - len(chunks)
    small, outs, kept, sems = rest[: extra // 2], rest[extra // 2 : -1 - extra // 2], rest[-1 - extra // 2 : -1], rest[-1]
    copies = [pltpu.make_async_copy(old, new, sems.at[i]) for i, (old, new) in enumerate(zip(small, kept))]
    for (first, count), out in zip(chunks, outs):
        here = pl.ds(first * HEAD_DIM, count * HEAD_DIM)
        for side, field in enumerate((keys, values)):
            to = pl.ds(side * count * HEAD_DIM, count * HEAD_DIM)
            for piece in range(PIECES):
                share = field.shape[1] // PIECES
                rows = pl.ds(piece * share, share)
                sem = sems.at[len(copies)]
                copies.append(pltpu.make_async_copy(field.at[0, rows, here], out.at[rows, to], sem))
    for copy in copies:
        copy.start()
    for copy in copies:
        copy.wait()


def normalize(field):
    inverse = lax.rsqrt(jnp.mean(field * field, -1, keepdims=True) + EPSILON)
    return field * inverse, inverse


def dot(left, right, over):
    return lax.dot_general(left, right, ((over[:1], over[1:]), ((), ())), preferred_element_type=F32)


def attend(
    first, count, at_own, at_x, at_near, at_far, segments, queries, out_grad, own, across_x, arrived_near, arrived_far,
    across_k, across_v,    query_gain, key_gain, *rest,
):
    attended, query_grad, part_own, part_near, part_far, third_k, third_v, part_next, gains = rest
    position = lax.axis_index("ctx")
    rows = queries.shape[1]
    band = (GREACH + 1) * rows
    gain_q = query_gain[...]
    gain_k = key_gain[...]

    def segment(distance):
        block = position - distance
        first = pl.multiple_of(jnp.maximum(block, 0) * rows, rows)
        return jnp.where(block >= 0, segments[:, pl.ds(first, rows)], -1)

    key_seg = jnp.concatenate([segment(distance) for distance in range(GREACH, -1, -1)], 1)
    query_seg = jnp.broadcast_to(segment(0), (rows, rows)).T[:, :1]
    back = (
        lax.broadcasted_iota(jnp.int32, (rows, band), 0)
        - lax.broadcasted_iota(jnp.int32, (rows, band), 1)
        + GREACH * rows
    )
    live = (query_seg == key_seg) & (back >= 0) & (back < WINDOW)
    live = jnp.concatenate([live] * GROUPS, 0)

    def band_of(index):
        third = (across_k, 0) if index < count else (across_v, across_v.shape[1] - 2 * count * HEAD_DIM)
        blocks = ((arrived_far, at_far), third, (arrived_near, at_near), (across_x, at_x), (own, at_own))
        return jnp.concatenate(
            [field[:, at + index * HEAD_DIM : at + (index + 1) * HEAD_DIM] for field, at in blocks], 0
        )

    def columns_of(index):
        return slice(index * HEAD_DIM, (index + 1) * HEAD_DIM)

    def query_rows(field, head):
        start = (first + head) * GROUPS
        return jnp.concatenate([field[0, :, columns_of(start + g)] for g in range(GROUPS)], 0)

    heads = range(count)
    grads = [query_rows(out_grad, head) for head in heads]
    band_v = [band_of(count + head) for head in heads]
    q_normed, q_inverse, q_scaled, k_normed, k_rounded, scores = [], [], [], [], [], []
    for head in heads:
        normed, inverse = normalize(query_rows(queries, head).astype(F32))
        q_normed.append(normed)
        q_inverse.append(inverse)
        q_scaled.append((normed * gain_q * HEAD_DIM ** (-0.5)).astype(BF16))
        k_normed.append(normalize(band_of(head).astype(F32))[0])
        k_rounded.append((k_normed[head] * gain_k).astype(BF16))
        scores.append(dot(q_scaled[head], k_rounded[head], (1, 1)))
    dprob = [dot(grads[head], band_v[head], (1, 1)) for head in heads]

    def give(parts, at):
        part_far[:, at] = parts[:rows]
        part_near[:, at] = parts[2 * rows : 3 * rows]
        part_next[:, at] = parts[3 * rows : 4 * rows].astype(BF16)
        part_own[:, at] = parts[4 * rows :]
        return parts[rows : 2 * rows].astype(BF16)

    dscore = []
    for head in heads:
        weights = jnp.where(live, jnp.exp(scores[head]), 0.0)
        probs = weights * (1.0 / jnp.sum(weights, -1, keepdims=True))
        probs_low = probs.astype(BF16)
        centre = jnp.sum(probs * dprob[head], -1, keepdims=True)
        dscore.append((probs * (dprob[head] - centre)).astype(BF16))
        third_v[:, columns_of(head)] = give(dot(probs_low, grads[head], (0, 0)), columns_of(count + head))
        output = dot(probs_low, band_v[head], (1, 0)).astype(BF16)
        for g in range(GROUPS):
            attended[:, columns_of(head * GROUPS + g)] = output[g * rows : (g + 1) * rows]
    query_gains = jnp.zeros((1, HEAD_DIM), F32)
    key_gains = jnp.zeros((1, HEAD_DIM), F32)
    for head in heads:
        key_parts = dot(dscore[head], q_scaled[head], (0, 0))
        third_k[:, columns_of(head)] = give(key_parts, columns_of(head))
        key_gains = key_gains + jnp.sum(key_parts * k_normed[head], 0, keepdims=True)
        dq = dot(dscore[head], k_rounded[head], (1, 0)) * HEAD_DIM ** (-0.5)
        scaled = dq * gain_q
        grad = q_inverse[head] * (scaled - q_normed[head] * jnp.mean(scaled * q_normed[head], -1, keepdims=True))
        for g in range(GROUPS):
            query_grad[:, columns_of(head * GROUPS + g)] = grad[g * rows : (g + 1) * rows].astype(BF16)
        query_gains = query_gains + jnp.sum(dq * q_normed[head], 0, keepdims=True)
    gains[0:1, :] = query_gains
    gains[1:2, :] = key_gains


def assemble(*refs):
    amount = len(CHUNKS)
    for index, out in enumerate(refs[-2:]):
        for (first, count), part in zip(CHUNKS, refs[index * amount : (index + 1) * amount]):
            out[0, :, first * GROUPS * HEAD_DIM : (first + count) * GROUPS * HEAD_DIM] = part[...]


def add(*refs):
    refs[-1][...] = sum(ref[...] for ref in refs[1:-1]) + refs[0][...]


def finish(count, at, factor, own, key_gain, part_own, swapped, arrived, *rest):
    if factor is None:
        key_grad, value_grad = rest
    else:
        gains, (key_grad, value_grad, query_gains, key_gains) = rest[:-4], rest[-4:]
        total = sum(ref[...] for ref in gains[1:]) + gains[0][...]
        query_gains[...] = total[0:1, :] * factor
        key_gains[...] = total[1:2, :] * factor
    rows = part_own.shape[0]
    gain_k = key_gain[...]
    for head in range(count):

        def total(index):
            here = slice(index * HEAD_DIM, (index + 1) * HEAD_DIM)
            there = slice(at + index * HEAD_DIM, at + (index + 1) * HEAD_DIM)
            extra = jnp.where(core_index() == 0, swapped[:, here].astype(F32), 0.0)
            return part_own[:, here] + extra + arrived[:, there].astype(F32)

        out = slice(head * HEAD_DIM, (head + 1) * HEAD_DIM)
        normed, inverse = normalize(own[:, out].astype(F32))
        scaled = total(head) * gain_k
        grad = inverse * (scaled - normed * jnp.mean(scaled * normed, -1, keepdims=True))
        key_grad[0, :, out] = grad.astype(BF16)
        value_grad[0, :, out] = total(count + head).astype(BF16)


def columns(rows, width, first):
    return pl.BlockSpec((1, rows, width), lambda i: (0, 0, first // width))


def move(field, axis, target):
    size = lax.axis_size(axis)
    return lax.ppermute(field, axis, [(i, target(i)) for i in range(size) if 0 <= target(i) < size])


def up(field, lowest=0):
    return move(field, "ctx", lambda i: i + 2 if i >= 2 * lowest else -1)


def down(field, lowest=0):
    return move(field, "ctx", lambda i: i - 2 if i - 2 >= 2 * lowest else -1)


def swap(field):
    return move(field, "ctx", lambda i: i ^ 1)


def total_over(field, axis, unit, end, most, cost=0, after=()):
    end = min(end, lax.axis_size(axis))
    while unit < end:
        group = min(most, end // unit)
        others = [move(field, axis, lambda i: i ^ (by * unit)) for by in range(1, group)]
        (field,) = call(add, "add", dict(enumerate([field, *others])), dict(o=shape(*field.shape, F32)), after, cost=cost)
        unit *= group
    return field


def shards(segment_ids, queries, keys, values, query_gain, key_gain, out_grad):
    rows = queries.shape[1]
    gain_q = query_gain.reshape(1, HEAD_DIM)
    gain_k = key_gain.reshape(1, HEAD_DIM)
    amount = len(CHUNKS)
    width = [2 * count * HEAD_DIM for _, count in CHUNKS] + [0] * LAG
    def gather(chunks, small=(), after=()):
        sources = [pltpu.with_memory_space_constraint(field, pltpu.HBM) for field in (keys, values, *small)]
        made = call(
            functools.partial(payload, chunks),
            "payload",
            dict(enumerate(sources)),
            dict(
                enumerate(
                    [shape(rows, 2 * count * HEAD_DIM) for _, count in chunks]
                    + [jax.ShapeDtypeStruct(field.shape, field.dtype) for field in small]
                )
            ),
            after,
            in_specs=dict.fromkeys(range(len(sources)), ANY),
            scratch_shapes=[pltpu.SemaphoreType.DMA((2 * len(chunks) * PIECES + len(small),))],
        )
        return made[: len(chunks)], made[len(chunks) :]

    own, _ = gather(CHUNKS[:1])
    near = {0: (up(own[0]), 0)}
    more, (segments, gain_q, gain_k) = gather(CHUNKS[1:], (segment_ids, gain_q, gain_k), own)
    own = [(field, 0) for field in (*own, *more)]
    for chunk in range(1, LAG):
        near[chunk] = (up(own[chunk][0]), 0)
    far, next_behind, third_behind = {}, {}, {}

    def climb(steps, after=()):
        ins, outs, jobs = {}, {}, []

        def use(place, chunk):
            field, at = place
            key = next((key for key, value in ins.items() if value is field), f"in{len(ins)}")
            ins[key] = field
            return key, slice(at, at + width[chunk])

        def exchange(to, chunk, first, second, halves=1):
            part = width[chunk] // halves
            for half in range(halves):
                pick = [(key, slice(at.start + half * part, at.start + (half + 1) * part)) for key, at in (use(first[chunk], chunk), use(second[chunk], chunk))]
                jobs.append((f"{to}{half}", 0, *pick))
                outs[f"{to}{half}"] = shape(rows, part)

        for step in steps:
            rise = 0
            if step + LAG < amount:
                jobs.append((f"rise{step}", rise, use(own[step + LAG], step + LAG), None))
                rise += width[step + LAG]
            if step < amount:
                jobs.append((f"rise{step}", rise, use(near[step], step), None))
                outs[f"rise{step}"] = shape(rows, rise + width[step])
                exchange("next", step, own, near)
            if step >= LAG:
                exchange("third", step - LAG, near, far, 1 if step > LAG else 2)

        def body(*refs):
            ref = dict(zip(list(ins) + list(outs), refs))
            for to, at, (key, here), other in jobs:
                value = ref[key][:, here]
                if other is not None:
                    value = jnp.where(core_index() == 0, value, ref[other[0]][:, other[1]])
                ref[to][:, at : at + value.shape[1]] = value

        made = dict(zip(outs, call(body, "climb", ins, outs, after, cost=10**9 * steps[0])))
        for step in steps:
            if step < amount:
                arrived = up(made[f"rise{step}"], 0 if step + LAG < amount else 1)
                ahead = 0
                if step + LAG < amount:
                    near[step + LAG] = (arrived, 0)
                    ahead = width[step + LAG]
                far[step] = (arrived, ahead)
                next_behind[step] = (swap(made["next0"]), 0)
            if step >= LAG:
                third_behind[step - LAG] = [swap(made[key]) for key in ("third0", "third1") if key in made]
        return [next(iter(made.values()))]

    parts, sunk = [], {}

    def sink(step, after=()):
        fresh, older = step < amount, step >= LAG
        mine, below = width[step], width[step - LAG] if older else 0
        ins = {}
        if fresh:
            ins.update(far=parts[step]["far"], third_k=parts[step]["third_k"], third_v=parts[step]["third_v"])
        if older:
            chunk = step - LAG
            ins.update(near=parts[chunk]["near"], arrived=sunk[chunk])
            ins.update(old_k=parts[chunk]["third_k"], old_v=parts[chunk]["third_v"], next_old=parts[chunk]["next"])

        def body(*refs):
            ref = dict(zip(list(ins) + ["out"], refs))
            first = core_index() == 0
            if fresh:
                for half, extra in ((slice(0, mine // 2), ref["third_k"]), (slice(mine // 2, mine), ref["third_v"])):
                    extra = jnp.where(first, 0.0, extra[...].astype(F32))
                    ref["out"][:, half] = (ref["far"][:, half] + extra).astype(BF16)
            if older:
                for half, extra in ((slice(0, below // 2), ref["old_k"]), (slice(below // 2, below), ref["old_v"])):
                    extra = jnp.where(first, extra[...], ref["next_old"][:, half]).astype(F32)
                    total = ref["near"][:, half] + extra + ref["arrived"][:, half].astype(F32)
                    ref["out"][:, mine + half.start : mine + half.stop] = total.astype(BF16)

        (total,) = call(body, "sink", ins, dict(out=shape(rows, mine + below)), after)
        sunk[step] = down(total, 0 if older else 1)
        return total

    made, gains, last, token = [], [], [], []
    order = []
    for step in range(LAG):
        order = climb([step], order)
    for chunk, (first, count) in enumerate(CHUNKS):
        order = climb([chunk + LAG], order + token)
        held = (own, next_behind, near, far)
        wide = shape(rows, GROUPS * count * HEAD_DIM)
        whole, low, half = shape(rows, width[chunk], F32), shape(rows, width[chunk]), shape(rows, width[chunk] // 2)
        result = call(
            functools.partial(attend, first, count, *(place[chunk][1] for place in held)),
            "attend",
            dict(
                segments=segments, queries=queries, out_grad=out_grad, own=own[chunk][0],
                **{f"behind{i}": place[chunk][0] for i, place in enumerate(held[1:])},
                third_k=third_behind[chunk][0], third_v=third_behind[chunk][-1], gain_q=gain_q, gain_k=gain_k,
            ),
            dict(
                attended=wide, query_grad=wide, own=whole, near=whole, far=whole,
                third_k=half, third_v=half, next=low,
                gains=shape(2, HEAD_DIM, F32),
            ),
            last,
        )
        made.append(result[:2])
        gains.append(result[8])
        token = [result[8]]
        parts.append(dict(zip(("own", "near", "far"), result[2:5])))
        parts[-1].update(third_k=swap(result[5]), third_v=swap(result[6]), next=swap(result[7]))
        if chunk == amount - 1:
            (total,) = call(add, "add", dict(enumerate(gains)), dict(o=shape(2, HEAD_DIM, F32)))
            total = total_over(total, "ctx", 1, 2, 2)
            last = [*last, total]
        last = [sink(chunk, last)]

    first_sink = last
    for step in range(amount, amount + LAG):
        hold = call(add, "hold", dict(total=total), dict(o=shape(2, HEAD_DIM, F32)), [sunk[step - LAG]], cost=COSTS[5])
        last = [sink(step, [*last, *(hold if step == amount else [])])]

    attended, query_grad = call(
        assemble,
        "assemble",
        {(i, chunk): made[chunk][i] for i in range(2) for chunk in range(amount)},
        dict(a=jax.ShapeDtypeStruct(queries.shape, BF16), b=jax.ShapeDtypeStruct(queries.shape, BF16)),
        last,
    )

    factor = (lax.axis_size("dp") * queries.shape[0] * lax.axis_size("ctx") * rows) ** (-0.5)
    row = shape(1, HEAD_DIM, F32)
    chips = lax.axis_size("ctx") // 2
    (total,) = call(add, "add", dict(total=total), dict(o=shape(2, HEAD_DIM, F32)), first_sink)
    while chips > 4:
        total = total_over(total, "ctx", chips, 2 * chips, 2)
        chips //= 2
    total = total_over(total, "ctx", 2, 2 * chips, 4, COSTS[0], [sunk[amount - 1]])
    half = lax.axis_size("dp") // 2
    total = total_over(total, "dp", 1, half, 2, COSTS[1], [pltpu.with_memory_space_constraint(attended, pltpu.HBM)])
    others = [move(total, "dp", lambda i: i ^ half)] if half else []
    key_outputs = []
    for chunk, (first, count) in enumerate(CHUNKS):
        narrow = columns(rows, count * HEAD_DIM, first * HEAD_DIM)
        ins = dict(
            keys=own[chunk][0], gain=gain_k, own=parts[chunk]["own"], next=parts[chunk]["next"], arrived=sunk[chunk + LAG]
        )
        outs = dict(
            key_grad=jax.ShapeDtypeStruct(keys.shape, BF16), value_grad=jax.ShapeDtypeStruct(keys.shape, BF16)
        )
        final = chunk == amount - 1
        if final:
            ins.update(enumerate([total, *others]))
            outs.update(query_gains=row, key_gains=row)
        key_outputs = call(
            functools.partial(finish, count, width[chunk + LAG], factor if final else None),
            "finish",
            ins,
            outs,
            key_outputs,
            cost=COSTS[3 + chunk],
            grid=(1,),
            out_specs=dict(key_grad=narrow, value_grad=narrow),
            input_output_aliases={len(ins) + i: i for i in range(len(key_outputs))},
        )
    key_grad, value_grad, query_gains, key_gains = key_outputs
    return attended, query_grad, key_grad, value_grad, query_gains[0], key_gains[0]


def solution(mesh):
    block = P("dp", "ctx", None)
    return jax.shard_map(
        shards,
        mesh=mesh,
        in_specs=(P("dp", None), block, block, block, P(), P(), block),
        out_specs=(block, block, block, block, P(), P()),
        check_vma=False,
    )
```
